32 devices in a mesh: fsdp: 32 (over z, y, x, core).
Axes of the slice: x: 2, y: 2, z: 4, core: 2. Of those that a mesh axis runs over, the one named last changes fastest.
Arguments:
- tokens: bfloat16 [2048, 32, 128], P('fsdp'), may hold values from -6 to 6
- features: bfloat16 [2048, 2, 49, 128], P('fsdp'), may hold values from -6 to 6
- proprio: bfloat16 [2048, 2, 32], P('fsdp'), may hold values from -6 to 6
- embodiment: int32 [2048], P('fsdp'), may hold values from 0 to 31
- trunk_attn: bfloat16 [2, 512, 128], P(None, 'fsdp')
- feedforward_up_weight: bfloat16 [2, 512, 128], P(None, 'fsdp'), may hold values from -0.5 to 0.5
- mlp_down: bfloat16 [2, 512, 128], P(None, 'fsdp'), may hold values from -0.25 to 0.25
- stem_mats: bfloat16 [2, 4096, 512], P(None, 'fsdp')
- stem_queries: bfloat16 [2, 512, 128], P(None, 'fsdp'), may hold values from -6 to 6
- prop_in: bfloat16 [2, 1024, 128], P(None, 'fsdp'), may hold values from -1 to 1
- trunk_vectors: bfloat16 [2, 8, 128], replicated
- mlp_bias: bfloat16 [2, 512], replicated, may hold values from -2 to 2
- stem_bias: bfloat16 [2, 32, 2, 128], replicated, may hold values from -2 to 2
- cotangent: bfloat16 [2048, 32, 128], P('fsdp'), may hold values from -6 to 6
Outputs:
- out_tokens: bfloat16 [2048, 32, 128], P('fsdp')
- grad_tokens: float32 [2048, 32, 128], P('fsdp')
- grad_features: float32 [2048, 2, 49, 128], P('fsdp')
- grad_proprio: float32 [2048, 2, 32], P('fsdp')
- grad_trunk_attn: float32 [2, 512, 128], P(None, 'fsdp')
- grad_mlp_up: float32 [2, 512, 128], P(None, 'fsdp')
- grad_mlp_down: float32 [2, 512, 128], P(None, 'fsdp')
- grad_stem_mats: float32 [2, 4096, 512], P(None, 'fsdp')
- grad_stem_queries: float32 [2, 512, 128], P(None, 'fsdp')
- grad_prop_in: float32 [2, 1024, 128], P(None, 'fsdp')
- grad_trunk_vectors: float32 [2, 8, 128], replicated
- grad_mlp_bias: float32 [2, 512], replicated
- grad_stem_bias: float32 [2, 32, 2, 128], replicated
The draws below stay inside these ranges and needn't reach their ends.
All inputs are finite; a program needn't handle non-finite values.
Results may differ from the reference program's by a relative error of at most 0.019.
Values may be sent and summed in bfloat16 or wider, within the bound.
A program may use at most 256 MiB of HBM per device.

```python
import math
import jax
import jax.numpy as jnp
import numpy as np
from jax import lax

D = 128
HEADS = 8
HD = 16
FF = 512
SQ = 16
FR = 49
PROP = 32
STEMS = 32
STEPS = 2
LAYERS = 2
TOK = 32
SAMPLES = 2048


def draw_trunk_attn(key, part):
    key = jax.random.fold_in(key, 11)
    normal_draw = jax.random.normal(key, (LAYERS, 4 * D, D), jnp.float32)
    block_index = jnp.arange(4 * D) // D
    factor = jnp.where(block_index == 3, 3.0, 1.0) / math.sqrt(D)
    return (normal_draw * factor[None, :, None]).astype(jnp.bfloat16)


def draw_stem_mats(key, part):
    key = jax.random.fold_in(key, 12)
    normal_draw = jax.random.normal(key, (LAYERS, STEMS * D, 4 * D), jnp.float32)
    block_index = jnp.arange(4 * D) // D
    factor = jnp.where(block_index == 2, 3.0, 1.0) / math.sqrt(D)
    return (normal_draw * factor[None, None, :]).astype(jnp.bfloat16)


def draw_trunk_vectors(key, part):
    key = jax.random.fold_in(key, 13)
    normal_draw = jax.random.normal(key, (LAYERS, 8, D), jnp.float32)
    row_index = jnp.arange(8)
    gain_rows = (row_index == 0) | (row_index == 5)
    values = jnp.where(gain_rows[None, :, None], 1.0 + 0.15 * normal_draw, 0.3 * normal_draw)
    return values.astype(jnp.bfloat16)


def place_ends(values, rng, least, top_value):
    spot = [jax.random.randint(jax.random.fold_in(rng, axis), (), 0, length) for axis, length in enumerate(values.shape)]
    main_axis = values.shape.index(max(values.shape))
    neighbour = spot[:main_axis] + [(spot[main_axis] + 1) % values.shape[main_axis]] + spot[main_axis + 1:]
    return values.at[tuple(spot)].set(least).at[tuple(neighbour)].set(top_value)


def level_of(stream_key, dims, split, smallest, high):
    factor_of, own = 1.0, jax.random.fold_in(stream_key, 6)
    for dim, shards_of in split:
        steps = jnp.exp(jax.random.uniform(jax.random.fold_in(own, dim), (shards_of,), jnp.float32, smallest / len(split), high / len(split)))
        factor_of = factor_of * jnp.repeat(steps, dims[dim] // shards_of).reshape([-1 if axis == dim else 1 for axis in range(len(dims))])
    return factor_of


def rank_table(amount, skew):
    weights = [(1 << 20) // math.isqrt(grade ** skew) + 1 for grade in range(1, amount + 1)]
    width = 1 + sum(weights) // (1 << 30)
    return np.cumsum(np.array([max(1, weight // width) for weight in weights]))


def skewed_ids(stream_key, dims, count, lean):
    grid = rank_table(count, lean)
    lot = jax.random.randint(jax.random.fold_in(stream_key, 1), dims, 0, int(grid[count - 1]))
    standing = jnp.searchsorted(jnp.asarray(grid, jnp.int32), lot, side="right")
    return jax.random.permutation(jax.random.fold_in(stream_key, 2), count)[standing].astype(jnp.int32)


def noise(own_key, shape, deviation, bound, shards=(), kind=jnp.bfloat16):
    drawn = deviation * jax.random.normal(own_key, shape, jnp.float32)
    if shards:
        drawn = drawn * level_of(own_key, shape, shards, -0.22, 0.18)
    return jnp.clip(drawn, -bound, bound).astype(kind)


def setup_inputs(seed: int = 0) -> dict:
    keys = jax.random.split(jax.random.key(seed), 15)
    tokens = noise(keys[0], (SAMPLES, TOK, D), 1.0, 6.0, ((0, 32),))
    features = noise(keys[1], (SAMPLES, STEPS, FR, D), 1.0, 6.0, ((0, 32),))
    proprio = noise(keys[2], (SAMPLES, STEPS, PROP), 1.0, 6.0, ((0, 32),))
    embodiment = place_ends(skewed_ids(keys[3], (SAMPLES,), STEMS, 2), jax.random.fold_in(keys[3], 3), 0, STEMS - 1).astype(jnp.int32)
    trunk_attn = draw_trunk_attn(jax.random.fold_in(keys[14], 71), 0)
    feedforward_up_weight = noise(keys[5], (LAYERS, FF, D), D ** -0.5, 0.5, ((1, 32),))
    mlp_down = noise(keys[6], (LAYERS, FF, D), FF ** -0.5, 0.25, ((1, 32),))
    stem_mats = draw_stem_mats(jax.random.fold_in(keys[14], 71), 0)
    stem_queries = noise(keys[8], (LAYERS, STEMS * SQ, D), 1.0, 6.0, ((1, 32),))
    prop_in = noise(keys[9], (LAYERS, STEMS * PROP, D), PROP ** -0.5, 1.0, ((1, 32),))
    trunk_vectors = draw_trunk_vectors(jax.random.fold_in(keys[14], 71), 0)
    mlp_bias = noise(keys[11], (LAYERS, FF), 0.3, 2.0)
    stem_bias = noise(keys[12], (LAYERS, STEMS, 2, D), 0.3, 2.0)
    cotangent = noise(keys[13], (SAMPLES, TOK, D), 1.0, 6.0, ((0, 32),))
    return dict(tokens=tokens, features=features, proprio=proprio, embodiment=embodiment, trunk_attn=trunk_attn, feedforward_up_weight=feedforward_up_weight, mlp_down=mlp_down, stem_mats=stem_mats, stem_queries=stem_queries, prop_in=prop_in, trunk_vectors=trunk_vectors, mlp_bias=mlp_bias, stem_bias=stem_bias, cotangent=cotangent)


@jax.custom_vjp
def low(v):
    return lax.optimization_barrier(v.astype(jnp.bfloat16)).astype(jnp.float32)

@jax.custom_vjp
def low_back(v):
    return v

def low_keep(v):
    return (low(v), None)

def low_pass(kept, grad):
    return (grad,)

def back_keep(v):
    return (v, None)

def back_low(kept, grad):
    return (low(grad),)
low.defvjp(low_keep, low_pass)
low_back.defvjp(back_keep, back_low)
HIGHEST = lax.Precision.HIGHEST

def layer_norm(values, gain_row, offset_row_vector):
    centred = values - lax.optimization_barrier(jnp.mean(values, -1, keepdims=True))
    inverse = lax.rsqrt(lax.optimization_barrier(jnp.mean(centred * centred, -1, keepdims=True)) + 1e-05)
    return centred * inverse * gain_row + offset_row_vector

def gelu_exact(values):
    return jax.nn.gelu(values, approximate=False)

def one_layer(hidden, features, proprio, embodiment, attn_w, up_w, down_w, stem_w, query_w, pin_w, vectors, mlp_b, stem_b):
    sample_count = hidden.shape[0]
    score_scale = 1.0 / math.sqrt(HD)
    context_rows = FR + 1
    tok_rows = STEPS * SQ
    per_stem = stem_w.reshape(STEMS, D, 4 * D)[embodiment]
    queries = query_w.reshape(STEMS, SQ, D)[embodiment]
    per_input = pin_w.reshape(STEMS, PROP, D)[embodiment]
    per_bias = stem_b[embodiment]
    prop_pre = low_back(jnp.einsum('stp,spd->std', proprio, per_input, precision=HIGHEST) + per_bias[:, 0][:, None, :])
    prop_act = low(gelu_exact(prop_pre))
    prop_row = jnp.einsum('std,sde->ste', prop_act, per_stem[:, :, 3 * D:], precision=HIGHEST) + per_bias[:, 1][:, None, :]
    context = low_back(low(jnp.concatenate([features, prop_row[:, :, None, :]], axis=2)))
    stem_keys = low(low_back(jnp.einsum('stcd,sde->stce', context, per_stem[:, :, :D], precision=HIGHEST)))
    stem_vals = low(low_back(jnp.einsum('stcd,sde->stce', context, per_stem[:, :, D:2 * D], precision=HIGHEST)))
    key_heads = stem_keys.reshape(sample_count, STEPS, context_rows, HEADS, HD)
    val_heads = stem_vals.reshape(sample_count, STEPS, context_rows, HEADS, HD)
    query_heads = queries.reshape(sample_count, SQ, HEADS, HD)
    stem_score = low_back(jnp.einsum('sqhe,stche->sthqc', query_heads, key_heads, precision=HIGHEST) * score_scale)
    stem_prob = low(jax.nn.softmax(stem_score, axis=-1))
    stem_mix = low(low_back(jnp.einsum('sthqc,stche->stqhe', stem_prob, val_heads, precision=HIGHEST).reshape(sample_count, STEPS, SQ, D)))
    stem_out = low_back(jnp.einsum('stqd,sde->stqe', stem_mix, per_stem[:, :, 2 * D:3 * D], precision=HIGHEST))
    first_sum = hidden + stem_out.reshape(sample_count, tok_rows, D)
    normed = low(layer_norm(first_sum, vectors[0], vectors[1]))
    query_t = low(low_back(jnp.einsum('sid,de->sie', normed, attn_w[:D], precision=HIGHEST) + vectors[2]))
    key_t = low(low_back(jnp.einsum('sid,de->sie', normed, attn_w[D:2 * D], precision=HIGHEST)))
    value_t = low(low_back(jnp.einsum('sid,de->sie', normed, attn_w[2 * D:3 * D], precision=HIGHEST) + vectors[3]))
    head_shape = (sample_count, tok_rows, HEADS, HD)
    self_score = low_back(jnp.einsum('sqhe,skhe->shqk', query_t.reshape(head_shape), key_t.reshape(head_shape), precision=HIGHEST) * score_scale)
    self_prob = low(jax.nn.softmax(self_score, axis=-1))
    self_mix = low(low_back(jnp.einsum('shqk,skhe->sqhe', self_prob, value_t.reshape(head_shape), precision=HIGHEST).reshape(sample_count, tok_rows, D)))
    attn_out = low_back(jnp.einsum('sid,de->sie', self_mix, attn_w[3 * D:], precision=HIGHEST) + vectors[4])
    second_sum = first_sum + attn_out
    mlp_in = low(layer_norm(second_sum, vectors[5], vectors[6]))
    mlp_pre = low_back(jnp.einsum('sid,fd->sif', mlp_in, up_w, precision=HIGHEST) + mlp_b)
    mlp_act = low(gelu_exact(mlp_pre))
    mlp_out = low_back(jnp.einsum('sif,fd->sid', mlp_act, down_w, precision=HIGHEST) + vectors[7])
    return second_sum + mlp_out

def reference(tokens, features, proprio, embodiment, trunk_attn, feedforward_up_weight, mlp_down, stem_mats, stem_queries, prop_in, trunk_vectors, mlp_bias, stem_bias, cotangent):
    primal_inputs = tuple((item.astype(jnp.float32) for item in (tokens, features, proprio, trunk_attn, feedforward_up_weight, mlp_down, stem_mats, stem_queries, prop_in, trunk_vectors, mlp_bias, stem_bias)))

    def forward(tok_in, feat_in, prop_state, attn_all, up_all, down_all, stem_all, query_stacked_rows, pin_all, vector_all, mbias_all, sbias_all):
        hidden = tok_in
        for layer_index in range(LAYERS):
            hidden = one_layer(hidden, feat_in, prop_state, embodiment, attn_all[layer_index], up_all[layer_index], down_all[layer_index], stem_all[layer_index], query_stacked_rows[layer_index], pin_all[layer_index], vector_all[layer_index], mbias_all[layer_index], sbias_all[layer_index])
        return hidden
    result, back_fn = jax.vjp(forward, *primal_inputs)
    grads = back_fn(cotangent.astype(jnp.float32))
    return (result.astype(jnp.bfloat16), grads[0], grads[1], grads[2], grads[3], grads[4], grads[5], grads[6], grads[7], grads[8], grads[9], grads[10], grads[11])
```

```python
import functools
import math

import jax
import jax.numpy as jnp
from jax import lax
from jax.experimental import pallas as pl
from jax.experimental.pallas import tpu as pltpu
from jax.sharding import PartitionSpec as P

D = 128
HEADS = 8
HD = 16
FF = 512
SQ = 16
FR = 49
CR = 64
PROP = 32
PR = 16
STEMS = 32
STEPS = 2
LAYERS = 2
TOK = 32
SB = 8

R_Q = 4 * D
R_PIN = R_Q + SQ
R_ATT = R_PIN + PROP
R_UP = R_ATT + 16
R_DOWN = R_UP + 16
ROWS = R_DOWN + 16
STEM_ROWS = R_ATT

F32 = jnp.float32
BF16 = jnp.bfloat16
VMEM_LIMIT = 60 * 1024 * 1024


def dot(a, b):
    return lax.dot_general(a, b, (((1,), (0,)), ((), ())), preferred_element_type=F32)


def dot_nt(a, b):
    return lax.dot_general(a, b, (((1,), (1,)), ((), ())), preferred_element_type=F32)


def dot_tn(a, b):
    return lax.dot_general(a, b, (((0,), (0,)), ((), ())), preferred_element_type=F32)


def gelu_parts(x):
    cdf = 0.5 + 0.5 * lax.erf(x * math.sqrt(0.5))
    slope = cdf + x * (jnp.exp(-0.5 * x * x) * (1.0 / math.sqrt(2.0 * math.pi)))
    return x * cdf, slope


def norm_parts(x):
    centred = x - jnp.mean(x, -1, keepdims=True)
    inverse = lax.rsqrt(jnp.mean(centred * centred, -1, keepdims=True) + 1e-05)
    return centred * inverse, inverse


def norm_back(grad, gain, hat, inverse):
    g = grad * gain
    return inverse * (
        g - jnp.mean(g, -1, keepdims=True) - hat * jnp.mean(g * hat, -1, keepdims=True)
    )


def head_mask(rows, value):
    row = lax.broadcasted_iota(jnp.int32, (HEADS * rows, D), 0) // rows
    lane = lax.broadcasted_iota(jnp.int32, (HEADS * rows, D), 1) // HD
    return jnp.where(row == lane, value, 0.0).astype(BF16)


def expand(rows, mask):
    return jnp.concatenate([rows] * HEADS, 0) * mask


def contract(wide, rows):
    lane = lax.broadcasted_iota(jnp.int32, (rows, D), 1) // HD
    out = wide[:rows]
    for head in range(1, HEADS):
        out = jnp.where(lane == head, wide[head * rows : (head + 1) * rows], out)
    return out


def fold(x):
    return jnp.sum(x.reshape(x.shape[0] // 8, 8, x.shape[1]), 0)


def trunk_weights(w_ref):
    attn = w_ref[:, R_ATT:R_UP, :].reshape(4 * D, D)
    up = w_ref[:, R_UP:R_DOWN, :].reshape(FF, D)
    down = w_ref[:, R_DOWN:ROWS, :].reshape(FF, D)
    wqkv = jnp.concatenate([attn[:D], attn[D : 2 * D], attn[2 * D : 3 * D]], 1)
    return wqkv, attn[3 * D :], up, down


def stem_kv_weight(w_ref, e):
    return jnp.concatenate([w_ref[e, 0:D, :], w_ref[e, D : 2 * D, :]], 1)


def softmax_rows(score):
    top = jnp.max(score, 0, keepdims=True)
    weight = jnp.exp(score - top)
    return weight * (1.0 / jnp.sum(weight, 0, keepdims=True))


def forward_block(es, hidden, feat_ref, prop_ref, w_ref, vec, mb, sb_ref):
    kept = {}
    pre = [
        dot(prop_ref[j].astype(BF16), w_ref[e, R_PIN:R_ATT, :]) + sb_ref[e, 0:1, :]
        for j, e in enumerate(es)
    ]
    pact, pslope = gelu_parts(jnp.concatenate(pre, 0))
    pact = pact.astype(BF16)
    kept["pact"], kept["pslope"] = pact, pslope
    row16 = lax.broadcasted_iota(jnp.int32, (16, D), 0)
    contexts = []
    for j, e in enumerate(es):
        prow = dot(pact[j * PR : (j + 1) * PR], w_ref[e, 3 * D : 4 * D, :]) + sb_ref[e, 1:2, :]
        parts = []
        for t in range(STEPS):
            last = feat_ref[j, t, 48:49, :].astype(F32)
            tail = jnp.where(row16 == 0, last, jnp.where(row16 == 1, prow[t : t + 1], 0.0))
            parts += [feat_ref[j, t, 0:48, :], tail.astype(BF16)]
        contexts.append(jnp.concatenate(parts, 0))
    kept["ctx"] = contexts
    kvs = [dot(contexts[j], stem_kv_weight(w_ref, e)).astype(BF16) for j, e in enumerate(es)]
    kept["kv"] = kvs
    mask16 = head_mask(SQ, 0.25)
    scores = [
        dot_nt(kvs[j][:, :D], expand(w_ref[e, R_Q:R_PIN, :], mask16)) for j, e in enumerate(es)
    ]
    row8 = lax.broadcasted_iota(jnp.int32, (56, D), 0)
    pad = jnp.zeros((8, D), F32)
    probs = []
    for j in range(SB):
        parts = []
        for t in range(STEPS):
            s = scores[j][t * CR : t * CR + 56]
            parts += [softmax_rows(jnp.where(row8 < FR + 1, s, -1e30)), pad]
        probs.append(jnp.concatenate(parts, 0))
    kept["prob"] = probs
    mixes = []
    for j in range(SB):
        low = probs[j].astype(BF16)
        mixes += [
            contract(
                dot_tn(low[t * CR : (t + 1) * CR], kvs[j][t * CR : (t + 1) * CR, D:]), SQ
            ).astype(BF16)
            for t in range(STEPS)
        ]
    mix = jnp.concatenate(mixes, 0)
    kept["mix"] = mix
    outs = [
        dot(mix[j * TOK : (j + 1) * TOK], w_ref[e, 2 * D : 3 * D, :]) for j, e in enumerate(es)
    ]
    first = hidden + jnp.concatenate(outs, 0)
    kept["first"] = first
    wqkv, wout, up, down = trunk_weights(w_ref)
    normed = (norm_parts(first)[0] * vec[0:1] + vec[1:2]).astype(BF16)
    bias = jnp.concatenate([vec[2:3], jnp.zeros((1, D), F32), vec[3:4]], 1)
    qkv = (dot(normed, wqkv) + bias).astype(BF16)
    kept["qkv"] = qkv
    mask32 = head_mask(TOK, 0.25)
    sprobs = []
    smixes = []
    for j in range(SB):
        rows = qkv[j * TOK : (j + 1) * TOK]
        p = softmax_rows(dot_nt(rows[:, D : 2 * D], expand(rows[:, :D], mask32)))
        sprobs.append(p)
        smixes.append(contract(dot_tn(p.astype(BF16), rows[:, 2 * D :]), TOK).astype(BF16))
    kept["sprob"] = sprobs
    smix = jnp.concatenate(smixes, 0)
    kept["smix"] = smix
    second = first + (dot(smix, wout) + vec[4:5])
    kept["second"] = second
    mlp_in = (norm_parts(second)[0] * vec[5:6] + vec[6:7]).astype(BF16)
    act, slope = gelu_parts(dot_nt(mlp_in, up) + mb)
    act = act.astype(BF16)
    kept["act"], kept["slope"] = act, slope
    return second + (dot(act, down) + vec[7:8]), kept


def backward_block(es, grad, kept, prop_ref, w_ref, vec, acc):
    wqkv, wout, up, down = trunk_weights(w_ref)
    out_low = grad.astype(BF16)
    acc["vec"][7] += fold(out_low.astype(F32))
    acc["down"][...] += dot_tn(out_low, kept["act"])
    grad_act = dot_nt(out_low, down)
    grad_pre = (grad_act * kept["slope"].astype(F32)).astype(BF16)
    acc["mb"][...] += fold(grad_pre.astype(F32))
    hat, inverse = norm_parts(kept["second"])
    mlp_in = (hat * vec[5:6] + vec[6:7]).astype(BF16)
    acc["up"][...] += dot_tn(mlp_in, grad_pre)
    grad_in = dot(grad_pre, up)
    acc["vec"][5] += fold(grad_in * hat)
    acc["vec"][6] += fold(grad_in)
    grad_second = grad + norm_back(grad_in, vec[5:6], hat, inverse)
    branch = grad_second.astype(BF16)
    acc["vec"][4] += fold(branch.astype(F32))
    acc["wout"][...] += dot_tn(kept["smix"], branch)
    grad_mix = dot_nt(branch, wout).astype(BF16)
    mask32 = head_mask(TOK, 0.25)
    mask32_one = head_mask(TOK, 1.0)
    grads_q, grads_k, grads_v = [], [], []
    for j in range(SB):
        rows = kept["qkv"][j * TOK : (j + 1) * TOK]
        p = kept["sprob"][j]
        wide = expand(grad_mix[j * TOK : (j + 1) * TOK], mask32_one)
        grad_p = dot_nt(rows[:, 2 * D :], wide)
        grads_v.append(dot(p.astype(BF16), wide))
        p = p.astype(F32)
        gs = (p * (grad_p - jnp.sum(grad_p * p, 0, keepdims=True))).astype(BF16)
        grads_q.append(contract(dot_tn(gs, rows[:, D : 2 * D]), TOK) * 0.25)
        grads_k.append(dot(gs, expand(rows[:, :D], mask32)))
    grad_qkv = jnp.concatenate(
        [jnp.concatenate(g, 0).astype(BF16) for g in (grads_q, grads_k, grads_v)], 1
    )
    acc["vec"][2] += fold(grad_qkv[:, :D].astype(F32))
    acc["vec"][3] += fold(grad_qkv[:, 2 * D :].astype(F32))
    hat, inverse = norm_parts(kept["first"])
    normed = (hat * vec[0:1] + vec[1:2]).astype(BF16)
    acc["wqkv"][...] += dot_tn(normed, grad_qkv)
    grad_normed = dot_nt(grad_qkv, wqkv)
    acc["vec"][0] += fold(grad_normed * hat)
    acc["vec"][1] += fold(grad_normed)
    grad_first = grad_second + norm_back(grad_normed, vec[0:1], hat, inverse)
    stem_grad = grad_first.astype(BF16)
    mask16 = head_mask(SQ, 0.25)
    mask16_one = head_mask(SQ, 1.0)
    row16 = lax.broadcasted_iota(jnp.int32, (PR, D), 0)
    grad_contexts, grad_props = [], []
    for j, e in enumerate(es):
        g = stem_grad[j * TOK : (j + 1) * TOK]
        grad_wo = dot_tn(kept["mix"][j * TOK : (j + 1) * TOK], g)
        gmix = dot_nt(g, w_ref[e, 2 * D : 3 * D, :]).astype(BF16)
        kv = kept["kv"][j]
        p = kept["prob"][j]
        p_low = p.astype(BF16)
        p = p.astype(F32)
        gss, gvs = [], []
        for t in range(STEPS):
            wide = expand(gmix[t * SQ : (t + 1) * SQ], mask16_one)
            grad_p = dot_nt(kv[t * CR : (t + 1) * CR, D:], wide)
            gvs.append(dot(p_low[t * CR : (t + 1) * CR], wide))
            pt = p[t * CR : (t + 1) * CR]
            gss.append(pt * (grad_p - jnp.sum(grad_p * pt, 0, keepdims=True)))
        gs = jnp.concatenate(gss, 0).astype(BF16)
        grad_q = contract(dot_tn(gs, kv[:, :D]), SQ) * 0.25
        gk = dot(gs, expand(w_ref[e, R_Q:R_PIN, :], mask16))
        gkv = jnp.concatenate([gk, jnp.concatenate(gvs, 0)], 1).astype(BF16)
        grad_wkv = dot_tn(kept["ctx"][j], gkv)
        grad_ctx = dot_nt(gkv, stem_kv_weight(w_ref, e)).astype(BF16)
        grad_contexts.append(grad_ctx)
        wide_ctx = grad_ctx.astype(F32)
        prow = jnp.where(
            row16 == 0,
            wide_ctx[FR : FR + 1],
            jnp.where(row16 == 1, wide_ctx[CR + FR : CR + FR + 1], 0.0),
        )
        prow_low = prow.astype(BF16)
        pact = kept["pact"][j * PR : (j + 1) * PR]
        grad_wp = dot_tn(pact, prow_low)
        gpact = dot_nt(prow_low, w_ref[e, 3 * D : 4 * D, :])
        gppre = (gpact * kept["pslope"][j * PR : (j + 1) * PR]).astype(BF16)
        grad_pin = dot_tn(prop_ref[j].astype(BF16), gppre)
        grad_props.append(dot_nt(gppre, w_ref[e, R_PIN:R_ATT, :]))
        stem = acc["stem"]
        stem[e, 0:D, :] += grad_wkv[:, :D]
        stem[e, D : 2 * D, :] += grad_wkv[:, D:]
        stem[e, 2 * D : 3 * D, :] += grad_wo
        stem[e, 3 * D : 4 * D, :] += grad_wp
        stem[e, R_Q:R_PIN, :] += grad_q
        stem[e, R_PIN:R_ATT, :] += grad_pin
        acc["sb"][e, 0:1, :] += jnp.sum(gppre.astype(F32), 0, keepdims=True)
        acc["sb"][e, 1:2, :] += jnp.sum(prow, 0, keepdims=True)
    return grad_first, grad_contexts, grad_props


ACC = ("stem", "sb", "wqkv", "wout", "up", "down", "vec", "mb")


def acc_shapes():
    return [
        pltpu.VMEM((STEMS, STEM_ROWS, D), F32),
        pltpu.VMEM((STEMS, 2, D), F32),
        pltpu.VMEM((D, 3 * D), F32),
        pltpu.VMEM((D, D), F32),
        pltpu.VMEM((D, FF), F32),
        pltpu.VMEM((D, FF), F32),
        pltpu.VMEM((8, 8, D), F32),
        pltpu.VMEM((8, FF), F32),
    ]


def clear(acc):
    for ref in acc.values():
        ref[...] = jnp.zeros(ref.shape, ref.dtype)


def finish(acc, grad_ref, vec_ref, mb_ref, sb_ref):
    def stem_out(e, carry):
        grad_ref[e, 0:STEM_ROWS, :] = acc["stem"][e].astype(grad_ref.dtype)
        return carry

    lax.fori_loop(0, STEMS, stem_out, 0)
    wqkv = acc["wqkv"][...]
    attn = [wqkv[:, :D], wqkv[:, D : 2 * D], wqkv[:, 2 * D :], acc["wout"][...]]
    for block in range(4):
        grad_ref[block * 8 : block * 8 + 8, R_ATT:R_UP, :] = (
            attn[block].astype(grad_ref.dtype).reshape(8, 16, D)
        )
    grad_ref[:, R_UP:R_DOWN, :] = acc["up"][...].T.astype(grad_ref.dtype).reshape(STEMS, 16, D)
    grad_ref[:, R_DOWN:ROWS, :] = acc["down"][...].T.astype(grad_ref.dtype).reshape(STEMS, 16, D)
    vec_ref[...] = jnp.sum(acc["vec"][...], 1)
    mb_ref[...] = jnp.sum(acc["mb"][...], 0, keepdims=True)
    sb_ref[...] = acc["sb"][...]


SAVED = ("ctx", "kv", "prob", "mix", "first", "qkv", "sprob", "smix", "second", "act", "slope", "pact", "pslope")
PER_SAMPLE = ("ctx", "kv", "prob", "sprob")


def saved_shapes(samples):
    rows = samples * TOK
    return dict(
        ctx=((samples, STEPS * CR, D), BF16),
        kv=((samples, STEPS * CR, 2 * D), BF16),
        prob=((samples, STEPS * CR, D), BF16),
        mix=((rows, D), BF16),
        first=((rows, D), F32),
        qkv=((rows, 3 * D), BF16),
        sprob=((samples, TOK, HEADS * TOK), BF16),
        smix=((rows, D), BF16),
        second=((rows, D), F32),
        act=((rows, FF), BF16),
        slope=((rows, FF), BF16),
        pact=((samples * PR, D), BF16),
        pslope=((samples * PR, D), F32),
    )


def forward_kernel(emb_ref, tok_ref, feat_ref, prop_ref, w_ref, vec_ref, mb_ref, sb_ref, out_ref, *saved):
    step = pl.program_id(0)
    es = [emb_ref[step * SB + j] for j in range(SB)]
    out, kept = forward_block(
        es, tok_ref[...].astype(F32), feat_ref, prop_ref, w_ref, vec_ref[...], mb_ref[...], sb_ref
    )
    out_ref[...] = out
    for name, ref in zip(SAVED, saved):
        if name in PER_SAMPLE:
            for j in range(SB):
                ref[j] = kept[name][j].astype(ref.dtype)
        else:
            ref[...] = kept[name].astype(ref.dtype)


def middle_kernel(
    emb_ref, hid_ref, feat_ref, prop_ref, w_ref, vec_ref, mb_ref, sb_ref, cot_ref,
    out_ref, ghid_ref, gfeat_ref, gprop_ref, gw_ref, gvec_ref, gmb_ref, gsb_ref, *accs
):
    step = pl.program_id(0)
    acc = dict(zip(ACC, accs))
    pl.when(step == 0)(lambda: clear(acc))
    es = [emb_ref[step * SB + j] for j in range(SB)]
    vec = vec_ref[...]
    out, kept = forward_block(es, hid_ref[...], feat_ref, prop_ref, w_ref, vec, mb_ref[...], sb_ref)
    out_ref[...] = out.astype(BF16)
    ghid, gctx, gprop = backward_block(
        es, cot_ref[...].astype(F32), kept, prop_ref, w_ref, vec, acc
    )
    ghid_ref[...] = ghid
    for j in range(SB):
        gfeat_ref[j] = gctx[j]
        gprop_ref[j] = gprop[j]
    pl.when(step == pl.num_programs(0) - 1)(lambda: finish(acc, gw_ref, gvec_ref, gmb_ref, gsb_ref))


def backward_kernel(emb_ref, grad_ref, prop_ref, w_ref, vec_ref, gfeat1_ref, gprop1_ref, *rest):
    saved = rest[: len(SAVED)]
    gtok_ref, gfeat_ref, gprop_ref, gw_ref, gvec_ref, gmb_ref, gsb_ref = rest[len(SAVED) : len(SAVED) + 7]
    acc = dict(zip(ACC, rest[len(SAVED) + 7 :]))
    step = pl.program_id(0)
    pl.when(step == 0)(lambda: clear(acc))
    es = [emb_ref[step * SB + j] for j in range(SB)]
    kept = {name: ref if name in PER_SAMPLE else ref[...] for name, ref in zip(SAVED, saved)}
    ghid, gctx, gprop = backward_block(es, grad_ref[...], kept, prop_ref, w_ref, vec_ref[...], acc)
    gtok_ref[...] = ghid
    for j in range(SB):
        total = gctx[j].astype(F32) + gfeat1_ref[j].astype(F32)
        for t in range(STEPS):
            gfeat_ref[j, t] = total[t * CR : t * CR + FR]
        gprop_ref[j] = (gprop[j] + gprop1_ref[j])[:STEPS]
    pl.when(step == pl.num_programs(0) - 1)(lambda: finish(acc, gw_ref, gvec_ref, gmb_ref, gsb_ref))


def blocked(shape, per_step):
    block = (per_step,) + tuple(shape[1:])
    zeros = (0,) * (len(shape) - 1)
    return pl.BlockSpec(block, lambda i, *_: (i,) + zeros)


def whole(shape):
    zeros = (0,) * len(shape)
    return pl.BlockSpec(tuple(shape), lambda i, *_: zeros, pipeline_mode=pl.Buffered(1))


def call(kernel, steps, emb, ins, outs, scratch):
    return pl.pallas_call(
        kernel,
        grid_spec=pltpu.PrefetchScalarGridSpec(
            num_scalar_prefetch=1,
            grid=(steps,),
            in_specs=[blocked(a.shape, n) if n else whole(a.shape) for a, n in ins],
            out_specs=[blocked(s, n) if n else whole(s) for s, _, n in outs],
            scratch_shapes=scratch,
        ),
        out_shape=[jax.ShapeDtypeStruct(s, d) for s, d, _ in outs],
        compiler_params=pltpu.CompilerParams(
            dimension_semantics=("arbitrary",), vmem_limit_bytes=VMEM_LIMIT
        ),
    )(emb, *[a for a, _ in ins])


def compute(tokens, features, proprio, emb, w0, w1, vecs, mbs, sbs, cot, wire):
    samples = emb.shape[0]
    steps = samples // SB
    rows = samples * TOK
    rb = SB * TOK
    tok = tokens.reshape(rows, D)
    prop = jnp.pad(proprio.astype(F32), ((0, 0), (0, PR - STEPS), (0, 0)))
    shapes = saved_shapes(samples)
    per = lambda s: s[0] // steps
    saved_outs = [(shapes[n][0], shapes[n][1], per(shapes[n][0])) for n in SAVED]
    res = call(
        forward_kernel, steps, emb,
        [(tok, rb), (features, SB), (prop, SB), (w0, 0), (vecs[0], 0), (mbs[0], 0), (sbs[0], 0)],
        [((rows, D), F32, rb)] + saved_outs, [],
    )
    hidden, saved = res[0], res[1:]
    grad_outs = [
        ((STEMS, ROWS, D), wire, 0), ((8, D), F32, 0), ((1, FF), F32, 0), ((STEMS, 2, D), F32, 0)
    ]
    out, ghid, gfeat1, gprop1, *grads1 = call(
        middle_kernel, steps, emb,
        [(hidden, rb), (features, SB), (prop, SB), (w1, 0), (vecs[1], 0), (mbs[1], 0), (sbs[1], 0),
         (cot.reshape(rows, D), rb)],
        [((rows, D), BF16, rb), ((rows, D), F32, rb), ((samples, STEPS * CR, D), BF16, SB),
         ((samples, PR, PROP), F32, SB)] + grad_outs,
        acc_shapes(),
    )
    gtok, gfeat, gprop, *grads0 = call(
        backward_kernel, steps, emb,
        [(ghid, rb), (prop, SB), (w0, 0), (vecs[0], 0), (gfeat1, SB), (gprop1, SB)]
        + [(a, per(a.shape)) for a in saved],
        [((rows, D), F32, rb), ((samples, STEPS, FR, D), F32, SB), ((samples, STEPS, PROP), F32, SB)]
        + grad_outs,
        acc_shapes(),
    )
    return (
        out.reshape(tokens.shape), gtok.reshape(tokens.shape), gfeat, gprop, grads0, grads1
    )


def pack(attn, up, down, stem, queries, pin, n):
    gathered = [lax.all_gather(a, "fsdp", axis=1, tiled=True) for a in (attn, up, down, stem, queries, pin)]
    attn, up, down, stem, queries, pin = gathered
    stem = stem.reshape(LAYERS, STEMS, D, 4, D).transpose(0, 1, 3, 2, 4).reshape(LAYERS, STEMS, 4 * D, D)
    parts = [stem] + [a.reshape(LAYERS, STEMS, -1, D) for a in (queries, pin, attn, up, down)]
    return jnp.concatenate(parts, 2)


def unpack_blocks(grad):
    lead = grad.shape[:-2]
    stem = grad[..., : 4 * D, :].reshape(lead + (4, D, D))
    stem = jnp.swapaxes(stem, -3, -2).reshape(lead + (D, 4 * D))
    return (
        grad[..., R_ATT:R_UP, :], grad[..., R_UP:R_DOWN, :], grad[..., R_DOWN:ROWS, :],
        stem, grad[..., R_Q:R_PIN, :], grad[..., R_PIN:R_ATT, :],
    )


def body(n, tokens, features, proprio, embodiment, trunk_attn, feedforward_up_weight, mlp_down,
         stem_mats, stem_queries, prop_in, trunk_vectors, mlp_bias, stem_bias, cotangent):
    if n == STEMS:
        stem = stem_mats.reshape(LAYERS, D, 4, D).transpose(0, 2, 1, 3).reshape(LAYERS, 4 * D, D)
        packed = jnp.concatenate(
            [stem, stem_queries, prop_in, trunk_attn, feedforward_up_weight, mlp_down], 1
        )
        w = lax.all_gather(packed, "fsdp", axis=1)
    else:
        w = pack(trunk_attn, feedforward_up_weight, mlp_down, stem_mats, stem_queries, prop_in, n)
    vecs = trunk_vectors.astype(F32)
    mbs = mlp_bias.astype(F32).reshape(LAYERS, 1, FF)
    sbs = stem_bias.astype(F32)
    out, gtok, gfeat, gprop, g0, g1 = compute(
        tokens, features, proprio, embodiment, w[0], w[1], vecs, mbs, sbs, cotangent, F32
    )
    grads = jnp.stack([g0[0], g1[0]])
    if n == STEMS:
        mine = lax.psum_scatter(grads, "fsdp", scatter_dimension=1, tiled=True)
        mats = [a[:, 0] for a in unpack_blocks(mine)]
    else:
        mats = [
            lax.psum_scatter(a.reshape(LAYERS, -1, a.shape[-1]), "fsdp", scatter_dimension=1, tiled=True)
            for a in unpack_blocks(grads)
        ]
    small = lax.psum(tuple(jnp.stack([a, b]) for a, b in zip(g0[1:], g1[1:])), "fsdp")
    return (out, gtok, gfeat, gprop, *mats, small[0], small[1].reshape(LAYERS, FF), small[2])


def solution(mesh):
    n = mesh.shape["fsdp"]
    return jax.shard_map(
        functools.partial(body, n),
        mesh=mesh,
        in_specs=(
            P("fsdp"), P("fsdp"), P("fsdp"), P("fsdp"),
            P(None, "fsdp"), P(None, "fsdp"), P(None, "fsdp"), P(None, "fsdp"), P(None, "fsdp"),
            P(None, "fsdp"), P(), P(), P(), P("fsdp"),
        ),
        out_specs=(
            P("fsdp"), P("fsdp"), P("fsdp"), P("fsdp"),
            P(None, "fsdp"), P(None, "fsdp"), P(None, "fsdp"), P(None, "fsdp"), P(None, "fsdp"),
            P(None, "fsdp"), P(), P(), P(),
        ),
        check_vma=False,
    )
```

```python
import functools
import math

import jax
import jax.numpy as jnp
from jax import lax
from jax.experimental import pallas as pl
from jax.experimental.pallas import tpu as pltpu
from jax.sharding import PartitionSpec as P

D = 128
HEADS = 8
HD = 16
FF = 512
SQ = 16
FR = 49
CR = 64
PROP = 32
PR = 16
STEMS = 32
STEPS = 2
LAYERS = 2
TOK = 32
SB = 8

R_Q = 4 * D
R_PIN = R_Q + SQ
R_ATT = R_PIN + PROP
R_UP = R_ATT + 16
R_DOWN = R_UP + 16
ROWS = R_DOWN + 16
STEM_ROWS = R_ATT
SMALL = 16 + 2 * STEMS

F32 = jnp.float32
BF16 = jnp.bfloat16
VMEM_LIMIT = 60 * 1024 * 1024


def dot(a, b):
    return lax.dot_general(a, b, (((1,), (0,)), ((), ())), preferred_element_type=F32)


def dot_nt(a, b):
    return lax.dot_general(a, b, (((1,), (1,)), ((), ())), preferred_element_type=F32)


def dot_tn(a, b):
    return lax.dot_general(a, b, (((0,), (0,)), ((), ())), preferred_element_type=F32)


def gelu_parts(x):
    cdf = 0.5 + 0.5 * lax.erf(x * math.sqrt(0.5))
    slope = cdf + x * (jnp.exp(-0.5 * x * x) * (1.0 / math.sqrt(2.0 * math.pi)))
    return x * cdf, slope


def norm_parts(x):
    centred = x - jnp.mean(x, -1, keepdims=True)
    inverse = lax.rsqrt(jnp.mean(centred * centred, -1, keepdims=True) + 1e-05)
    return centred * inverse, inverse


def norm_back(grad, gain, hat, inverse):
    g = grad * gain
    return inverse * (
        g - jnp.mean(g, -1, keepdims=True) - hat * jnp.mean(g * hat, -1, keepdims=True)
    )


def head_mask(rows, value):
    row = lax.broadcasted_iota(jnp.int32, (HEADS * rows, D), 0) // rows
    lane = lax.broadcasted_iota(jnp.int32, (HEADS * rows, D), 1) // HD
    return jnp.where(row == lane, value, 0.0).astype(BF16)


def expand(rows, mask):
    return jnp.concatenate([rows] * HEADS, 0) * mask


def contract(wide, rows):
    lane = lax.broadcasted_iota(jnp.int32, (rows, D), 1) // HD
    out = wide[:rows]
    for head in range(1, HEADS):
        out = jnp.where(lane == head, wide[head * rows : (head + 1) * rows], out)
    return out


def fold(x):
    return jnp.sum(x.reshape(x.shape[0] // 8, 8, x.shape[1]), 0)


def trunk_weights(w_ref):
    attn = w_ref[:, R_ATT:R_UP, :].reshape(4 * D, D)
    up = w_ref[:, R_UP:R_DOWN, :].reshape(FF, D)
    down = w_ref[:, R_DOWN:ROWS, :].reshape(FF, D)
    wqkv = jnp.concatenate([attn[:D], attn[D : 2 * D], attn[2 * D : 3 * D]], 1)
    return wqkv, attn[3 * D :], up, down


def stem_kv_weight(w_ref, e):
    return jnp.concatenate([w_ref[e, 0:D, :], w_ref[e, D : 2 * D, :]], 1)


def softmax_rows(score):
    top = jnp.max(score, 0, keepdims=True)
    weight = jnp.exp(score - top)
    return weight * (1.0 / jnp.sum(weight, 0, keepdims=True))


def forward_block(es, hidden, feat_ref, prop_ref, w_ref, vec, mb, sb_ref):
    kept = {}
    pre = [
        dot(prop_ref[j].astype(BF16), w_ref[e, R_PIN:R_ATT, :]) + sb_ref[e, 0:1, :]
        for j, e in enumerate(es)
    ]
    pact, pslope = gelu_parts(jnp.concatenate(pre, 0))
    pact = pact.astype(BF16)
    kept["pact"], kept["pslope"] = pact, pslope
    row16 = lax.broadcasted_iota(jnp.int32, (16, D), 0)
    contexts = []
    for j, e in enumerate(es):
        prow = dot(pact[j * PR : (j + 1) * PR], w_ref[e, 3 * D : 4 * D, :]) + sb_ref[e, 1:2, :]
        parts = []
        for t in range(STEPS):
            last = feat_ref[j, t, 48:49, :].astype(F32)
            tail = jnp.where(row16 == 0, last, jnp.where(row16 == 1, prow[t : t + 1], 0.0))
            parts += [feat_ref[j, t, 0:48, :], tail.astype(BF16)]
        contexts.append(jnp.concatenate(parts, 0))
    kept["ctx"] = contexts
    kvs = [dot(contexts[j], stem_kv_weight(w_ref, e)).astype(BF16) for j, e in enumerate(es)]
    kept["kv"] = kvs
    mask16 = head_mask(SQ, 0.25)
    scores = [
        dot_nt(kvs[j][:, :D], expand(w_ref[e, R_Q:R_PIN, :], mask16)) for j, e in enumerate(es)
    ]
    row8 = lax.broadcasted_iota(jnp.int32, (56, D), 0)
    pad = jnp.zeros((8, D), F32)
    probs = []
    for j in range(SB):
        parts = []
        for t in range(STEPS):
            s = scores[j][t * CR : t * CR + 56]
            parts += [softmax_rows(jnp.where(row8 < FR + 1, s, -1e30)), pad]
        probs.append(jnp.concatenate(parts, 0))
    kept["prob"] = probs
    mixes = []
    for j in range(SB):
        low = probs[j].astype(BF16)
        mixes += [
            contract(
                dot_tn(low[t * CR : (t + 1) * CR], kvs[j][t * CR : (t + 1) * CR, D:]), SQ
            ).astype(BF16)
            for t in range(STEPS)
        ]
    mix = jnp.concatenate(mixes, 0)
    kept["mix"] = mix
    outs = [
        dot(mix[j * TOK : (j + 1) * TOK], w_ref[e, 2 * D : 3 * D, :]) for j, e in enumerate(es)
    ]
    first = hidden + jnp.concatenate(outs, 0)
    kept["first"] = first
    wqkv, wout, up, down = trunk_weights(w_ref)
    normed = (norm_parts(first)[0] * vec[0:1] + vec[1:2]).astype(BF16)
    bias = jnp.concatenate([vec[2:3], jnp.zeros((1, D), F32), vec[3:4]], 1)
    qkv = (dot(normed, wqkv) + bias).astype(BF16)
    kept["qkv"] = qkv
    mask32 = head_mask(TOK, 0.25)
    sprobs = []
    smixes = []
    for j in range(SB):
        rows = qkv[j * TOK : (j + 1) * TOK]
        p = softmax_rows(dot_nt(rows[:, D : 2 * D], expand(rows[:, :D], mask32)))
        sprobs.append(p)
        smixes.append(contract(dot_tn(p.astype(BF16), rows[:, 2 * D :]), TOK).astype(BF16))
    kept["sprob"] = sprobs
    smix = jnp.concatenate(smixes, 0)
    kept["smix"] = smix
    second = first + (dot(smix, wout) + vec[4:5])
    kept["second"] = second
    mlp_in = (norm_parts(second)[0] * vec[5:6] + vec[6:7]).astype(BF16)
    act, slope = gelu_parts(dot_nt(mlp_in, up) + mb)
    act = act.astype(BF16)
    kept["act"], kept["slope"] = act, slope
    return second + (dot(act, down) + vec[7:8]), kept


def backward_block(es, grad, kept, prop_ref, w_ref, vec, acc):
    wqkv, wout, up, down = trunk_weights(w_ref)
    out_low = grad.astype(BF16)
    acc["vec"][7] += fold(out_low.astype(F32))
    acc["down"][...] += dot_tn(out_low, kept["act"])
    grad_act = dot_nt(out_low, down)
    grad_pre = (grad_act * kept["slope"].astype(F32)).astype(BF16)
    acc["mb"][...] += fold(grad_pre.astype(F32))
    hat, inverse = norm_parts(kept["second"])
    mlp_in = (hat * vec[5:6] + vec[6:7]).astype(BF16)
    acc["up"][...] += dot_tn(mlp_in, grad_pre)
    grad_in = dot(grad_pre, up)
    acc["vec"][5] += fold(grad_in * hat)
    acc["vec"][6] += fold(grad_in)
    grad_second = grad + norm_back(grad_in, vec[5:6], hat, inverse)
    branch = grad_second.astype(BF16)
    acc["vec"][4] += fold(branch.astype(F32))
    acc["wout"][...] += dot_tn(kept["smix"], branch)
    grad_mix = dot_nt(branch, wout).astype(BF16)
    mask32 = head_mask(TOK, 0.25)
    mask32_one = head_mask(TOK, 1.0)
    grads_q, grads_k, grads_v = [], [], []
    for j in range(SB):
        rows = kept["qkv"][j * TOK : (j + 1) * TOK]
        p = kept["sprob"][j]
        wide = expand(grad_mix[j * TOK : (j + 1) * TOK], mask32_one)
        grad_p = dot_nt(rows[:, 2 * D :], wide)
        grads_v.append(dot(p.astype(BF16), wide))
        p = p.astype(F32)
        gs = (p * (grad_p - jnp.sum(grad_p * p, 0, keepdims=True))).astype(BF16)
        grads_q.append(contract(dot_tn(gs, rows[:, D : 2 * D]), TOK) * 0.25)
        grads_k.append(dot(gs, expand(rows[:, :D], mask32)))
    grad_qkv = jnp.concatenate(
        [jnp.concatenate(g, 0).astype(BF16) for g in (grads_q, grads_k, grads_v)], 1
    )
    acc["vec"][2] += fold(grad_qkv[:, :D].astype(F32))
    acc["vec"][3] += fold(grad_qkv[:, 2 * D :].astype(F32))
    hat, inverse = norm_parts(kept["first"])
    normed = (hat * vec[0:1] + vec[1:2]).astype(BF16)
    acc["wqkv"][...] += dot_tn(normed, grad_qkv)
    grad_normed = dot_nt(grad_qkv, wqkv)
    acc["vec"][0] += fold(grad_normed * hat)
    acc["vec"][1] += fold(grad_normed)
    grad_first = grad_second + norm_back(grad_normed, vec[0:1], hat, inverse)
    stem_grad = grad_first.astype(BF16)
    mask16 = head_mask(SQ, 0.25)
    mask16_one = head_mask(SQ, 1.0)
    row16 = lax.broadcasted_iota(jnp.int32, (PR, D), 0)
    grad_contexts, grad_props = [], []
    for j, e in enumerate(es):
        g = stem_grad[j * TOK : (j + 1) * TOK]
        grad_wo = dot_tn(kept["mix"][j * TOK : (j + 1) * TOK], g)
        gmix = dot_nt(g, w_ref[e, 2 * D : 3 * D, :]).astype(BF16)
        kv = kept["kv"][j]
        p = kept["prob"][j]
        p_low = p.astype(BF16)
        p = p.astype(F32)
        gss, gvs = [], []
        for t in range(STEPS):
            wide = expand(gmix[t * SQ : (t + 1) * SQ], mask16_one)
            grad_p = dot_nt(kv[t * CR : (t + 1) * CR, D:], wide)
            gvs.append(dot(p_low[t * CR : (t + 1) * CR], wide))
            pt = p[t * CR : (t + 1) * CR]
            gss.append(pt * (grad_p - jnp.sum(grad_p * pt, 0, keepdims=True)))
        gs = jnp.concatenate(gss, 0).astype(BF16)
        grad_q = contract(dot_tn(gs, kv[:, :D]), SQ) * 0.25
        gk = dot(gs, expand(w_ref[e, R_Q:R_PIN, :], mask16))
        gkv = jnp.concatenate([gk, jnp.concatenate(gvs, 0)], 1).astype(BF16)
        grad_wkv = dot_tn(kept["ctx"][j], gkv)
        grad_ctx = dot_nt(gkv, stem_kv_weight(w_ref, e)).astype(BF16)
        grad_contexts.append(grad_ctx)
        wide_ctx = grad_ctx.astype(F32)
        prow = jnp.where(
            row16 == 0,
            wide_ctx[FR : FR + 1],
            jnp.where(row16 == 1, wide_ctx[CR + FR : CR + FR + 1], 0.0),
        )
        prow_low = prow.astype(BF16)
        pact = kept["pact"][j * PR : (j + 1) * PR]
        grad_wp = dot_tn(pact, prow_low)
        gpact = dot_nt(prow_low, w_ref[e, 3 * D : 4 * D, :])
        gppre = (gpact * kept["pslope"][j * PR : (j + 1) * PR]).astype(BF16)
        grad_pin = dot_tn(prop_ref[j].astype(BF16), gppre)
        grad_props.append(dot_nt(gppre, w_ref[e, R_PIN:R_ATT, :]))
        stem = acc["stem"]
        stem[e, 0:D, :] += grad_wkv[:, :D]
        stem[e, D : 2 * D, :] += grad_wkv[:, D:]
        stem[e, 2 * D : 3 * D, :] += grad_wo
        stem[e, 3 * D : 4 * D, :] += grad_wp
        stem[e, R_Q:R_PIN, :] += grad_q
        stem[e, R_PIN:R_ATT, :] += grad_pin
        acc["sb"][0, pl.ds(e, 1), :] += jnp.sum(gppre.astype(F32), 0, keepdims=True)
        acc["sb"][1, pl.ds(e, 1), :] += jnp.sum(prow, 0, keepdims=True)
    return grad_first, grad_contexts, grad_props


ACC = ("stem", "sb", "wqkv", "wout", "up", "down", "vec", "mb")


def acc_shapes():
    return [
        pltpu.VMEM((STEMS, STEM_ROWS, D), F32),
        pltpu.VMEM((2, STEMS, D), F32),
        pltpu.VMEM((D, 3 * D), F32),
        pltpu.VMEM((D, D), F32),
        pltpu.VMEM((D, FF), F32),
        pltpu.VMEM((D, FF), F32),
        pltpu.VMEM((8, 8, D), F32),
        pltpu.VMEM((8, FF), F32),
    ]


def clear(acc):
    for ref in acc.values():
        ref[...] = jnp.zeros(ref.shape, ref.dtype)


def finish(acc, grad_ref, small_ref):
    def stem_out(e, carry):
        grad_ref[e, 0:STEM_ROWS, :] = acc["stem"][e].astype(grad_ref.dtype)
        return carry

    lax.fori_loop(0, STEMS, stem_out, 0)
    wqkv = acc["wqkv"][...]
    attn = [wqkv[:, :D], wqkv[:, D : 2 * D], wqkv[:, 2 * D :], acc["wout"][...]]
    for block in range(4):
        grad_ref[block * 8 : block * 8 + 8, R_ATT:R_UP, :] = (
            attn[block].astype(grad_ref.dtype).reshape(8, 16, D)
        )
    grad_ref[:, R_UP:R_DOWN, :] = acc["up"][...].T.astype(grad_ref.dtype).reshape(STEMS, 16, D)
    grad_ref[:, R_DOWN:ROWS, :] = acc["down"][...].T.astype(grad_ref.dtype).reshape(STEMS, 16, D)
    small_ref[0:8, :] = jnp.sum(acc["vec"][...], 1)
    mb = jnp.sum(acc["mb"][...], 0, keepdims=True)
    small_ref[8:16, :] = jnp.concatenate(
        [mb[:, i * D : (i + 1) * D] for i in range(4)] + [jnp.zeros((4, D), F32)], 0
    )
    for i in range(2):
        small_ref[16 + i * STEMS : 16 + (i + 1) * STEMS, :] = acc["sb"][i]


SAVED = ("ctx", "kv", "prob", "mix", "first", "qkv", "sprob", "smix", "second", "act", "slope", "pact", "pslope")
PER_SAMPLE = ("ctx", "kv", "prob", "sprob")


def saved_shapes(samples):
    rows = samples * TOK
    return dict(
        ctx=((samples, STEPS * CR, D), BF16),
        kv=((samples, STEPS * CR, 2 * D), BF16),
        prob=((samples, STEPS * CR, D), BF16),
        mix=((rows, D), BF16),
        first=((rows, D), F32),
        qkv=((rows, 3 * D), BF16),
        sprob=((samples, TOK, HEADS * TOK), BF16),
        smix=((rows, D), BF16),
        second=((rows, D), F32),
        act=((rows, FF), BF16),
        slope=((rows, FF), BF16),
        pact=((samples * PR, D), BF16),
        pslope=((samples * PR, D), F32),
    )


def forward_kernel(emb_ref, tok_ref, feat_ref, prop_ref, w_ref, vec_ref, mb_ref, sb_ref, out_ref, *saved):
    step = pl.program_id(0)
    es = [emb_ref[step * SB + j] for j in range(SB)]
    out, kept = forward_block(
        es, tok_ref[...].astype(F32), feat_ref, prop_ref, w_ref, vec_ref[...], mb_ref[...], sb_ref
    )
    out_ref[...] = out
    for name, ref in zip(SAVED, saved):
        if name in PER_SAMPLE:
            for j in range(SB):
                ref[j] = kept[name][j].astype(ref.dtype)
        else:
            ref[...] = kept[name].astype(ref.dtype)


def middle_kernel(
    emb_ref, hid_ref, feat_ref, prop_ref, w_ref, vec_ref, mb_ref, sb_ref, cot_ref,
    out_ref, ghid_ref, gfeat_ref, gprop_ref, gw_ref, gsmall_ref, *accs
):
    step = pl.program_id(0)
    acc = dict(zip(ACC, accs))
    pl.when(step == 0)(lambda: clear(acc))
    es = [emb_ref[step * SB + j] for j in range(SB)]
    vec = vec_ref[...]
    out, kept = forward_block(es, hid_ref[...], feat_ref, prop_ref, w_ref, vec, mb_ref[...], sb_ref)
    out_ref[...] = out.astype(BF16)
    ghid, gctx, gprop = backward_block(
        es, cot_ref[...].astype(F32), kept, prop_ref, w_ref, vec, acc
    )
    ghid_ref[...] = ghid
    for j in range(SB):
        gfeat_ref[j] = gctx[j]
        gprop_ref[j] = gprop[j]
    pl.when(step == pl.num_programs(0) - 1)(lambda: finish(acc, gw_ref, gsmall_ref))


def backward_kernel(emb_ref, grad_ref, prop_ref, w_ref, vec_ref, gfeat1_ref, gprop1_ref, *rest):
    saved = rest[: len(SAVED)]
    gtok_ref, gfeat_ref, gprop_ref, gw_ref, gsmall_ref = rest[len(SAVED) : len(SAVED) + 5]
    acc = dict(zip(ACC, rest[len(SAVED) + 5 :]))
    step = pl.program_id(0)
    pl.when(step == 0)(lambda: clear(acc))
    es = [emb_ref[step * SB + j] for j in range(SB)]
    kept = {name: ref if name in PER_SAMPLE else ref[...] for name, ref in zip(SAVED, saved)}
    ghid, gctx, gprop = backward_block(es, grad_ref[...], kept, prop_ref, w_ref, vec_ref[...], acc)
    gtok_ref[...] = ghid
    for j in range(SB):
        total = gctx[j].astype(F32) + gfeat1_ref[j].astype(F32)
        for t in range(STEPS):
            gfeat_ref[j, t] = total[t * CR : t * CR + FR]
        gprop_ref[j] = (gprop[j] + gprop1_ref[j])[:STEPS]
    pl.when(step == pl.num_programs(0) - 1)(lambda: finish(acc, gw_ref, gsmall_ref))


def blocked(shape, per_step):
    block = (per_step,) + tuple(shape[1:])
    zeros = (0,) * (len(shape) - 1)
    return pl.BlockSpec(block, lambda i, *_: (i,) + zeros)


def whole(shape):
    zeros = (0,) * len(shape)
    return pl.BlockSpec(tuple(shape), lambda i, *_: zeros, pipeline_mode=pl.Buffered(1))


def call(kernel, steps, emb, ins, outs, scratch):
    return pl.pallas_call(
        kernel,
        grid_spec=pltpu.PrefetchScalarGridSpec(
            num_scalar_prefetch=1,
            grid=(steps,),
            in_specs=[blocked(a.shape, n) if n else whole(a.shape) for a, n in ins],
            out_specs=[blocked(s, n) if n else whole(s) for s, _, n in outs],
            scratch_shapes=scratch,
        ),
        out_shape=[jax.ShapeDtypeStruct(s, d) for s, d, _ in outs],
        compiler_params=pltpu.CompilerParams(
            dimension_semantics=("arbitrary",), vmem_limit_bytes=VMEM_LIMIT
        ),
    )(emb, *[a for a, _ in ins])


def compute(tokens, features, proprio, emb, w0, w1, vecs, mbs, sbs, cot, wire):
    samples = emb.shape[0]
    steps = samples // SB
    rows = samples * TOK
    rb = SB * TOK
    tok = tokens.reshape(rows, D)
    prop = jnp.pad(proprio.astype(F32), ((0, 0), (0, PR - STEPS), (0, 0)))
    shapes = saved_shapes(samples)
    per = lambda s: s[0] // steps
    saved_outs = [(shapes[n][0], shapes[n][1], per(shapes[n][0])) for n in SAVED]
    res = call(
        forward_kernel, steps, emb,
        [(tok, rb), (features, SB), (prop, SB), (w0, 0), (vecs[0], 0), (mbs[0], 0), (sbs[0], 0)],
        [((rows, D), F32, rb)] + saved_outs, [],
    )
    hidden, saved = res[0], res[1:]
    grad_outs = [((STEMS, ROWS, D), wire, 0), ((SMALL, D), F32, 0)]
    out, ghid, gfeat1, gprop1, *grads1 = call(
        middle_kernel, steps, emb,
        [(hidden, rb), (features, SB), (prop, SB), (w1, 0), (vecs[1], 0), (mbs[1], 0), (sbs[1], 0),
         (cot.reshape(rows, D), rb)],
        [((rows, D), BF16, rb), ((rows, D), F32, rb), ((samples, STEPS * CR, D), BF16, SB),
         ((samples, PR, PROP), F32, SB)] + grad_outs,
        acc_shapes(),
    )
    gtok, gfeat, gprop, *grads0 = call(
        backward_kernel, steps, emb,
        [(ghid, rb), (prop, SB), (w0, 0), (vecs[0], 0), (gfeat1, SB), (gprop1, SB)]
        + [(a, per(a.shape)) for a in saved],
        [((rows, D), F32, rb), ((samples, STEPS, FR, D), F32, SB), ((samples, STEPS, PROP), F32, SB)]
        + grad_outs,
        acc_shapes(),
    )
    return (
        out.reshape(tokens.shape), gtok.reshape(tokens.shape), gfeat, gprop, grads0, grads1
    )


STREAMS = (
    (0, 256, ("z", "x", "y")),
    (256, 256, ("z", "y", "x")),
    (512, 48, ("x", "y", "z")),
    (560, 48, ("y", "x", "z")),
)
SIZES = {"z": 4, "y": 2, "x": 2, "c": 2}
AXES = ("z", "y", "x", "c")
MESH = pl.DeviceIdType.MESH


def place():
    me = lax.axis_index("fsdp")
    return {"z": me // 8, "y": (me // 4) % 2, "x": (me // 2) % 2, "c": me % 2}


def number(at):
    return ((at["z"] * 2 + at["y"]) * 2 + at["x"]) * 2 + at["c"]


def moved(at, axis, by):
    out = dict(at)
    out[axis] = (at[axis] + by) % SIZES[axis]
    return out


def greet(at):
    barrier = pltpu.get_barrier_semaphore()
    count = 0
    for axis in AXES:
        for by in range(1, SIZES[axis]):
            pl.semaphore_signal(
                barrier, inc=1, device_id=(number(moved(at, axis, by)),), device_id_type=MESH
            )
            count += 1
    pl.semaphore_wait(barrier, count)


def block(ref, at, done, row, count):
    index = tuple(pl.ds(0, SIZES[a]) if a in done else pl.ds(at[a], 1) for a in AXES)
    return ref.at[index + (pl.ds(row, count), slice(None))]


def gather_kernel(att, up, down, stem, q, pin, g0, g1, local_sem, send_sem, recv_sem):
    at = place()
    outs = (g0, g1)
    locals_ = []
    for layer in range(LAYERS):
        slot = outs[layer].at[at["z"], at["y"], at["x"], at["c"]]
        pieces = [
            (stem.at[layer, :, pl.ds(j * D, D)], j * D, D) for j in range(4)
        ] + [
            (q.at[layer], R_Q, SQ), (pin.at[layer], R_PIN, PROP), (att.at[layer], R_ATT, 16),
            (up.at[layer], R_UP, 16), (down.at[layer], R_DOWN, 16),
        ]
        for i, (piece, row, count) in enumerate(pieces):
            copy = pltpu.make_async_copy(piece, slot.at[pl.ds(row, count), :], local_sem.at[layer, i])
            copy.start()
            locals_.append(copy)
    greet(at)
    for copy in locals_:
        copy.wait()
    chains = [(layer, s) for layer in range(LAYERS) for s in range(len(STREAMS))]
    pending = {}
    sent = []
    for phase in range(4):
        for chain in chains:
            layer, s = chain
            row, count, order = STREAMS[s]
            order = order + ("c",)
            for copy in pending.pop(chain, ()):
                copy.wait_recv()
            axis, done = order[phase], order[:phase]
            got = []
            for by in range(1, SIZES[axis]):
                to = moved(at, axis, by)
                sem = (layer * 4 + s, AXES.index(axis), by - 1)
                mine = block(outs[layer], at, done, row, count)
                copy = pltpu.make_async_remote_copy(
                    mine, mine, send_sem.at[sem], recv_sem.at[sem],
                    device_id=(number(to),), device_id_type=MESH,
                )
                copy.start()
                sent.append(copy)
                theirs = block(outs[layer], moved(at, axis, -by), done, row, count)
                got.append(
                    pltpu.make_async_remote_copy(
                        theirs, theirs, send_sem.at[sem], recv_sem.at[sem],
                        device_id=(number(to),), device_id_type=MESH,
                    )
                )
            pending[chain] = got
    for chain in chains:
        for copy in pending.pop(chain):
            copy.wait_recv()
    for copy in sent:
        copy.wait_send()


def gather(att, up, down, stem, q, pin):
    shape = jax.ShapeDtypeStruct((4, 2, 2, 2, ROWS, D), BF16)
    any_spec = pl.BlockSpec(memory_space=pl.ANY)
    return pl.pallas_call(
        gather_kernel,
        out_shape=[shape, shape],
        in_specs=[any_spec] * 6,
        out_specs=[any_spec] * 2,
        scratch_shapes=[
            pltpu.SemaphoreType.DMA((LAYERS, 9)),
            pltpu.SemaphoreType.DMA((8, 4, 3)),
            pltpu.SemaphoreType.DMA((8, 4, 3)),
        ],
        compiler_params=pltpu.CompilerParams(collective_id=0, has_side_effects=True),
    )(att, up, down, stem, q, pin)


def scatter_kernel(
    g0, g1, s0, s1, att, up, down, stem, q, pin, small,
    acc0, acc1, rc0, rc1, rx0, rx1, ry0, ry1, rz0, rz1, sm, smr, smz,
    send_sem, recv_sem, ssend, srecv,
):
    at = place()
    grads = (g0, g1)
    accs = (acc0, acc1)
    lands = {"c": (rc0, rc1), "x": (rx0, rx1), "y": (ry0, ry1), "z": (rz0, rz1)}
    greet(at)
    chains = [(layer, s) for layer in (1, 0) for s in range(len(STREAMS))]
    sent = []

    def start(chain, phase):
        layer, s = chain
        row, count, order = STREAMS[s]
        order = ("c",) + order[::-1]
        axis = order[phase]
        left = [a for a in AXES if a not in order[: phase + 1]]
        source = grads[layer] if phase == 0 else accs[layer]
        got = []
        for by in range(1, SIZES[axis]):
            to = moved(at, axis, by)
            index = []
            for a in AXES:
                if a == "c" and phase > 0:
                    continue
                if a == axis:
                    index.append(to[a])
                else:
                    index.append(pl.ds(0, SIZES[a]) if a in left else at[a])
            src = source.at[tuple(index) + (pl.ds(row, count), slice(None))]
            index = [] if axis != "z" else [by - 1]
            for a in AXES:
                if a != axis and a != "c":
                    index.append(pl.ds(0, SIZES[a]) if a in left else 0)
            dst = lands[axis][layer].at[tuple(index) + (pl.ds(row, count), slice(None))]
            sem = (layer * 4 + s, AXES.index(axis), by - 1)
            copy = pltpu.make_async_remote_copy(
                src, dst, send_sem.at[sem], recv_sem.at[sem],
                device_id=(number(to),), device_id_type=MESH,
            )
            copy.start()
            sent.append(copy)
            got.append(copy)
        return got

    def add(chain, phase):
        layer, s = chain
        row, count, order = STREAMS[s]
        order = ("c",) + order[::-1]
        axis = order[phase]
        left = [a for a in AXES if a not in order[: phase + 1]]
        source = grads[layer] if phase == 0 else accs[layer]
        acc, land = accs[layer], lands[axis][layer]
        rows = pl.ds(row, count)
        total = 1
        for a in left:
            total *= SIZES[a]

        def one(i, carry):
            spot = dict(at)
            lspot = {"z": 0, "y": 0, "x": 0}
            rest = i
            for a in left[::-1]:
                spot[a] = rest % SIZES[a]
                lspot[a] = spot[a]
                rest = rest // SIZES[a]
            keep = (spot["z"], spot["y"], spot["x"])
            mine = source[keep + ((at["c"],) if phase == 0 else ()) + (rows, slice(None))]
            value = mine.astype(F32)
            for by in range(1, SIZES[axis]):
                index = () if axis != "z" else (by - 1,)
                index += tuple(lspot[a] for a in AXES if a != axis and a != "c")
                value = value + land[index + (rows, slice(None))].astype(F32)
            if phase < 3:
                acc[keep + (rows, slice(None))] = value.astype(BF16)
            else:
                finish_rows(layer, s, value)
            return carry

        if total == 1:
            one(0, 0)
        else:
            lax.fori_loop(0, total, one, 0)

    def finish_rows(layer, s, value):
        if s < 2:
            for j in range(2):
                col = (2 * s + j) * D
                stem[layer, :, col : col + D] = value[j * D : (j + 1) * D]
        elif s == 2:
            q[layer] = value[:SQ]
            pin[layer] = value[SQ:]
        else:
            att[layer] = value[0:16]
            up[layer] = value[16:32]
            down[layer] = value[32:48]

    smalls = ("c", "x", "y", "z")

    def small_start(phase):
        axis = smalls[phase]
        for by in range(1, SIZES[axis]):
            to = moved(at, axis, by)
            dst = smr.at[phase] if axis != "z" else smz.at[at["z"]]
            sem = (phase, by - 1)
            copy = pltpu.make_async_remote_copy(
                sm.at[phase], dst, ssend.at[sem], srecv.at[sem],
                device_id=(number(to),), device_id_type=MESH,
            )
            copy.start()
            sent.append(copy)

    def small_land(phase):
        axis = smalls[phase]
        for by in range(1, SIZES[axis]):
            src = moved(at, axis, -by)
            dst = smr.at[phase] if axis != "z" else smz.at[src["z"]]
            sem = (phase, by - 1)
            pltpu.make_async_remote_copy(
                sm.at[phase], dst, ssend.at[sem], srecv.at[sem],
                device_id=(number(moved(at, axis, by)),), device_id_type=MESH,
            ).wait_recv()
        if axis != "z":
            sm[phase + 1] = sm[phase] + smr[phase]
        else:
            smz[at["z"]] = sm[phase]
            small[...] = (smz[0] + smz[1]) + (smz[2] + smz[3])

    pending = {chain: start(chain, 0) for chain in chains}
    sm[0, 0] = s0[...]
    sm[0, 1] = s1[...]
    small_start(0)
    for phase in range(4):
        for chain in chains:
            for copy in pending.pop(chain):
                copy.wait_recv()
            add(chain, phase)
            if phase < 3:
                pending[chain] = start(chain, phase + 1)
        small_land(phase)
        if phase < 3:
            small_start(phase + 1)
    for copy in sent:
        copy.wait_send()


def scatter(g0, g1, s0, s1):
    def out(*shape):
        return jax.ShapeDtypeStruct(shape, F32)

    vmem = pl.BlockSpec(memory_space=pltpu.VMEM)
    lead = (4, 2, 2, 2, ROWS, D)
    scratch = []
    for shape in ((4, 2, 2), (4, 2, 2), (4, 2), (4, 2), (3, 2, 2)):
        scratch += [pltpu.VMEM(shape + (ROWS, D), BF16)] * 2
    return pl.pallas_call(
        scatter_kernel,
        out_shape=[
            out(LAYERS, 16, D), out(LAYERS, 16, D), out(LAYERS, 16, D), out(LAYERS, D, 4 * D),
            out(LAYERS, SQ, D), out(LAYERS, PROP, D), out(LAYERS, SMALL, D),
        ],
        in_specs=[vmem] * 4,
        out_specs=[vmem] * 7,
        scratch_shapes=scratch
        + [
            pltpu.VMEM((4, LAYERS, SMALL, D), F32),
            pltpu.VMEM((3, LAYERS, SMALL, D), F32),
            pltpu.VMEM((4, LAYERS, SMALL, D), F32),
            pltpu.SemaphoreType.DMA((8, 4, 3)),
            pltpu.SemaphoreType.DMA((8, 4, 3)),
            pltpu.SemaphoreType.DMA((4, 3)),
            pltpu.SemaphoreType.DMA((4, 3)),
        ],
        compiler_params=pltpu.CompilerParams(
            collective_id=1, has_side_effects=True, vmem_limit_bytes=VMEM_LIMIT
        ),
    )(g0.reshape(lead), g1.reshape(lead), s0, s1)


def pack(attn, up, down, stem, queries, pin):
    gathered = [lax.all_gather(a, "fsdp", axis=1, tiled=True) for a in (attn, up, down, stem, queries, pin)]
    attn, up, down, stem, queries, pin = gathered
    stem = stem.reshape(LAYERS, STEMS, D, 4, D).transpose(0, 1, 3, 2, 4).reshape(LAYERS, STEMS, 4 * D, D)
    parts = [stem] + [a.reshape(LAYERS, STEMS, -1, D) for a in (queries, pin, attn, up, down)]
    return jnp.concatenate(parts, 2)


def unpack_blocks(grad):
    lead = grad.shape[:-2]
    stem = grad[..., : 4 * D, :].reshape(lead + (4, D, D))
    stem = jnp.swapaxes(stem, -3, -2).reshape(lead + (D, 4 * D))
    return (
        grad[..., R_ATT:R_UP, :], grad[..., R_UP:R_DOWN, :], grad[..., R_DOWN:ROWS, :],
        stem, grad[..., R_Q:R_PIN, :], grad[..., R_PIN:R_ATT, :],
    )


def body(n, tokens, features, proprio, embodiment, trunk_attn, feedforward_up_weight, mlp_down,
         stem_mats, stem_queries, prop_in, trunk_vectors, mlp_bias, stem_bias, cotangent):
    shards = (trunk_attn, feedforward_up_weight, mlp_down, stem_mats, stem_queries, prop_in)
    vecs = trunk_vectors.astype(F32)
    mbs = mlp_bias.astype(F32).reshape(LAYERS, 1, FF)
    sbs = stem_bias.astype(F32)
    if n == 32:
        w0, w1 = (w.reshape(STEMS, ROWS, D) for w in gather(*shards))
    else:
        w0, w1 = pack(*shards)
    out, gtok, gfeat, gprop, g0, g1 = compute(
        tokens, features, proprio, embodiment, w0, w1, vecs, mbs, sbs, cotangent, BF16
    )
    if n == 32:
        *mats, small = scatter(g0[0], g1[0], g0[1], g1[1])
    else:
        mats = [
            lax.psum_scatter(a.reshape(LAYERS, -1, a.shape[-1]), "fsdp", scatter_dimension=1, tiled=True)
            for a in unpack_blocks(jnp.stack([g0[0], g1[0]]).astype(F32))
        ]
        small = lax.psum(jnp.stack([g0[1], g1[1]]), "fsdp")
    gvec = small[:, :8]
    gmb = small[:, 8:12].reshape(LAYERS, FF)
    gsb = jnp.swapaxes(small[:, 16:].reshape(LAYERS, 2, STEMS, D), 1, 2)
    return (out, gtok, gfeat, gprop, *mats, gvec, gmb, gsb)


def solution(mesh):
    n = mesh.shape["fsdp"]
    return jax.shard_map(
        functools.partial(body, n),
        mesh=mesh,
        in_specs=(
            P("fsdp"), P("fsdp"), P("fsdp"), P("fsdp"),
            P(None, "fsdp"), P(None, "fsdp"), P(None, "fsdp"), P(None, "fsdp"), P(None, "fsdp"),
            P(None, "fsdp"), P(), P(), P(), P("fsdp"),
        ),
        out_specs=(
            P("fsdp"), P("fsdp"), P("fsdp"), P("fsdp"),
            P(None, "fsdp"), P(None, "fsdp"), P(None, "fsdp"), P(None, "fsdp"), P(None, "fsdp"),
            P(None, "fsdp"), P(), P(), P(),
        ),
        check_vma=False,
    )
```

```python
import functools
import math

import jax
import jax.numpy as jnp
from jax import lax
from jax.experimental import pallas as pl
from jax.experimental.pallas import tpu as pltpu
from jax.sharding import PartitionSpec as P

D = 128
HEADS = 8
HD = 16
FF = 512
SQ = 16
FR = 49
CR = 112
PROP = 32
PR = 16
STEMS = 32
STEPS = 2
LAYERS = 2
TOK = 32
SB = 16

R_Q = 4 * D
R_PIN = R_Q + SQ
R_ATT = R_PIN + PROP
R_UP = R_ATT + 16
R_DOWN = R_UP + 16
ROWS = R_DOWN + 16
STEM_ROWS = R_ATT
SMALL = 16 + 2 * STEMS

F32 = jnp.float32
BF16 = jnp.bfloat16
VMEM_LIMIT = 60 * 1024 * 1024


def dot(a, b):
    return lax.dot_general(a, b, (((1,), (0,)), ((), ())), preferred_element_type=F32)


def dot_nt(a, b):
    return lax.dot_general(a, b, (((1,), (1,)), ((), ())), preferred_element_type=F32)


def dot_tn(a, b):
    return lax.dot_general(a, b, (((0,), (0,)), ((), ())), preferred_element_type=F32)


def gelu_parts(x):
    cdf = 0.5 + 0.5 * lax.erf(x * math.sqrt(0.5))
    slope = cdf + x * (jnp.exp(-0.5 * x * x) * (1.0 / math.sqrt(2.0 * math.pi)))
    return x * cdf, slope


def norm_parts(x):
    centred = x - jnp.mean(x, -1, keepdims=True)
    inverse = lax.rsqrt(jnp.mean(centred * centred, -1, keepdims=True) + 1e-05)
    return centred * inverse, inverse


def norm_back(grad, gain, hat, inverse):
    g = grad * gain
    return inverse * (
        g - jnp.mean(g, -1, keepdims=True) - hat * jnp.mean(g * hat, -1, keepdims=True)
    )


def head_mask(rows, value):
    row = lax.broadcasted_iota(jnp.int32, (HEADS * rows, D), 0) // rows
    lane = lax.broadcasted_iota(jnp.int32, (HEADS * rows, D), 1) // HD
    return jnp.where(row == lane, value, 0.0).astype(BF16)


def expand(rows, mask):
    return jnp.concatenate([rows] * HEADS, 0) * mask


def contract(wide, rows):
    lane = lax.broadcasted_iota(jnp.int32, (rows, D), 1) // HD
    out = wide[:rows]
    for head in range(1, HEADS):
        out = jnp.where(lane == head, wide[head * rows : (head + 1) * rows], out)
    return out


def fold(x):
    return jnp.sum(x.reshape(x.shape[0] // 8, 8, x.shape[1]), 0)


def slot(w_ref, e, start, stop):
    if len(w_ref.shape) == 3:
        return w_ref[e, start:stop, :]
    return w_ref[e // 8, (e // 4) % 2, (e // 2) % 2, e % 2, start:stop, :]


def all_slots(w_ref, start, stop):
    index = (slice(None),) * (len(w_ref.shape) - 2)
    return w_ref[index + (slice(start, stop), slice(None))].reshape(STEMS * (stop - start), D)


def trunk_weights(w_ref):
    attn = all_slots(w_ref, R_ATT, R_UP)
    up = all_slots(w_ref, R_UP, R_DOWN)
    down = all_slots(w_ref, R_DOWN, ROWS)
    wqkv = jnp.concatenate([attn[:D], attn[D : 2 * D], attn[2 * D : 3 * D]], 1)
    return wqkv, attn[3 * D :], up, down


def stem_kv_weight(w_ref, e):
    return jnp.concatenate([slot(w_ref, e, 0, D), slot(w_ref, e, D, 2 * D)], 1)


def step_reduce(x, op):
    x = x.reshape(x.shape[0] // 8, 8, x.shape[1])
    out = x[0]
    for i in range(1, x.shape[0]):
        out = op(out, x[i])
    out = op(out, pltpu.roll(out, 4, 0))
    return op(out, pltpu.roll(out, 2, 0))


def step_apply(x, y, op):
    return op(x.reshape(x.shape[0] // 8, 8, x.shape[1]), y[None]).reshape(x.shape)


def step_masks():
    odd = lax.broadcasted_iota(jnp.int32, (CR, D), 0) % 2
    return (odd == 0).astype(BF16), odd.astype(BF16)


def split_steps(p, masks):
    return jnp.concatenate([p * masks[0], p * masks[1]], 1)


def softmax_rows(score):
    top = jnp.max(score, 0, keepdims=True)
    weight = jnp.exp(score - top)
    return weight * (1.0 / jnp.sum(weight, 0, keepdims=True))


def forward_block(es, hidden, feat_ref, props, w_ref, vec, mb, sb):
    kept = {}
    pre = [
        dot(props[j * PR : (j + 1) * PR], slot(w_ref, e, R_PIN, R_ATT))
        + sb(e)[0:1, :]
        for j, e in enumerate(es)
    ]
    pact, pslope = gelu_parts(jnp.concatenate(pre, 0))
    pact = pact.astype(BF16)
    kept["pact"], kept["pslope"] = pact, pslope
    row16 = lax.broadcasted_iota(jnp.int32, (PR, D), 0)
    prows = [
        dot(pact[j * PR : (j + 1) * PR], slot(w_ref, e, 3 * D, 4 * D)) + sb(e)[1:2, :]
        for j, e in enumerate(es)
    ]
    contexts = []
    for j in range(SB):
        rows = feat_ref[j * STEPS * FR : (j + 1) * STEPS * FR, :]
        last = jnp.concatenate([rows[96:98], jnp.zeros((14, D), BF16)], 0).astype(F32)
        tail = jnp.where(row16 < 2, last, jnp.where(row16 < 4, prows[j], 0.0))
        contexts.append(jnp.concatenate([rows[:96], tail.astype(BF16)], 0))
    kept["ctx"] = contexts
    kvs = [dot(contexts[j], stem_kv_weight(w_ref, e)).astype(BF16) for j, e in enumerate(es)]
    kept["kv"] = kvs
    mask16 = head_mask(SQ, 0.25)
    scores = [
        dot_nt(kvs[j][:, :D], expand(slot(w_ref, e, R_Q, R_PIN), mask16)) for j, e in enumerate(es)
    ]
    valid = lax.broadcasted_iota(jnp.int32, (104, D), 0) < STEPS * (FR + 1)
    pad = jnp.zeros((8, D), F32)
    probs = []
    for j in range(SB):
        s = jnp.where(valid, scores[j][:104], -1e30)
        weight = jnp.exp(step_apply(s, step_reduce(s, jnp.maximum), jnp.subtract))
        scale = 1.0 / step_reduce(weight, jnp.add)
        probs.append(jnp.concatenate([step_apply(weight, scale, jnp.multiply), pad], 0))
    kept["prob"] = probs
    masks = step_masks()
    mixes = []
    for j in range(SB):
        wide = dot_tn(split_steps(probs[j].astype(BF16), masks), kvs[j][:, D:])
        mixes += [contract(wide[t * D : (t + 1) * D], SQ).astype(BF16) for t in range(STEPS)]
    mix = jnp.concatenate(mixes, 0)
    kept["mix"] = mix
    outs = [
        dot(mix[j * TOK : (j + 1) * TOK], slot(w_ref, e, 2 * D, 3 * D)) for j, e in enumerate(es)
    ]
    first = hidden + jnp.concatenate(outs, 0)
    kept["first"] = first
    wqkv, wout, up, down = trunk_weights(w_ref)
    normed = (norm_parts(first)[0] * vec[0:1] + vec[1:2]).astype(BF16)
    bias = jnp.concatenate([vec[2:3], jnp.zeros((1, D), F32), vec[3:4]], 1)
    qkv = (dot(normed, wqkv) + bias).astype(BF16)
    kept["qkv"] = qkv
    mask32 = head_mask(TOK, 0.25)
    rows = [qkv[j * TOK : (j + 1) * TOK] for j in range(SB)]
    scores = [dot_nt(rows[j][:, D : 2 * D], expand(rows[j][:, :D], mask32)) for j in range(SB)]
    sprobs = [softmax_rows(s) for s in scores]
    smixes = [
        contract(dot_tn(sprobs[j].astype(BF16), rows[j][:, 2 * D :]), TOK).astype(BF16)
        for j in range(SB)
    ]
    kept["sprob"] = sprobs
    smix = jnp.concatenate(smixes, 0)
    kept["smix"] = smix
    second = first + (dot(smix, wout) + vec[4:5])
    kept["second"] = second
    mlp_in = (norm_parts(second)[0] * vec[5:6] + vec[6:7]).astype(BF16)
    act, slope = gelu_parts(dot_nt(mlp_in, up) + mb)
    act = act.astype(BF16)
    kept["act"], kept["slope"] = act, slope
    return second + (dot(act, down) + vec[7:8]), kept


def backward_block(es, grad, kept, props, w_ref, vec, acc):
    wqkv, wout, up, down = trunk_weights(w_ref)
    out_low = grad.astype(BF16)
    acc["vec"][7] += fold(out_low.astype(F32))
    acc["down"][...] += dot_tn(out_low, kept["act"])
    grad_act = dot_nt(out_low, down)
    grad_pre = (grad_act * kept["slope"].astype(F32)).astype(BF16)
    acc["mb"][...] += fold(grad_pre.astype(F32))
    hat, inverse = norm_parts(kept["second"])
    mlp_in = (hat * vec[5:6] + vec[6:7]).astype(BF16)
    acc["up"][...] += dot_tn(mlp_in, grad_pre)
    grad_in = dot(grad_pre, up)
    acc["vec"][5] += fold(grad_in * hat)
    acc["vec"][6] += fold(grad_in)
    grad_second = grad + norm_back(grad_in, vec[5:6], hat, inverse)
    branch = grad_second.astype(BF16)
    acc["vec"][4] += fold(branch.astype(F32))
    acc["wout"][...] += dot_tn(kept["smix"], branch)
    grad_mix = dot_nt(branch, wout).astype(BF16)
    mask32 = head_mask(TOK, 0.25)
    mask32_one = head_mask(TOK, 1.0)
    rows = [kept["qkv"][j * TOK : (j + 1) * TOK] for j in range(SB)]
    wides = [expand(grad_mix[j * TOK : (j + 1) * TOK], mask32_one) for j in range(SB)]
    grad_ps = [dot_nt(rows[j][:, 2 * D :], wides[j]) for j in range(SB)]
    grads_v = [dot(kept["sprob"][j].astype(BF16), wides[j]) for j in range(SB)]
    gss = []
    for j in range(SB):
        p = kept["sprob"][j].astype(F32)
        gss.append((p * (grad_ps[j] - jnp.sum(grad_ps[j] * p, 0, keepdims=True))).astype(BF16))
    grads_q = [contract(dot_tn(gss[j], rows[j][:, D : 2 * D]), TOK) * 0.25 for j in range(SB)]
    grads_k = [dot(gss[j], expand(rows[j][:, :D], mask32)) for j in range(SB)]
    grad_qkv = jnp.concatenate(
        [jnp.concatenate(g, 0).astype(BF16) for g in (grads_q, grads_k, grads_v)], 1
    )
    acc["vec"][2] += fold(grad_qkv[:, :D].astype(F32))
    acc["vec"][3] += fold(grad_qkv[:, 2 * D :].astype(F32))
    hat, inverse = norm_parts(kept["first"])
    normed = (hat * vec[0:1] + vec[1:2]).astype(BF16)
    acc["wqkv"][...] += dot_tn(normed, grad_qkv)
    grad_normed = dot_nt(grad_qkv, wqkv)
    acc["vec"][0] += fold(grad_normed * hat)
    acc["vec"][1] += fold(grad_normed)
    grad_first = grad_second + norm_back(grad_normed, vec[0:1], hat, inverse)
    stem_grad = grad_first.astype(BF16)
    mask16 = head_mask(SQ, 0.25)
    mask16_one = head_mask(SQ, 1.0)
    row16 = lax.broadcasted_iota(jnp.int32, (PR, D), 0)
    gs_in = [stem_grad[j * TOK : (j + 1) * TOK] for j in range(SB)]
    gmixes = [dot_nt(gs_in[j], slot(w_ref, e, 2 * D, 3 * D)).astype(BF16) for j, e in enumerate(es)]
    grad_wo = [dot_tn(kept["mix"][j * TOK : (j + 1) * TOK], gs_in[j]) for j in range(SB)]
    kvs = [kept["kv"][j] for j in range(SB)]
    probs = [kept["prob"][j] for j in range(SB)]
    wides = [
        jnp.concatenate(
            [expand(gmixes[j][t * SQ : (t + 1) * SQ], mask16_one) for t in range(STEPS)], 0
        )
        for j in range(SB)
    ]
    grad_ps = [dot_nt(kvs[j][:, D:], wides[j]) for j in range(SB)]
    masks = step_masks()
    gvs = [dot(split_steps(probs[j].astype(BF16), masks), wides[j]) for j in range(SB)]
    even = lax.broadcasted_iota(jnp.int32, (104, D), 0) % 2 == 0
    pad = jnp.zeros((8, D), F32)
    gss = []
    for j in range(SB):
        p = probs[j][:104].astype(F32)
        gp = jnp.where(even, grad_ps[j][:104, :D], grad_ps[j][:104, D:])
        gs = p * step_apply(gp, step_reduce(gp * p, jnp.add), jnp.subtract)
        gss.append(jnp.concatenate([gs, pad], 0).astype(BF16))
    gks = [dot(gss[j], expand(slot(w_ref, e, R_Q, R_PIN), mask16)) for j, e in enumerate(es)]
    gkvs = [
        jnp.concatenate([gks[j], gvs[j]], 1).astype(BF16) for j in range(SB)
    ]
    grad_contexts = [
        dot_nt(gkvs[j], stem_kv_weight(w_ref, e)).astype(BF16) for j, e in enumerate(es)
    ]
    prows = [
        jnp.where((row16 == 2) | (row16 == 3), grad_contexts[j][96:112].astype(F32), 0.0)
        for j in range(SB)
    ]
    prow_low = [p.astype(BF16) for p in prows]
    gpacts = [dot_nt(prow_low[j], slot(w_ref, e, 3 * D, 4 * D)) for j, e in enumerate(es)]
    gppres = [
        (gpacts[j] * kept["pslope"][j * PR : (j + 1) * PR]).astype(BF16) for j in range(SB)
    ]
    grad_props = [dot_nt(gppres[j], slot(w_ref, e, R_PIN, R_ATT)) for j, e in enumerate(es)]
    grad_q = [contract(dot_tn(gss[j], kvs[j][:, :D]), SQ) * 0.25 for j in range(SB)]
    grad_wkv = [dot_tn(kept["ctx"][j], gkvs[j]) for j in range(SB)]
    grad_wp = [dot_tn(kept["pact"][j * PR : (j + 1) * PR], prow_low[j]) for j in range(SB)]
    grad_pin = [dot_tn(props[j * PR : (j + 1) * PR], gppres[j]) for j in range(SB)]
    stem = acc["stem"]
    for j, e in enumerate(es):
        stem[e, 0:D, :] += grad_wkv[j][:, :D]
        stem[e, D : 2 * D, :] += grad_wkv[j][:, D:]
        stem[e, 2 * D : 3 * D, :] += grad_wo[j]
        stem[e, 3 * D : 4 * D, :] += grad_wp[j]
        stem[e, R_Q:R_PIN, :] += grad_q[j]
        stem[e, R_PIN:R_ATT, :] += grad_pin[j]
        acc["sb"][pl.ds(2 * e, 1), :] += jnp.sum(gppres[j].astype(F32), 0, keepdims=True)
        acc["sb"][pl.ds(2 * e + 1, 1), :] += jnp.sum(prows[j], 0, keepdims=True)
    return grad_first, grad_contexts, grad_props


ACC = ("stem", "sb", "wqkv", "wout", "up", "down", "vec", "mb")


def acc_shapes():
    return [
        pltpu.VMEM((STEMS, STEM_ROWS, D), F32),
        pltpu.VMEM((2 * STEMS, D), F32),
        pltpu.VMEM((D, 3 * D), F32),
        pltpu.VMEM((D, D), F32),
        pltpu.VMEM((D, FF), F32),
        pltpu.VMEM((D, FF), F32),
        pltpu.VMEM((8, 8, D), F32),
        pltpu.VMEM((8, FF), F32),
    ]


def clear(acc):
    for ref in acc.values():
        ref[...] = jnp.zeros(ref.shape, ref.dtype)


def finish(acc, grad_ref, small_ref):
    def stem_out(e, carry):
        grad_ref[e, 0:STEM_ROWS, :] = acc["stem"][e].astype(grad_ref.dtype)
        return carry

    lax.fori_loop(0, STEMS, stem_out, 0)
    wqkv = acc["wqkv"][...]
    attn = [wqkv[:, :D], wqkv[:, D : 2 * D], wqkv[:, 2 * D :], acc["wout"][...]]
    for block in range(4):
        grad_ref[block * 8 : block * 8 + 8, R_ATT:R_UP, :] = (
            attn[block].astype(grad_ref.dtype).reshape(8, 16, D)
        )
    grad_ref[:, R_UP:R_DOWN, :] = acc["up"][...].T.astype(grad_ref.dtype).reshape(STEMS, 16, D)
    grad_ref[:, R_DOWN:ROWS, :] = acc["down"][...].T.astype(grad_ref.dtype).reshape(STEMS, 16, D)
    small_ref[0:8, :] = jnp.sum(acc["vec"][...], 1)
    mb = jnp.sum(acc["mb"][...], 0, keepdims=True)
    small_ref[8:16, :] = jnp.concatenate(
        [mb[:, i * D : (i + 1) * D] for i in range(4)] + [jnp.zeros((4, D), F32)], 0
    )
    small_ref[16:SMALL, :] = acc["sb"][...]


SAVED = ("ctx", "kv", "prob", "mix", "first", "qkv", "sprob", "smix", "second", "act", "slope", "pact", "pslope")
PER_SAMPLE = ("ctx", "kv", "prob", "sprob")


def saved_shapes(samples):
    rows = samples * TOK
    return dict(
        ctx=((samples, CR, D), BF16),
        kv=((samples, CR, 2 * D), BF16),
        prob=((samples, CR, D), BF16),
        mix=((rows, D), BF16),
        first=((rows, D), F32),
        qkv=((rows, 3 * D), BF16),
        sprob=((samples, TOK, HEADS * TOK), BF16),
        smix=((rows, D), BF16),
        second=((rows, D), F32),
        act=((rows, FF), BF16),
        slope=((rows, FF), BF16),
        pact=((samples * PR, D), BF16),
        pslope=((samples * PR, D), F32),
    )


def step_rows(step, samples):
    shape = (SB * PR, STEPS * samples)
    row = lax.broadcasted_iota(jnp.int32, shape, 0)
    column = (row % PR - 2) * samples + step * SB + row // PR
    held = (row % PR == 2) | (row % PR == 3)
    return jnp.where(held & (lax.broadcasted_iota(jnp.int32, shape, 1) == column), 1.0, 0.0).astype(BF16)


def prop_block(prop_ref, step):
    both = jnp.concatenate([prop_ref[t] for t in range(STEPS)], 1)
    return dot_nt(step_rows(step, prop_ref.shape[2]), both).astype(BF16)


def layer_inputs(layer, vec_ref, mb_ref, sb_ref):
    return (
        vec_ref[layer].astype(F32), mb_ref[layer : layer + 1, :].astype(F32),
        lambda e: sb_ref[layer, e].astype(F32),
    )


def forward_kernel(emb_ref, tok_ref, feat_ref, prop_ref, w_ref, vec_ref, mb_ref, sb_ref, out_ref, *rest):
    saved = rest
    step = pl.program_id(0)
    es = [emb_ref[step * SB + j] for j in range(SB)]
    out, kept = forward_block(
        es, tok_ref[...].astype(F32), feat_ref, prop_block(prop_ref, step), w_ref,
        *layer_inputs(0, vec_ref, mb_ref, sb_ref)
    )
    out_ref[...] = out
    for name, ref in zip(SAVED, saved):
        if name in PER_SAMPLE:
            for j in range(SB):
                ref[j] = kept[name][j].astype(ref.dtype)
        else:
            ref[...] = kept[name].astype(ref.dtype)


def middle_kernel(
    emb_ref, hid_ref, feat_ref, prop_ref, w_ref, vec_ref, mb_ref, sb_ref, cot_ref,
    out_ref, ghid_ref, gfeat_ref, gprop_ref, gw_ref, gsmall_ref, *accs
):
    step = pl.program_id(0)
    acc = dict(zip(ACC, accs))

    pl.when(step == 0)(lambda: clear(acc))

    es = [emb_ref[step * SB + j] for j in range(SB)]
    vec, mb, sb = layer_inputs(1, vec_ref, mb_ref, sb_ref)
    props = prop_block(prop_ref, step)
    out, kept = forward_block(es, hid_ref[...], feat_ref, props, w_ref, vec, mb, sb)
    out_ref[...] = out.astype(BF16)
    ghid, gctx, gprop = backward_block(es, cot_ref[...].astype(F32), kept, props, w_ref, vec, acc)
    ghid_ref[...] = ghid
    for j in range(SB):
        gfeat_ref[j] = gctx[j]
        gprop_ref[j * PR : (j + 1) * PR, :] = gprop[j]
    pl.when(step == pl.num_programs(0) - 1)(lambda: finish(acc, gw_ref, gsmall_ref))


def backward_kernel(emb_ref, grad_ref, prop_ref, w_ref, vec_ref, gfeat1_ref, gprop1_ref, *rest):
    n = len(SAVED)
    saved = rest[:n]
    gtok_ref, gfeat_ref, gprop_ref, gw_ref, gsmall_ref, gprops = rest[n : n + 6]
    acc = dict(zip(ACC, rest[n + 6 :]))
    step = pl.program_id(0)

    pl.when(step == 0)(lambda: clear(acc))

    es = [emb_ref[step * SB + j] for j in range(SB)]
    kept = {name: [ref[j] for j in range(SB)] if name in PER_SAMPLE else ref[...] for name, ref in zip(SAVED, saved)}
    props = prop_block(prop_ref, step)
    vec = vec_ref[0].astype(F32)
    ghid, gctx, gprop = backward_block(es, grad_ref[...], kept, props, w_ref, vec, acc)
    gtok_ref[...] = ghid
    for j in range(0, SB, 4):
        totals = [gctx[i].astype(F32) + gfeat1_ref[i].astype(F32) for i in range(j, j + 4)]
        gfeat_ref[j * STEPS * FR : (j + 4) * STEPS * FR, :] = jnp.concatenate(
            [total[: STEPS * FR] for total in totals], 0
        )
    add_proprio(jnp.concatenate(gprop, 0) + gprop1_ref[...], gprops, step)

    @pl.when(step == pl.num_programs(0) - 1)
    def _():
        finish(acc, gw_ref, gsmall_ref)
        write_proprio(gprops, gprop_ref)


def add_proprio(rows, gprops, step):
    place_ = step_rows(step, gprops.shape[1] // STEPS)
    high = rows.astype(BF16)
    rest = rows - high.astype(F32)
    middle = rest.astype(BF16)
    low = (rest - middle.astype(F32)).astype(BF16)
    part = dot_tn(high, place_) + (dot_tn(middle, place_) + dot_tn(low, place_))
    gprops[...] = jnp.where(step == 0, part, gprops[...] + part)


def write_proprio(gprops, gprop_ref):
    samples = gprop_ref.shape[2]
    for t in range(STEPS):
        gprop_ref[t] = gprops[:, t * samples : (t + 1) * samples]


def blocked(shape, per_step):
    block = (per_step,) + tuple(shape[1:])
    zeros = (0,) * (len(shape) - 1)
    return pl.BlockSpec(block, lambda i, *_: (i,) + zeros)


def whole(shape):
    zeros = (0,) * len(shape)
    return pl.BlockSpec(tuple(shape), lambda i, *_: zeros, pipeline_mode=pl.Buffered(1))


def call(kernel, steps, emb, ins, outs, scratch):
    return pl.pallas_call(
        kernel,
        grid_spec=pltpu.PrefetchScalarGridSpec(
            num_scalar_prefetch=1,
            grid=(steps,),
            in_specs=[blocked(a.shape, n) if n else whole(a.shape) for a, n in ins],
            out_specs=[blocked(s, n) if n else whole(s) for s, _, n in outs],
            scratch_shapes=scratch,
        ),
        out_shape=[jax.ShapeDtypeStruct(s, d) for s, d, _ in outs],
        compiler_params=pltpu.CompilerParams(
            dimension_semantics=("arbitrary",), vmem_limit_bytes=VMEM_LIMIT
        ),
    )(emb, *[a for a, _ in ins])


def compute(tokens, features, proprio, emb, shards, vecs, mbs, sbs, cot, weights=None):
    samples = emb.shape[0]
    steps = samples // SB
    rows = samples * TOK
    rb = SB * TOK
    tok = tokens.reshape(rows, D)
    feat = jnp.swapaxes(features, 1, 2).reshape(samples * FR * STEPS, D)
    prop = proprio.transpose(1, 2, 0)
    fb = SB * FR * STEPS
    shapes = saved_shapes(samples)
    per = lambda s: s[0] // steps
    if weights is None:
        hidden, saved, w0, w1 = gather_forward(tok, feat, prop, emb, vecs, mbs, sbs, shards)
    else:
        w0, w1 = weights
        saved_outs = [(shapes[n][0], shapes[n][1], per(shapes[n][0])) for n in SAVED]
        res = call(
            forward_kernel, steps, emb,
            [(tok, rb), (feat, fb), (prop, 0), (w0, 0), (vecs, 0), (mbs, 0), (sbs, 0)],
            [((rows, D), F32, rb)] + saved_outs, [],
        )
        hidden, saved = res[0], res[1:]
    grad_outs = [((STEMS, ROWS, D), BF16, 0), ((SMALL, D), F32, 0)]
    out, ghid, gfeat1, gprop1, *grads1 = call(
        middle_kernel, steps, emb,
        [(hidden, rb), (feat, fb), (prop, 0), (w1, 0), (vecs, 0), (mbs, 0), (sbs, 0),
         (cot.reshape(rows, D), rb)],
        [((rows, D), BF16, rb), ((rows, D), F32, rb), ((samples, CR, D), BF16, SB),
         ((samples * PR, PROP), F32, SB * PR)] + grad_outs,
        acc_shapes(),
    )
    gtok, gfeat, gprop, *grads0 = call(
        backward_kernel, steps, emb,
        [(ghid, rb), (prop, 0), (w0, 0), (vecs, 0), (gfeat1, SB), (gprop1, SB * PR)]
        + [(a, per(a.shape)) for a in saved],
        [((rows, D), F32, rb), ((samples * FR * STEPS, D), F32, fb), ((STEPS, PROP, samples), F32, 0)]
        + grad_outs,
        [pltpu.VMEM((PROP, STEPS * samples), F32)] + acc_shapes(),
    )
    gfeat = jnp.swapaxes(gfeat.reshape(samples, FR, STEPS, D), 1, 2)
    return (
        out.reshape(tokens.shape), gtok.reshape(tokens.shape), gfeat, gprop.transpose(2, 0, 1),
        grads0, grads1
    )


def chunks_of(layer, bounds):
    groups = []
    for start, stop in zip(bounds[:-1], bounds[1:]):
        half = (stop - start) // 32 * 16
        groups.append(
            [(layer, start, half, ("z", "x", "y")), (layer, start + half, stop - start - half, ("z", "y", "x"))]
        )
    return groups


SIZES = {"z": 4, "y": 2, "x": 2, "c": 2}
AXES = ("z", "y", "x", "c")
MESH = pl.DeviceIdType.MESH


def place():
    me = lax.axis_index("fsdp")
    return {"z": me // 8, "y": (me // 4) % 2, "x": (me // 2) % 2, "c": me % 2}


def number(at):
    return ((at["z"] * 2 + at["y"]) * 2 + at["x"]) * 2 + at["c"]


def moved(at, axis, by):
    out = dict(at)
    out[axis] = (at[axis] + by) % SIZES[axis]
    return out


def greet(at):
    barrier = pltpu.get_barrier_semaphore()
    count = 0
    for axis in AXES:
        for by in range(1, SIZES[axis]):
            pl.semaphore_signal(
                barrier, inc=1, device_id=(number(moved(at, axis, by)),), device_id_type=MESH
            )
            count += 1
    pl.semaphore_wait(barrier, count)


def block(ref, at, done, row, count):
    index = tuple(pl.ds(0, SIZES[a]) if a in done else pl.ds(at[a], 1) for a in AXES)
    return ref.at[index + (pl.ds(row, count), slice(None))]


class Gather:
    def __init__(self, at, outs, groups, send_sem, recv_sem):
        self.at, self.outs, self.groups = at, outs, groups
        self.send_sem, self.recv_sem = send_sem, recv_sem

    def copies(self, g, phase, arriving):
        for i, (layer, row, count, order) in enumerate(self.groups[g]):
            order = order + ("c",)
            axis, done = order[phase], order[:phase]
            for by in range(1, SIZES[axis]):
                whose = moved(self.at, axis, -by) if arriving else self.at
                ref = block(self.outs[layer], whose, done, row, count)
                sem = (2 * g + i, AXES.index(axis), by - 1)
                yield pltpu.make_async_remote_copy(
                    ref, ref, self.send_sem.at[sem], self.recv_sem.at[sem],
                    device_id=(number(moved(self.at, axis, by)),), device_id_type=MESH,
                )

    def start(self, g, phase):
        for copy in self.copies(g, phase, False):
            copy.start()

    def land(self, g, phase):
        for copy in self.copies(g, phase, True):
            copy.wait_recv()

    def run(self, moves):
        for g, phase in moves:
            if phase > 0:
                self.land(g, phase - 1)
            if phase < 4:
                self.start(g, phase)

    def close(self):
        for g in range(len(self.groups)):
            for phase in range(4):
                for copy in self.copies(g, phase, False):
                    copy.wait_send()


BOUNDS = (0, 160, 320, 480, ROWS)
GATHER_GROUPS = chunks_of(0, BOUNDS) + chunks_of(1, BOUNDS)
GATHER_FIRST = (
    (0, 0), (1, 0), (0, 1), (2, 0), (1, 1), (0, 2), (3, 0), (2, 1), (1, 2), (0, 3), (4, 0), (3, 1), (2, 2),
    (1, 3), (5, 0), (0, 4), (3, 2), (2, 3), (1, 4), (6, 0), (3, 3), (7, 0), (2, 4), (3, 4),
)
GATHER_LATER = (
    ((4, 1), (5, 1), (6, 1), (7, 1)),
    ((4, 2), (5, 2)),
    ((6, 2), (7, 2)),
    ((4, 3), (5, 3)),
    ((6, 3), (7, 3), (4, 4), (5, 4), (6, 4), (7, 4)),
)


def place_own(at, shards, outs, local_sem):
    att, up, down, stem, q, pin = shards
    copies = []
    for layer in range(LAYERS):
        own = outs[layer].at[at["z"], at["y"], at["x"], at["c"]]
        pieces = [
            (stem.at[layer, :, pl.ds(j * D, D)], j * D, D) for j in range(4)
        ] + [
            (q.at[layer], R_Q, SQ), (pin.at[layer], R_PIN, PROP), (att.at[layer], R_ATT, 16),
            (up.at[layer], R_UP, 16), (down.at[layer], R_DOWN, 16),
        ]
        for i, (piece, row, count) in enumerate(pieces):
            copies.append(
                pltpu.make_async_copy(piece, own.at[pl.ds(row, count), :], local_sem.at[layer, i])
            )
    return copies


def gather_forward_kernel(emb_ref, tok_ref, feat_ref, prop_ref, vec_ref, mb_ref, sb_ref, *rest):
    shards, (out_ref, g0, g1), rest = rest[:6], rest[6:9], rest[9:]
    saved, (w_ref, local_sem, send_sem, recv_sem, keep_sem) = rest[:-5], rest[-5:]
    step = pl.program_id(0)
    at = place()
    move = Gather(at, (w_ref, g1), GATHER_GROUPS, send_sem, recv_sem)
    keep = pltpu.make_async_copy(w_ref, g0, keep_sem)
    @pl.when(step == 0)
    def _():
        local = place_own(at, shards, (w_ref, g1), local_sem)
        for copy in local:
            copy.start()
        greet(at)
        for copy in local:
            copy.wait()
        move.run(GATHER_FIRST)
        keep.start()

    for i, moves in enumerate(GATHER_LATER[:-1]):
        pl.when(step == i)(functools.partial(move.run, moves))

    es = [emb_ref[step * SB + j] for j in range(SB)]
    out, kept = forward_block(
        es, tok_ref[...].astype(F32), feat_ref, prop_block(prop_ref, step), w_ref,
        *layer_inputs(0, vec_ref, mb_ref, sb_ref)
    )
    out_ref[...] = out
    for name, ref in zip(SAVED, saved):
        if name in PER_SAMPLE:
            for j in range(SB):
                ref[j] = kept[name][j].astype(ref.dtype)
        else:
            ref[...] = kept[name].astype(ref.dtype)

    @pl.when(step == pl.num_programs(0) - 1)
    def _():
        move.run(GATHER_LATER[-1])
        keep.wait()
        move.close()


def gather_forward(tokens, feat, prop, emb, vecs, mbs, sbs, shards):
    samples = emb.shape[0]
    steps = samples // SB
    assert steps == 4
    rows = samples * TOK
    shapes = saved_shapes(samples)
    lead = (4, 2, 2, 2, ROWS, D)
    any_spec = pl.BlockSpec(memory_space=pl.ANY)
    smem = pl.BlockSpec(memory_space=pltpu.SMEM)
    saved = [(shapes[n][0], shapes[n][1], shapes[n][0][0] // steps) for n in SAVED]
    outs = [((rows, D), F32, SB * TOK)] + saved
    weights = jax.ShapeDtypeStruct(lead, BF16)
    res = pl.pallas_call(
        gather_forward_kernel,
        grid=(steps,),
        in_specs=[smem, blocked(tokens.shape, SB * TOK), blocked(feat.shape, SB * FR * STEPS)]
        + [whole(a.shape) for a in (prop, vecs, mbs, sbs)] + [any_spec] * 6,
        out_specs=[blocked(*((outs[0][0], outs[0][2]))), any_spec, any_spec]
        + [blocked(s, n) for s, _, n in outs[1:]],
        out_shape=[jax.ShapeDtypeStruct(*outs[0][:2]), weights, weights]
        + [jax.ShapeDtypeStruct(s, d) for s, d, _ in outs[1:]],
        scratch_shapes=[
            pltpu.VMEM(lead, BF16),
            pltpu.SemaphoreType.DMA((LAYERS, 9)),
            pltpu.SemaphoreType.DMA((2 * len(GATHER_GROUPS), 4, 3)),
            pltpu.SemaphoreType.DMA((2 * len(GATHER_GROUPS), 4, 3)),
            pltpu.SemaphoreType.DMA(()),
        ],
        compiler_params=pltpu.CompilerParams(
            dimension_semantics=("arbitrary",), vmem_limit_bytes=VMEM_LIMIT, collective_id=0,
            has_side_effects=True,
        ),
    )(emb, tokens, feat, prop, vecs, mbs, sbs, *shards)
    hidden, w0, w1 = res[:3]
    return hidden, res[3:], w0.reshape(STEMS, ROWS, D), w1.reshape(STEMS, ROWS, D)


STREAMS = (
    (0, 256, ("z", "x", "y")),
    (256, 256, ("z", "y", "x")),
    (512, 48, ("x", "y", "z")),
    (560, 48, ("y", "x", "z")),
)


def scatter_kernel(
    g0, g1, s0, s1, mats, small,
    acc0, acc1, rc0, rc1, rx0, rx1, ry0, ry1, rz0, rz1, sm, smr, smz,
    send_sem, recv_sem, ssend, srecv,
):
    at = place()
    grads = (g0, g1)
    accs = (acc0, acc1)
    lands = {"c": (rc0, rc1), "x": (rx0, rx1), "y": (ry0, ry1), "z": (rz0, rz1)}
    greet(at)
    chains = [(layer, s) for layer in (1, 0) for s in range(len(STREAMS))]
    sent = []

    def start(chain, phase):
        layer, s = chain
        row, count, order = STREAMS[s]
        order = ("c",) + order[::-1]
        axis = order[phase]
        left = [a for a in AXES if a not in order[: phase + 1]]
        source = grads[layer] if phase == 0 else accs[layer]
        got = []
        for by in range(1, SIZES[axis]):
            to = moved(at, axis, by)
            index = []
            for a in AXES:
                if a == "c" and phase > 0:
                    continue
                if a == axis:
                    index.append(to[a])
                else:
                    index.append(pl.ds(0, SIZES[a]) if a in left else at[a])
            src = source.at[tuple(index) + (pl.ds(row, count), slice(None))]
            index = [] if axis != "z" else [by - 1]
            for a in AXES:
                if a != axis and a != "c":
                    index.append(pl.ds(0, SIZES[a]) if a in left else 0)
            dst = lands[axis][layer].at[tuple(index) + (pl.ds(row, count), slice(None))]
            sem = (layer * 4 + s, AXES.index(axis), by - 1)
            copy = pltpu.make_async_remote_copy(
                src, dst, send_sem.at[sem], recv_sem.at[sem],
                device_id=(number(to),), device_id_type=MESH,
            )
            copy.start()
            sent.append(copy)
            got.append(copy)
        return got

    def add(chain, phase):
        layer, s = chain
        row, count, order = STREAMS[s]
        order = ("c",) + order[::-1]
        axis = order[phase]
        left = [a for a in AXES if a not in order[: phase + 1]]
        source = grads[layer] if phase == 0 else accs[layer]
        acc, land = accs[layer], lands[axis][layer]
        rows = pl.ds(row, count)
        total = 1
        for a in left:
            total *= SIZES[a]

        def one(i, carry):
            spot = dict(at)
            lspot = {"z": 0, "y": 0, "x": 0}
            rest = i
            for a in left[::-1]:
                spot[a] = rest % SIZES[a]
                lspot[a] = spot[a]
                rest = rest // SIZES[a]
            keep = (spot["z"], spot["y"], spot["x"])
            mine = source[keep + ((at["c"],) if phase == 0 else ()) + (rows, slice(None))]
            value = mine.astype(F32)
            for by in range(1, SIZES[axis]):
                index = () if axis != "z" else (by - 1,)
                index += tuple(lspot[a] for a in AXES if a != axis and a != "c")
                value = value + land[index + (rows, slice(None))].astype(F32)
            if phase < 3:
                acc[keep + (rows, slice(None))] = value.astype(BF16)
            else:
                mats[layer, rows, :] = value
            return carry

        if total == 1:
            one(0, 0)
        else:
            lax.fori_loop(0, total, one, 0)

    smalls = ("c", "x", "y", "z")

    def small_start(phase):
        axis = smalls[phase]
        for by in range(1, SIZES[axis]):
            to = moved(at, axis, by)
            dst = smr.at[phase] if axis != "z" else smz.at[at["z"]]
            sem = (phase, by - 1)
            copy = pltpu.make_async_remote_copy(
                sm.at[phase], dst, ssend.at[sem], srecv.at[sem],
                device_id=(number(to),), device_id_type=MESH,
            )
            copy.start()
            sent.append(copy)

    def small_land(phase):
        axis = smalls[phase]
        for by in range(1, SIZES[axis]):
            src = moved(at, axis, -by)
            dst = smr.at[phase] if axis != "z" else smz.at[src["z"]]
            sem = (phase, by - 1)
            pltpu.make_async_remote_copy(
                sm.at[phase], dst, ssend.at[sem], srecv.at[sem],
                device_id=(number(moved(at, axis, by)),), device_id_type=MESH,
            ).wait_recv()
        if axis != "z":
            sm[phase + 1] = sm[phase] + smr[phase]
        else:
            smz[at["z"]] = sm[phase]
            small[...] = (smz[0] + smz[1]) + (smz[2] + smz[3])

    pending = {chain: start(chain, 0) for chain in chains}
    sm[0, 0] = s0[...]
    sm[0, 1] = s1[...]
    small_start(0)
    for phase in range(4):
        for chain in chains:
            for copy in pending.pop(chain):
                copy.wait_recv()
            add(chain, phase)
            if phase < 3:
                pending[chain] = start(chain, phase + 1)
        small_land(phase)
        if phase < 3:
            small_start(phase + 1)
    for copy in sent:
        copy.wait_send()


def scatter(g0, g1, s0, s1):
    def out(*shape):
        return jax.ShapeDtypeStruct(shape, F32)

    vmem = pl.BlockSpec(memory_space=pltpu.VMEM)
    lead = (4, 2, 2, 2, ROWS, D)
    scratch = []
    for shape in ((4, 2, 2), (4, 2, 2), (4, 2), (4, 2), (3, 2, 2)):
        scratch += [pltpu.VMEM(shape + (ROWS, D), BF16)] * 2
    return pl.pallas_call(
        scatter_kernel,
        out_shape=[out(LAYERS, ROWS, D), out(LAYERS, SMALL, D)],
        in_specs=[vmem] * 4,
        out_specs=[vmem] * 2,
        scratch_shapes=scratch
        + [
            pltpu.VMEM((4, LAYERS, SMALL, D), F32),
            pltpu.VMEM((3, LAYERS, SMALL, D), F32),
            pltpu.VMEM((4, LAYERS, SMALL, D), F32),
            pltpu.SemaphoreType.DMA((8, 4, 3)),
            pltpu.SemaphoreType.DMA((8, 4, 3)),
            pltpu.SemaphoreType.DMA((4, 3)),
            pltpu.SemaphoreType.DMA((4, 3)),
        ],
        compiler_params=pltpu.CompilerParams(
            collective_id=1, has_side_effects=True, vmem_limit_bytes=VMEM_LIMIT
        ),
    )(g0.reshape(lead), g1.reshape(lead), s0, s1)


def unpack_kernel(mats, small, att, up, down, stem, q, pin, vec, mb, sb):
    for layer in range(LAYERS):
        for j in range(4):
            stem[layer, :, j * D : (j + 1) * D] = mats[layer, j * D : (j + 1) * D, :]
        q[layer] = mats[layer, R_Q:R_PIN, :]
        pin[layer] = mats[layer, R_PIN:R_ATT, :]
        att[layer] = mats[layer, R_ATT:R_UP, :]
        up[layer] = mats[layer, R_UP:R_DOWN, :]
        down[layer] = mats[layer, R_DOWN:ROWS, :]
        vec[layer] = small[layer, 0:8, :]
        for i in range(4):
            mb[layer : layer + 1, i * D : (i + 1) * D] = small[layer, 8 + i : 9 + i, :]
        sb[layer] = small[layer, 16:SMALL, :]


def unpack(mats, small):
    def out(*shape):
        return jax.ShapeDtypeStruct(shape, F32)

    vmem = pl.BlockSpec(memory_space=pltpu.VMEM)
    return pl.pallas_call(
        unpack_kernel,
        out_shape=[
            out(LAYERS, 16, D), out(LAYERS, 16, D), out(LAYERS, 16, D), out(LAYERS, D, 4 * D),
            out(LAYERS, SQ, D), out(LAYERS, PROP, D), out(LAYERS, 8, D), out(LAYERS, FF),
            out(LAYERS, 2 * STEMS, D),
        ],
        in_specs=[vmem] * 2,
        out_specs=[vmem] * 9,
    )(mats, small)


def pack(attn, up, down, stem, queries, pin):
    gathered = [lax.all_gather(a, "fsdp", axis=1, tiled=True) for a in (attn, up, down, stem, queries, pin)]
    attn, up, down, stem, queries, pin = gathered
    stem = stem.reshape(LAYERS, STEMS, D, 4, D).transpose(0, 1, 3, 2, 4).reshape(LAYERS, STEMS, 4 * D, D)
    parts = [stem] + [a.reshape(LAYERS, STEMS, -1, D) for a in (queries, pin, attn, up, down)]
    return jnp.concatenate(parts, 2)


def unpack_blocks(grad):
    lead = grad.shape[:-2]
    stem = grad[..., : 4 * D, :].reshape(lead + (4, D, D))
    stem = jnp.swapaxes(stem, -3, -2).reshape(lead + (D, 4 * D))
    return (
        grad[..., R_ATT:R_UP, :], grad[..., R_UP:R_DOWN, :], grad[..., R_DOWN:ROWS, :],
        stem, grad[..., R_Q:R_PIN, :], grad[..., R_PIN:R_ATT, :],
    )


def body(n, tokens, features, proprio, embodiment, trunk_attn, feedforward_up_weight, mlp_down,
         stem_mats, stem_queries, prop_in, trunk_vectors, mlp_bias, stem_bias, cotangent):
    shards = (trunk_attn, feedforward_up_weight, mlp_down, stem_mats, stem_queries, prop_in)
    out, gtok, gfeat, gprop, g0, g1 = compute(
        tokens, features, proprio, embodiment, shards, trunk_vectors, mlp_bias, stem_bias,
        cotangent, None if n == 32 else pack(*shards),
    )
    if n == 32:
        *rest, gsb = unpack(*scatter(g0[0], g1[0], g0[1], g1[1]))
        return (out, gtok, gfeat, gprop, *rest, gsb.reshape(LAYERS, STEMS, 2, D))
    mats = [
        lax.psum_scatter(a.reshape(LAYERS, -1, a.shape[-1]), "fsdp", scatter_dimension=1, tiled=True)
        for a in unpack_blocks(jnp.stack([g0[0], g1[0]]).astype(F32))
    ]
    small = lax.psum(jnp.stack([g0[1], g1[1]]), "fsdp")
    gvec = small[:, :8]
    gmb = small[:, 8:12].reshape(LAYERS, FF)
    gsb = small[:, 16:].reshape(LAYERS, STEMS, 2, D)
    return (out, gtok, gfeat, gprop, *mats, gvec, gmb, gsb)


def solution(mesh):
    n = mesh.shape["fsdp"]
    return jax.shard_map(
        functools.partial(body, n),
        mesh=mesh,
        in_specs=(
            P("fsdp"), P("fsdp"), P("fsdp"), P("fsdp"),
            P(None, "fsdp"), P(None, "fsdp"), P(None, "fsdp"), P(None, "fsdp"), P(None, "fsdp"),
            P(None, "fsdp"), P(), P(), P(), P("fsdp"),
        ),
        out_specs=(
            P("fsdp"), P("fsdp"), P("fsdp"), P("fsdp"),
            P(None, "fsdp"), P(None, "fsdp"), P(None, "fsdp"), P(None, "fsdp"), P(None, "fsdp"),
            P(None, "fsdp"), P(), P(), P(),
        ),
        check_vma=False,
    )
```

```python
import functools
import math

import jax
import jax.numpy as jnp
from jax import lax
from jax.experimental import pallas as pl
from jax.experimental.pallas import tpu as pltpu
from jax.sharding import PartitionSpec as P

D = 128
HEADS = 8
HD = 16
FF = 512
SQ = 16
FR = 49
CR = 112
PROP = 32
PR = 16
STEMS = 32
STEPS = 2
LAYERS = 2
TOK = 32
SB = 16

R_Q = 4 * D
R_PIN = R_Q + SQ
R_ATT = R_PIN + PROP
R_UP = R_ATT + 16
R_DOWN = R_UP + 16
ROWS = R_DOWN + 16
STEM_ROWS = R_ATT
SMALL = 16 + 2 * STEMS

F32 = jnp.float32
BF16 = jnp.bfloat16
VMEM_LIMIT = 60 * 1024 * 1024


def dot(a, b):
    return lax.dot_general(a, b, (((1,), (0,)), ((), ())), preferred_element_type=F32)


def dot_nt(a, b):
    return lax.dot_general(a, b, (((1,), (1,)), ((), ())), preferred_element_type=F32)


def dot_tn(a, b):
    return lax.dot_general(a, b, (((0,), (0,)), ((), ())), preferred_element_type=F32)


def gelu_parts(x):
    cdf = 0.5 + 0.5 * lax.erf(x * math.sqrt(0.5))
    slope = cdf + x * (jnp.exp(-0.5 * x * x) * (1.0 / math.sqrt(2.0 * math.pi)))
    return x * cdf, slope


def norm_parts(x):
    centred = x - jnp.mean(x, -1, keepdims=True)
    inverse = lax.rsqrt(jnp.mean(centred * centred, -1, keepdims=True) + 1e-05)
    return centred * inverse, inverse


def norm_back(grad, gain, hat, inverse):
    g = grad * gain
    return inverse * (
        g - jnp.mean(g, -1, keepdims=True) - hat * jnp.mean(g * hat, -1, keepdims=True)
    )


def head_mask(rows, value):
    row = lax.broadcasted_iota(jnp.int32, (HEADS * rows, D), 0) // rows
    lane = lax.broadcasted_iota(jnp.int32, (HEADS * rows, D), 1) // HD
    return jnp.where(row == lane, value, 0.0).astype(BF16)


def expand(rows, mask):
    return jnp.concatenate([rows] * HEADS, 0) * mask


def contract(wide, rows):
    lane = lax.broadcasted_iota(jnp.int32, (rows, D), 1) // HD
    out = wide[:rows]
    for head in range(1, HEADS):
        out = jnp.where(lane == head, wide[head * rows : (head + 1) * rows], out)
    return out


def fold(x):
    return jnp.sum(x.reshape(x.shape[0] // 8, 8, x.shape[1]), 0)


def slot(w_ref, e, start, stop):
    if len(w_ref.shape) == 3:
        return w_ref[e, start:stop, :]
    return w_ref[e // 8, (e // 4) % 2, (e // 2) % 2, e % 2, start:stop, :]


def all_slots(w_ref, start, stop):
    index = (slice(None),) * (len(w_ref.shape) - 2)
    return w_ref[index + (slice(start, stop), slice(None))].reshape(STEMS * (stop - start), D)


def trunk_weights(w_ref):
    attn = all_slots(w_ref, R_ATT, R_UP)
    up = all_slots(w_ref, R_UP, R_DOWN)
    down = all_slots(w_ref, R_DOWN, ROWS)
    wqkv = jnp.concatenate([attn[:D], attn[D : 2 * D], attn[2 * D : 3 * D]], 1)
    return wqkv, attn[3 * D :], up, down


def stem_kv_weight(w_ref, e):
    return jnp.concatenate([slot(w_ref, e, 0, D), slot(w_ref, e, D, 2 * D)], 1)


def step_reduce(x, op):
    x = x.reshape(x.shape[0] // 8, 8, x.shape[1])
    out = x[0]
    for i in range(1, x.shape[0]):
        out = op(out, x[i])
    out = op(out, pltpu.roll(out, 4, 0))
    return op(out, pltpu.roll(out, 2, 0))


def step_apply(x, y, op):
    return op(x.reshape(x.shape[0] // 8, 8, x.shape[1]), y[None]).reshape(x.shape)


def step_masks():
    odd = lax.broadcasted_iota(jnp.int32, (CR, D), 0) % 2
    return (odd == 0).astype(BF16), odd.astype(BF16)


def split_steps(p, masks):
    return jnp.concatenate([p * masks[0], p * masks[1]], 1)


def softmax_rows(score):
    top = jnp.max(score, 0, keepdims=True)
    weight = jnp.exp(score - top)
    return weight * (1.0 / jnp.sum(weight, 0, keepdims=True))


def forward_block(es, hidden, feat_ref, props, w_ref, vec, mb, sb, tick=None):
    kept = {}
    pre = [
        dot(props[j * PR : (j + 1) * PR], slot(w_ref, e, R_PIN, R_ATT))
        + sb(e)[0:1, :]
        for j, e in enumerate(es)
    ]
    pact, pslope = gelu_parts(jnp.concatenate(pre, 0))
    pact = pact.astype(BF16)
    kept["pact"], kept["pslope"] = pact, pslope
    row16 = lax.broadcasted_iota(jnp.int32, (PR, D), 0)
    prows = [
        dot(pact[j * PR : (j + 1) * PR], slot(w_ref, e, 3 * D, 4 * D)) + sb(e)[1:2, :]
        for j, e in enumerate(es)
    ]
    contexts = []
    for j in range(SB):
        rows = feat_ref[j * STEPS * FR : (j + 1) * STEPS * FR, :]
        last = jnp.concatenate([rows[96:98], jnp.zeros((14, D), BF16)], 0).astype(F32)
        tail = jnp.where(row16 < 2, last, jnp.where(row16 < 4, prows[j], 0.0))
        contexts.append(jnp.concatenate([rows[:96], tail.astype(BF16)], 0))
    kept["ctx"] = contexts
    kvs = [dot(contexts[j], stem_kv_weight(w_ref, e)).astype(BF16) for j, e in enumerate(es)]
    kept["kv"] = kvs
    mask16 = head_mask(SQ, 0.25)
    scores = [
        dot_nt(kvs[j][:, :D], expand(slot(w_ref, e, R_Q, R_PIN), mask16)) for j, e in enumerate(es)
    ]
    valid = lax.broadcasted_iota(jnp.int32, (104, D), 0) < STEPS * (FR + 1)
    pad = jnp.zeros((8, D), F32)
    probs = []
    for j in range(SB):
        s = jnp.where(valid, scores[j][:104], -1e30)
        weight = jnp.exp(step_apply(s, step_reduce(s, jnp.maximum), jnp.subtract))
        scale = 1.0 / step_reduce(weight, jnp.add)
        probs.append(jnp.concatenate([step_apply(weight, scale, jnp.multiply), pad], 0))
    kept["prob"] = probs
    masks = step_masks()
    mixes = []
    for j in range(SB):
        wide = dot_tn(split_steps(probs[j].astype(BF16), masks), kvs[j][:, D:])
        mixes += [contract(wide[t * D : (t + 1) * D], SQ).astype(BF16) for t in range(STEPS)]
    mix = jnp.concatenate(mixes, 0)
    kept["mix"] = mix
    if tick is not None:
        tick()
    outs = [
        dot(mix[j * TOK : (j + 1) * TOK], slot(w_ref, e, 2 * D, 3 * D)) for j, e in enumerate(es)
    ]
    first = hidden + jnp.concatenate(outs, 0)
    kept["first"] = first
    wqkv, wout, up, down = trunk_weights(w_ref)
    normed = (norm_parts(first)[0] * vec[0:1] + vec[1:2]).astype(BF16)
    bias = jnp.concatenate([vec[2:3], jnp.zeros((1, D), F32), vec[3:4]], 1)
    qkv = (dot(normed, wqkv) + bias).astype(BF16)
    kept["qkv"] = qkv
    mask32 = head_mask(TOK, 0.25)
    rows = [qkv[j * TOK : (j + 1) * TOK] for j in range(SB)]
    scores = [dot_nt(rows[j][:, D : 2 * D], expand(rows[j][:, :D], mask32)) for j in range(SB)]
    sprobs = [softmax_rows(s) for s in scores]
    smixes = [
        contract(dot_tn(sprobs[j].astype(BF16), rows[j][:, 2 * D :]), TOK).astype(BF16)
        for j in range(SB)
    ]
    kept["sprob"] = sprobs
    smix = jnp.concatenate(smixes, 0)
    kept["smix"] = smix
    second = first + (dot(smix, wout) + vec[4:5])
    kept["second"] = second
    mlp_in = (norm_parts(second)[0] * vec[5:6] + vec[6:7]).astype(BF16)
    act, slope = gelu_parts(dot_nt(mlp_in, up) + mb)
    act = act.astype(BF16)
    kept["act"], kept["slope"] = act, slope
    return second + (dot(act, down) + vec[7:8]), kept


def backward_block(es, grad, kept, props, w_ref, vec, acc, tick=None):
    wqkv, wout, up, down = trunk_weights(w_ref)
    out_low = grad.astype(BF16)
    acc["vec"][7] += fold(out_low.astype(F32))
    acc["down"][...] += dot_tn(out_low, kept["act"])
    grad_act = dot_nt(out_low, down)
    grad_pre = (grad_act * kept["slope"].astype(F32)).astype(BF16)
    acc["mb"][...] += fold(grad_pre.astype(F32))
    hat, inverse = norm_parts(kept["second"])
    mlp_in = (hat * vec[5:6] + vec[6:7]).astype(BF16)
    acc["up"][...] += dot_tn(mlp_in, grad_pre)
    grad_in = dot(grad_pre, up)
    acc["vec"][5] += fold(grad_in * hat)
    acc["vec"][6] += fold(grad_in)
    grad_second = grad + norm_back(grad_in, vec[5:6], hat, inverse)
    branch = grad_second.astype(BF16)
    acc["vec"][4] += fold(branch.astype(F32))
    acc["wout"][...] += dot_tn(kept["smix"], branch)
    grad_mix = dot_nt(branch, wout).astype(BF16)
    mask32 = head_mask(TOK, 0.25)
    mask32_one = head_mask(TOK, 1.0)
    rows = [kept["qkv"][j * TOK : (j + 1) * TOK] for j in range(SB)]
    wides = [expand(grad_mix[j * TOK : (j + 1) * TOK], mask32_one) for j in range(SB)]
    grad_ps = [dot_nt(rows[j][:, 2 * D :], wides[j]) for j in range(SB)]
    grads_v = [dot(kept["sprob"][j].astype(BF16), wides[j]) for j in range(SB)]
    gss = []
    for j in range(SB):
        p = kept["sprob"][j].astype(F32)
        gss.append((p * (grad_ps[j] - jnp.sum(grad_ps[j] * p, 0, keepdims=True))).astype(BF16))
    grads_q = [contract(dot_tn(gss[j], rows[j][:, D : 2 * D]), TOK) * 0.25 for j in range(SB)]
    grads_k = [dot(gss[j], expand(rows[j][:, :D], mask32)) for j in range(SB)]
    grad_qkv = jnp.concatenate(
        [jnp.concatenate(g, 0).astype(BF16) for g in (grads_q, grads_k, grads_v)], 1
    )
    acc["vec"][2] += fold(grad_qkv[:, :D].astype(F32))
    acc["vec"][3] += fold(grad_qkv[:, 2 * D :].astype(F32))
    hat, inverse = norm_parts(kept["first"])
    normed = (hat * vec[0:1] + vec[1:2]).astype(BF16)
    acc["wqkv"][...] += dot_tn(normed, grad_qkv)
    grad_normed = dot_nt(grad_qkv, wqkv)
    acc["vec"][0] += fold(grad_normed * hat)
    acc["vec"][1] += fold(grad_normed)
    grad_first = grad_second + norm_back(grad_normed, vec[0:1], hat, inverse)
    stem_grad = grad_first.astype(BF16)
    mask16 = head_mask(SQ, 0.25)
    mask16_one = head_mask(SQ, 1.0)
    row16 = lax.broadcasted_iota(jnp.int32, (PR, D), 0)
    row8 = lax.broadcasted_iota(jnp.int32, (8, D), 0)
    if tick is not None:
        tick()
    gs_in = [stem_grad[j * TOK : (j + 1) * TOK] for j in range(SB)]
    gmixes = [dot_nt(gs_in[j], slot(w_ref, e, 2 * D, 3 * D)).astype(BF16) for j, e in enumerate(es)]
    grad_wo = [dot_tn(kept["mix"][j * TOK : (j + 1) * TOK], gs_in[j]) for j in range(SB)]
    kvs = [kept["kv"][j] for j in range(SB)]
    probs = [kept["prob"][j] for j in range(SB)]
    wides = [
        jnp.concatenate(
            [expand(gmixes[j][t * SQ : (t + 1) * SQ], mask16_one) for t in range(STEPS)], 0
        )
        for j in range(SB)
    ]
    grad_ps = [dot_nt(kvs[j][:, D:], wides[j]) for j in range(SB)]
    masks = step_masks()
    gvs = [dot(split_steps(probs[j].astype(BF16), masks), wides[j]) for j in range(SB)]
    even = lax.broadcasted_iota(jnp.int32, (104, D), 0) % 2 == 0
    pad = jnp.zeros((8, D), F32)
    gss = []
    for j in range(SB):
        p = probs[j][:104].astype(F32)
        gp = jnp.where(even, grad_ps[j][:104, :D], grad_ps[j][:104, D:])
        gs = p * step_apply(gp, step_reduce(gp * p, jnp.add), jnp.subtract)
        gss.append(jnp.concatenate([gs, pad], 0).astype(BF16))
    gks = [dot(gss[j], expand(slot(w_ref, e, R_Q, R_PIN), mask16)) for j, e in enumerate(es)]
    gkvs = [
        jnp.concatenate([gks[j], gvs[j]], 1).astype(BF16) for j in range(SB)
    ]
    grad_contexts = [
        dot_nt(gkvs[j], stem_kv_weight(w_ref, e)).astype(BF16) for j, e in enumerate(es)
    ]
    prows = [
        jnp.where((row16 == 2) | (row16 == 3), grad_contexts[j][96:112].astype(F32), 0.0)
        for j in range(SB)
    ]
    prow_low = [p.astype(BF16) for p in prows]
    gpacts = [dot_nt(prow_low[j], slot(w_ref, e, 3 * D, 4 * D)) for j, e in enumerate(es)]
    gppres = [
        (gpacts[j] * kept["pslope"][j * PR : (j + 1) * PR]).astype(BF16) for j in range(SB)
    ]
    grad_props = [dot_nt(gppres[j], slot(w_ref, e, R_PIN, R_ATT)) for j, e in enumerate(es)]
    grad_q = [contract(dot_tn(gss[j], kvs[j][:, :D]), SQ) * 0.25 for j in range(SB)]
    grad_wkv = [dot_tn(kept["ctx"][j], gkvs[j]) for j in range(SB)]
    grad_wp = [dot_tn(kept["pact"][j * PR : (j + 1) * PR], prow_low[j]) for j in range(SB)]
    grad_pin = [dot_tn(props[j * PR : (j + 1) * PR], gppres[j]) for j in range(SB)]
    for j, e in enumerate(es):
        bias = jnp.where(
            row8 == 0,
            jnp.sum(gppres[j].astype(F32), 0, keepdims=True),
            jnp.where(row8 == 1, jnp.sum(prows[j], 0, keepdims=True), 0.0),
        )
        acc["add"](
            j, e,
            (
                (0, grad_wkv[j][:, :D]), (D, grad_wkv[j][:, D:]), (2 * D, grad_wo[j]),
                (3 * D, grad_wp[j]), (R_Q, grad_q[j]), (R_PIN, grad_pin[j]), (R_ATT, bias),
            ),
        )
    return grad_first, grad_contexts, grad_props


ACC = ("stem", "wqkv", "wout", "up", "down", "vec", "mb")


def acc_shapes(entries):
    return [
        pltpu.VMEM((entries, STEM_ROWS + 8, D), F32),
        pltpu.VMEM((D, 3 * D), F32),
        pltpu.VMEM((D, D), F32),
        pltpu.VMEM((D, FF), F32),
        pltpu.VMEM((D, FF), F32),
        pltpu.VMEM((8, 8, D), F32),
        pltpu.VMEM((8, FF), F32),
    ]


def clear(acc):
    for ref in acc.values():
        ref[...] = jnp.zeros(ref.shape, ref.dtype)


def add_in_place(acc):
    def add(j, e, pieces):
        for row, value in pieces:
            acc["stem"][e, row : row + value.shape[0], :] += value

    return {**acc, "add": add}


def trunk_blocks(acc):
    wqkv = acc["wqkv"][...]
    attn = [wqkv[:, :D], wqkv[:, D : 2 * D], wqkv[:, 2 * D :], acc["wout"][...]]
    return (
        jnp.concatenate(attn, 0).astype(BF16).reshape(STEMS, 16, D),
        acc["up"][...].T.astype(BF16).reshape(STEMS, 16, D),
        acc["down"][...].T.astype(BF16).reshape(STEMS, 16, D),
    )


def small_rows(acc):
    mb = jnp.sum(acc["mb"][...], 0, keepdims=True)
    return jnp.concatenate(
        [jnp.sum(acc["vec"][...], 1)] + [mb[:, i * D : (i + 1) * D] for i in range(4)]
        + [jnp.zeros((4, D), F32)], 0
    )


def finish(acc, grad_ref, small_ref):
    def stem_out(e, carry):
        grad_ref[e, 0:STEM_ROWS, :] = acc["stem"][e, 0:STEM_ROWS, :].astype(grad_ref.dtype)
        return carry

    lax.fori_loop(0, STEMS, stem_out, 0)
    for i, part in enumerate(trunk_blocks(acc)):
        grad_ref[:, R_ATT + 16 * i : R_ATT + 16 * (i + 1), :] = part
    small_ref[0:16, :] = small_rows(acc)
    for e in range(STEMS):
        small_ref[16 + 2 * e : 18 + 2 * e, :] = acc["stem"][e, STEM_ROWS : STEM_ROWS + 2, :]


SAVED = ("ctx", "kv", "prob", "mix", "first", "qkv", "sprob", "smix", "second", "act", "slope", "pact", "pslope")
PER_SAMPLE = ("ctx", "kv", "prob", "sprob")


def saved_shapes(samples):
    rows = samples * TOK
    return dict(
        ctx=((samples, CR, D), BF16),
        kv=((samples, CR, 2 * D), BF16),
        prob=((samples, CR, D), BF16),
        mix=((rows, D), BF16),
        first=((rows, D), F32),
        qkv=((rows, 3 * D), BF16),
        sprob=((samples, TOK, HEADS * TOK), BF16),
        smix=((rows, D), BF16),
        second=((rows, D), F32),
        act=((rows, FF), BF16),
        slope=((rows, FF), BF16),
        pact=((samples * PR, D), BF16),
        pslope=((samples * PR, D), F32),
    )


def step_rows(step, samples):
    shape = (SB * PR, STEPS * samples)
    row = lax.broadcasted_iota(jnp.int32, shape, 0)
    column = (row % PR - 2) * samples + step * SB + row // PR
    held = (row % PR == 2) | (row % PR == 3)
    return jnp.where(held & (lax.broadcasted_iota(jnp.int32, shape, 1) == column), 1.0, 0.0).astype(BF16)


def prop_block(prop_ref, step):
    both = jnp.concatenate([prop_ref[t] for t in range(STEPS)], 1)
    return dot_nt(step_rows(step, prop_ref.shape[2]), both).astype(BF16)


def layer_inputs(layer, vec_ref, mb_ref, sb_ref):
    return (
        vec_ref[layer].astype(F32), mb_ref[layer : layer + 1, :].astype(F32),
        lambda e: sb_ref[layer, e].astype(F32),
    )


def forward_kernel(emb_ref, tok_ref, feat_ref, prop_ref, w_ref, vec_ref, mb_ref, sb_ref, out_ref, *rest):
    saved = rest
    step = pl.program_id(0)
    es = [emb_ref[step * SB + j] for j in range(SB)]
    out, kept = forward_block(
        es, tok_ref[...].astype(F32), feat_ref, prop_block(prop_ref, step), w_ref,
        *layer_inputs(0, vec_ref, mb_ref, sb_ref)
    )
    out_ref[...] = out
    for name, ref in zip(SAVED, saved):
        if name in PER_SAMPLE:
            for j in range(SB):
                ref[j] = kept[name][j].astype(ref.dtype)
        else:
            ref[...] = kept[name].astype(ref.dtype)


def link_samples(emb_ref, before_ref, last_ref):
    def unset(e, carry):
        last_ref[e] = -1
        return carry

    def link(s, carry):
        e = emb_ref[s]
        before_ref[s] = last_ref[e]
        last_ref[e] = s
        return carry

    lax.fori_loop(0, STEMS, unset, 0)
    lax.fori_loop(0, before_ref.shape[0], link, 0)


def middle_kernel(
    emb_ref, hid_ref, feat_ref, prop_ref, w_ref, vec_ref, mb_ref, sb_ref, cot_ref,
    out_ref, ghid_ref, gfeat_ref, gprop_ref, gw_ref, gsmall_ref, before_ref, last_ref, *accs
):
    step = pl.program_id(0)
    acc = dict(zip(ACC, accs))

    @pl.when(step == 0)
    def _():
        clear(acc)
        link_samples(emb_ref, before_ref, last_ref)

    es = [emb_ref[step * SB + j] for j in range(SB)]
    vec, mb, sb = layer_inputs(1, vec_ref, mb_ref, sb_ref)
    props = prop_block(prop_ref, step)
    out, kept = forward_block(es, hid_ref[...], feat_ref, props, w_ref, vec, mb, sb)
    out_ref[...] = out.astype(BF16)
    ghid, gctx, gprop = backward_block(es, cot_ref[...].astype(F32), kept, props, w_ref, vec, add_in_place(acc))
    ghid_ref[...] = ghid
    for j in range(SB):
        gfeat_ref[j] = gctx[j]
        gprop_ref[j * PR : (j + 1) * PR, :] = gprop[j]
    pl.when(step == pl.num_programs(0) - 1)(lambda: finish(acc, gw_ref, gsmall_ref))


def backward_kernel(emb_ref, grad_ref, prop_ref, w_ref, vec_ref, gfeat1_ref, gprop1_ref, *rest):
    n = len(SAVED)
    saved = rest[:n]
    gtok_ref, gfeat_ref, gprop_ref, gw_ref, gsmall_ref, gprops = rest[n : n + 6]
    acc = dict(zip(ACC, rest[n + 6 :]))
    step = pl.program_id(0)

    pl.when(step == 0)(lambda: clear(acc))

    es = [emb_ref[step * SB + j] for j in range(SB)]
    kept = {name: [ref[j] for j in range(SB)] if name in PER_SAMPLE else ref[...] for name, ref in zip(SAVED, saved)}
    props = prop_block(prop_ref, step)
    vec = vec_ref[0].astype(F32)
    ghid, gctx, gprop = backward_block(es, grad_ref[...], kept, props, w_ref, vec, add_in_place(acc))
    gtok_ref[...] = ghid
    for j in range(0, SB, 4):
        totals = [gctx[i].astype(F32) + gfeat1_ref[i].astype(F32) for i in range(j, j + 4)]
        gfeat_ref[j * STEPS * FR : (j + 4) * STEPS * FR, :] = jnp.concatenate(
            [total[: STEPS * FR] for total in totals], 0
        )
    add_proprio(jnp.concatenate(gprop, 0) + gprop1_ref[...], gprops, step)

    @pl.when(step == pl.num_programs(0) - 1)
    def _():
        finish(acc, gw_ref, gsmall_ref)
        write_proprio(gprops, gprop_ref)


def add_proprio(rows, gprops, step):
    place_ = step_rows(step, gprops.shape[1] // STEPS)
    high = rows.astype(BF16)
    rest = rows - high.astype(F32)
    middle = rest.astype(BF16)
    low = (rest - middle.astype(F32)).astype(BF16)
    part = dot_tn(high, place_) + (dot_tn(middle, place_) + dot_tn(low, place_))
    gprops[...] = jnp.where(step == 0, part, gprops[...] + part)


def write_proprio(gprops, gprop_ref):
    samples = gprop_ref.shape[2]
    for t in range(STEPS):
        gprop_ref[t] = gprops[:, t * samples : (t + 1) * samples]


def blocked(shape, per_step):
    block = (per_step,) + tuple(shape[1:])
    zeros = (0,) * (len(shape) - 1)
    return pl.BlockSpec(block, lambda i, *_: (i,) + zeros)


def whole(shape):
    zeros = (0,) * len(shape)
    return pl.BlockSpec(tuple(shape), lambda i, *_: zeros, pipeline_mode=pl.Buffered(1))


def call(kernel, steps, emb, ins, outs, scratch):
    return pl.pallas_call(
        kernel,
        grid_spec=pltpu.PrefetchScalarGridSpec(
            num_scalar_prefetch=1,
            grid=(steps,),
            in_specs=[blocked(a.shape, n) if n else whole(a.shape) for a, n in ins],
            out_specs=[
                pl.BlockSpec(memory_space=pltpu.SMEM) if n is None else blocked(s, n) if n else whole(s)
                for s, _, n in outs
            ],
            scratch_shapes=scratch,
        ),
        out_shape=[jax.ShapeDtypeStruct(s, d) for s, d, _ in outs],
        compiler_params=pltpu.CompilerParams(
            dimension_semantics=("arbitrary",), vmem_limit_bytes=VMEM_LIMIT
        ),
    )(emb, *[a for a, _ in ins])


def compute(tokens, features, proprio, emb, shards, vecs, mbs, sbs, cot, weights=None):
    samples = emb.shape[0]
    steps = samples // SB
    rows = samples * TOK
    rb = SB * TOK
    tok = tokens.reshape(rows, D)
    feat = jnp.swapaxes(features, 1, 2).reshape(samples * FR * STEPS, D)
    prop = proprio.transpose(1, 2, 0)
    fb = SB * FR * STEPS
    shapes = saved_shapes(samples)
    per = lambda s: s[0] // steps
    if weights is None:
        hidden, saved, w0, w1 = gather_forward(tok, feat, prop, emb, vecs, mbs, sbs, shards)
    else:
        w0, w1 = weights
        saved_outs = [(shapes[n][0], shapes[n][1], per(shapes[n][0])) for n in SAVED]
        res = call(
            forward_kernel, steps, emb,
            [(tok, rb), (feat, fb), (prop, 0), (w0, 0), (vecs, 0), (mbs, 0), (sbs, 0)],
            [((rows, D), F32, rb)] + saved_outs, [],
        )
        hidden, saved = res[0], res[1:]
    grad_outs = [((STEMS, ROWS, D), BF16, 0), ((SMALL, D), F32, 0)]
    out, ghid, gfeat1, gprop1, *grads1, before, last = call(
        middle_kernel, steps, emb,
        [(hidden, rb), (feat, fb), (prop, 0), (w1, 0), (vecs, 0), (mbs, 0), (sbs, 0),
         (cot.reshape(rows, D), rb)],
        [((rows, D), BF16, rb), ((rows, D), F32, rb), ((samples, CR, D), BF16, SB),
         ((samples * PR, PROP), F32, SB * PR)] + grad_outs
        + [((samples,), jnp.int32, None), ((STEMS,), jnp.int32, None)],
        acc_shapes(STEMS),
    )
    backward_ins = (
        [(ghid, rb), (prop, 0), (w0, 0), (vecs, 0), (gfeat1, SB), (gprop1, SB * PR)]
        + [(a, per(a.shape)) for a in saved]
    )
    backward_outs = [
        ((rows, D), F32, rb), ((samples * FR * STEPS, D), F32, fb), ((STEPS, PROP, samples), F32, 0)
    ]
    if weights is None:
        gtok, gfeat, gprop, mats, small = backward_scatter(
            steps, (emb, before, last), backward_ins, backward_outs, *grads1
        )
        gtok, gfeat, *mats, small = unpack(mats, small, gtok, gfeat)
    else:
        gtok, gfeat, gprop, *grads0 = call(
            backward_kernel, steps, emb, backward_ins, backward_outs + grad_outs,
            [pltpu.VMEM((PROP, STEPS * samples), F32)] + acc_shapes(STEMS),
        )
        mats, small = (jnp.stack(pair) for pair in zip(grads0, grads1))
    gfeat = jnp.swapaxes(gfeat.reshape(samples, FR, STEPS, D), 1, 2)
    return (
        out.reshape(tokens.shape), gtok.reshape(tokens.shape), gfeat, gprop.transpose(2, 0, 1),
        mats, small
    )


def chunks_of(layer, bounds):
    groups = []
    for start, stop in zip(bounds[:-1], bounds[1:]):
        half = (stop - start) // 32 * 16
        groups.append(
            [(layer, start, half, ("z", "x", "y")), (layer, start + half, stop - start - half, ("z", "y", "x"))]
        )
    return groups


SIZES = {"z": 4, "y": 2, "x": 2, "c": 2}
AXES = ("z", "y", "x", "c")
MESH = pl.DeviceIdType.MESH


def place():
    me = lax.axis_index("fsdp")
    return {"z": me // 8, "y": (me // 4) % 2, "x": (me // 2) % 2, "c": me % 2}


def number(at):
    return ((at["z"] * 2 + at["y"]) * 2 + at["x"]) * 2 + at["c"]


def moved(at, axis, by):
    out = dict(at)
    out[axis] = (at[axis] + by) % SIZES[axis]
    return out


def greet(at):
    barrier = pltpu.get_barrier_semaphore()
    count = 0
    for axis in AXES:
        for by in range(1, SIZES[axis]):
            pl.semaphore_signal(
                barrier, inc=1, device_id=(number(moved(at, axis, by)),), device_id_type=MESH
            )
            count += 1
    pl.semaphore_wait(barrier, count)


def block(ref, at, done, row, count):
    index = tuple(pl.ds(0, SIZES[a]) if a in done else pl.ds(at[a], 1) for a in AXES)
    return ref.at[index + (pl.ds(row, count), slice(None))]


class Gather:
    def __init__(self, at, outs, groups, send_sem, recv_sem):
        self.at, self.outs, self.groups = at, outs, groups
        self.send_sem, self.recv_sem = send_sem, recv_sem

    def copies(self, g, phase, arriving):
        for i, (layer, row, count, order) in enumerate(self.groups[g]):
            order = order + ("c",)
            axis, done = order[phase], order[:phase]
            for by in range(1, SIZES[axis]):
                whose = moved(self.at, axis, -by) if arriving else self.at
                ref = block(self.outs[layer], whose, done, row, count)
                sem = (2 * g + i, AXES.index(axis), by - 1)
                yield pltpu.make_async_remote_copy(
                    ref, ref, self.send_sem.at[sem], self.recv_sem.at[sem],
                    device_id=(number(moved(self.at, axis, by)),), device_id_type=MESH,
                )

    def start(self, g, phase):
        for copy in self.copies(g, phase, False):
            copy.start()

    def land(self, g, phase):
        for copy in self.copies(g, phase, True):
            copy.wait_recv()

    def run(self, moves):
        for g, phase in moves:
            if phase > 0:
                self.land(g, phase - 1)
            if phase < 4:
                self.start(g, phase)

    def close(self):
        for g in range(len(self.groups)):
            for phase in range(4):
                for copy in self.copies(g, phase, False):
                    copy.wait_send()


BOUNDS = (0, 160, 320, 480, ROWS)
GATHER_GROUPS = chunks_of(0, BOUNDS) + chunks_of(1, BOUNDS)
GATHER_FIRST = (
    (0, 0), (1, 0), (0, 1), (2, 0), (1, 1), (0, 2), (3, 0), (2, 1), (1, 2), (0, 3), (4, 0), (3, 1), (2, 2),
    (1, 3), (0, 4), (5, 0), (3, 2), (4, 1), (2, 3), (1, 4), (6, 0), (5, 1), (3, 3), (2, 4), (7, 0), (3, 4),
)
GATHER_LATER = (
    ((4, 2), (6, 1)),
    ((7, 1),),
    ((5, 2),),
    ((6, 2),),
    ((4, 3),),
    ((7, 2),),
    ((5, 3),),
    ((6, 3),),
)
GATHER_END = ((7, 3), (4, 4), (5, 4), (6, 4), (7, 4))


def place_own(at, shards, outs, local_sem):
    att, up, down, stem, q, pin = shards
    copies = []
    for layer in range(LAYERS):
        own = outs[layer].at[at["z"], at["y"], at["x"], at["c"]]
        pieces = [
            (stem.at[layer, :, pl.ds(j * D, D)], j * D, D) for j in range(4)
        ] + [
            (q.at[layer], R_Q, SQ), (pin.at[layer], R_PIN, PROP), (att.at[layer], R_ATT, 16),
            (up.at[layer], R_UP, 16), (down.at[layer], R_DOWN, 16),
        ]
        for i, (piece, row, count) in enumerate(pieces):
            copies.append(
                pltpu.make_async_copy(piece, own.at[pl.ds(row, count), :], local_sem.at[layer, i])
            )
    return copies


def gather_forward_kernel(emb_ref, tok_ref, feat_ref, prop_ref, vec_ref, mb_ref, sb_ref, *rest):
    shards, (out_ref, g0, g1), rest = rest[:6], rest[6:9], rest[9:]
    saved, (w_ref, local_sem, send_sem, recv_sem, keep_sem) = rest[:-5], rest[-5:]
    step = pl.program_id(0)
    at = place()
    move = Gather(at, (w_ref, g1), GATHER_GROUPS, send_sem, recv_sem)
    keep = pltpu.make_async_copy(w_ref, g0, keep_sem)
    @pl.when(step == 0)
    def _():
        local = place_own(at, shards, (w_ref, g1), local_sem)
        for copy in local:
            copy.start()
        greet(at)
        for copy in local:
            copy.wait()
        move.run(GATHER_FIRST)
        keep.start()

    def moves_at(half):
        for i in range(len(GATHER_LATER) // 2):
            pl.when(step == i)(functools.partial(move.run, GATHER_LATER[2 * i + half]))

    moves_at(0)
    es = [emb_ref[step * SB + j] for j in range(SB)]
    out, kept = forward_block(
        es, tok_ref[...].astype(F32), feat_ref, prop_block(prop_ref, step), w_ref,
        *layer_inputs(0, vec_ref, mb_ref, sb_ref), tick=lambda: moves_at(1)
    )
    out_ref[...] = out
    for name, ref in zip(SAVED, saved):
        if name in PER_SAMPLE:
            for j in range(SB):
                ref[j] = kept[name][j].astype(ref.dtype)
        else:
            ref[...] = kept[name].astype(ref.dtype)

    @pl.when(step == pl.num_programs(0) - 1)
    def _():
        move.run(GATHER_END)
        keep.wait()
        move.close()


def gather_forward(tokens, feat, prop, emb, vecs, mbs, sbs, shards):
    samples = emb.shape[0]
    steps = samples // SB
    assert steps == 4
    rows = samples * TOK
    shapes = saved_shapes(samples)
    lead = (4, 2, 2, 2, ROWS, D)
    any_spec = pl.BlockSpec(memory_space=pl.ANY)
    smem = pl.BlockSpec(memory_space=pltpu.SMEM)
    saved = [(shapes[n][0], shapes[n][1], shapes[n][0][0] // steps) for n in SAVED]
    outs = [((rows, D), F32, SB * TOK)] + saved
    weights = jax.ShapeDtypeStruct(lead, BF16)
    res = pl.pallas_call(
        gather_forward_kernel,
        grid=(steps,),
        in_specs=[smem, blocked(tokens.shape, SB * TOK), blocked(feat.shape, SB * FR * STEPS)]
        + [whole(a.shape) for a in (prop, vecs, mbs, sbs) + tuple(shards)],
        out_specs=[blocked(*((outs[0][0], outs[0][2]))), any_spec, any_spec]
        + [blocked(s, n) for s, _, n in outs[1:]],
        out_shape=[jax.ShapeDtypeStruct(*outs[0][:2]), weights, weights]
        + [jax.ShapeDtypeStruct(s, d) for s, d, _ in outs[1:]],
        scratch_shapes=[
            pltpu.VMEM(lead, BF16),
            pltpu.SemaphoreType.DMA((LAYERS, 9)),
            pltpu.SemaphoreType.DMA((2 * len(GATHER_GROUPS), 4, 3)),
            pltpu.SemaphoreType.DMA((2 * len(GATHER_GROUPS), 4, 3)),
            pltpu.SemaphoreType.DMA(()),
        ],
        compiler_params=pltpu.CompilerParams(
            dimension_semantics=("arbitrary",), vmem_limit_bytes=VMEM_LIMIT, collective_id=0,
            has_side_effects=True,
        ),
    )(emb, tokens, feat, prop, vecs, mbs, sbs, *shards)
    hidden, w0, w1 = res[:3]
    return hidden, res[3:], w0.reshape(STEMS, ROWS, D), w1.reshape(STEMS, ROWS, D)


class Scatter:
    def __init__(self, at, groups, source, acc, lands, out, small, sems):
        self.at, self.groups, self.source, self.acc, self.lands, self.out = at, groups, source, acc, lands, out
        self.send_sem, self.recv_sem, self.small_send, self.small_recv = sems
        self.sm, self.smr, self.smz, self.small_out = small

    def order(self, chunk):
        return ("c",) + chunk[3][::-1]

    def left(self, chunk, phase):
        return [a for a in AXES if a not in self.order(chunk)[: phase + 1]]

    def copies(self, g, phase):
        for i, chunk in enumerate(self.groups[g]):
            _, row, count, _ = chunk
            axis, left = self.order(chunk)[phase], self.left(chunk, phase)
            for by in range(1, SIZES[axis]):
                to = moved(self.at, axis, by)
                src = []
                for a in "zyx":
                    spot = to if a == axis else self.at
                    src.append(pl.ds(0, SIZES[a]) if a in left else spot[a])
                dst = [by - 1] if axis == "z" else [pl.ds(0, SIZES[a]) for a in left]
                source = self.source(to["c"]) if phase == 0 else self.acc
                rows = (pl.ds(row, count), slice(None))
                sem = (2 * g + i, AXES.index(axis), by - 1)
                yield pltpu.make_async_remote_copy(
                    source.at[tuple(src) + rows], self.lands[phase].at[tuple(dst) + rows],
                    self.send_sem.at[sem], self.recv_sem.at[sem],
                    device_id=(number(to),), device_id_type=MESH,
                )

    def add(self, g, phase):
        for chunk in self.groups[g]:
            _, row, count, _ = chunk
            axis, left = self.order(chunk)[phase], self.left(chunk, phase)
            rows = (pl.ds(row, count), slice(None))
            total = 1
            for a in left:
                total *= SIZES[a]

            def one(i, carry):
                spot = dict(self.at)
                rest = i
                for a in left[::-1]:
                    spot[a] = rest % SIZES[a]
                    rest = rest // SIZES[a]
                keep = (spot["z"], spot["y"], spot["x"])
                value = self.acc[keep + rows].astype(F32)
                if axis == "z":
                    for by in range(SIZES["z"] - 1):
                        value = value + self.lands[3][(by,) + rows].astype(F32)
                    self.out[rows] = value
                else:
                    land = tuple(spot[a] for a in left)
                    self.acc[keep + rows] = (value + self.lands[phase][land + rows].astype(F32)).astype(BF16)
                return carry

            if total == 1:
                one(0, 0)
            else:
                lax.fori_loop(0, total, one, 0)

    def small_copies(self, phase, arriving):
        axis = "cxyz"[phase]
        for by in range(1, SIZES[axis]):
            whose = moved(self.at, axis, -by) if arriving else self.at
            dst = self.smz.at[whose["z"]] if axis == "z" else self.smr.at[phase]
            yield pltpu.make_async_remote_copy(
                self.sm.at[phase], dst, self.small_send.at[phase, by - 1], self.small_recv.at[phase, by - 1],
                device_id=(number(moved(self.at, axis, by)),), device_id_type=MESH,
            )

    def small_add(self, phase):
        if phase < 3:
            self.sm[phase + 1] = self.sm[phase] + self.smr[phase]
        else:
            self.smz[self.at["z"]] = self.sm[phase]
            self.small_out[...] = (self.smz[0] + self.smz[1]) + (self.smz[2] + self.smz[3])

    def run(self, moves):
        for g, phase in moves:
            if phase > 0:
                for copy in self.small_copies(phase - 1, True) if g < 0 else self.copies(g, phase - 1):
                    copy.wait_recv()
                self.small_add(phase - 1) if g < 0 else self.add(g, phase - 1)
            if phase < 4:
                for copy in self.small_copies(phase, False) if g < 0 else self.copies(g, phase):
                    copy.start()

    def close(self):
        for phase in range(4):
            for g in range(len(self.groups)):
                for copy in self.copies(g, phase):
                    copy.wait_send()
            for copy in self.small_copies(phase, False):
                copy.wait_send()


SCATTER_GROUPS = chunks_of(0, BOUNDS)
SCATTER_BESIDE = (
    ((0, 0), (1, 0), (2, 0), (3, 0), (-1, 0)),
    ((0, 1), (1, 1), (-1, 1)),
    ((2, 1), (3, 1), (-1, 2)),
    (),
    ((0, 2), (1, 2), (-1, 3)),
    ((2, 2), (-1, 4)),
    ((3, 2),),
    ((0, 3), (1, 3)),
)
SCATTER_END = ((2, 3), (3, 3))


def scatter_last():
    n = len(SCATTER_GROUPS)
    for t in range(n + 4):
        for phase in range(5):
            if 0 <= t - phase < n:
                yield 0, t - phase, phase
        if t < 5:
            yield 0, -1, t
        if 2 <= t < 2 + n:
            yield 1, t - 2, 4


def backward_scatter_kernel(emb_ref, before_ref, last_ref, grad_ref, prop_ref, w_ref, vec_ref, gfeat1_ref, gprop1_ref, *rest):
    n = len(SAVED)
    saved, (g1, s1), rest = rest[:n], rest[n : n + 2], rest[n + 2 :]
    (gtok_ref, gfeat_ref, gprop_ref, mats_ref, small_ref, gprops), rest = rest[:6], rest[6:]
    acc, rest = dict(zip(ACC, rest[: len(ACC)])), rest[len(ACC) :]
    trunk, sbuf, own_sem = rest[:3]
    per_layer = rest[3:]
    step = pl.program_id(0)
    samples = before_ref.shape[0]
    at = place()

    def scatter_of(layer):
        accum, r0, r1, r2, r3, sm, smr, smz, *sems = per_layer[12 * layer : 12 * (layer + 1)]
        source = (lambda c: g1.at[:, :, :, c]) if layer else (lambda c: sbuf)
        return Scatter(
            at, SCATTER_GROUPS, source, accum, (r0, r1, r2, r3), mats_ref.at[layer],
            (sm, smr, smz, small_ref.at[layer]), sems,
        )

    first, second = scatter_of(0), scatter_of(1)
    own = pltpu.make_async_copy(g1.at[:, :, :, at["c"]], second.acc, own_sem)

    @pl.when(step == 0)
    def _():
        own.start()
        greet(at)
        for name in ACC[1:]:
            acc[name][...] = jnp.zeros(acc[name].shape, F32)
        second.sm[0] = s1[...]
        own.wait()
        second.run(SCATTER_BESIDE[0])

    def moves_at(half):
        for i in range(len(SCATTER_BESIDE) // 2):
            if 2 * i + half:
                pl.when(step == i)(functools.partial(second.run, SCATTER_BESIDE[2 * i + half]))

    moves_at(0)
    es = [emb_ref[step * SB + j] for j in range(SB)]
    befores = [before_ref[step * SB + j] for j in range(SB)]
    stem = acc["stem"]

    def add(j, e, pieces):
        for row, value in pieces:
            old = stem[jnp.maximum(befores[j], 0), row : row + value.shape[0], :]
            stem[step * SB + j, row : row + value.shape[0], :] = value + jnp.where(befores[j] >= 0, old, 0.0)

    kept = {
        name: [ref[j] for j in range(SB)] if name in PER_SAMPLE else ref[...]
        for name, ref in zip(SAVED, saved)
    }
    props = prop_block(prop_ref, step)
    ghid, gctx, gprop = backward_block(
        es, grad_ref[...], kept, props, w_ref, vec_ref[0].astype(F32), {**acc, "add": add}, lambda: moves_at(1)
    )
    gtok_ref[...] = ghid
    for j in range(0, SB, 4):
        totals = [gctx[i].astype(F32) + gfeat1_ref[i].astype(F32) for i in range(j, j + 4)]
        gfeat_ref[j * STEPS * FR : (j + 4) * STEPS * FR, :] = jnp.concatenate(
            [total[: STEPS * FR] for total in totals], 0
        )
    add_proprio(jnp.concatenate(gprop, 0) + gprop1_ref[...], gprops, step)

    def gather_group(g):
        start, stop = BOUNDS[g], BOUNDS[g + 1]
        middle = min(stop, STEM_ROWS)

        def one(i, carry):
            spot = (i // 4, (i // 2) % 2, i % 2)
            for ref, c in ((first.acc, at["c"]), (sbuf, 1 - at["c"])):
                e = 2 * i + c
                s = last_ref[e]
                value = stem[jnp.maximum(s, 0), start:middle, :]
                ref[spot + (slice(start, middle), slice(None))] = jnp.where(s >= 0, value, 0.0).astype(BF16)
                if stop > middle:
                    ref[spot + (slice(middle, stop), slice(None))] = trunk[e]
            return carry

        lax.fori_loop(0, STEMS // 2, one, 0)

    @pl.when(step == pl.num_programs(0) - 1)
    def _():
        for i, part in enumerate(trunk_blocks(acc)):
            trunk[:, 16 * i : 16 * (i + 1), :] = part
        first.sm[0, 0:16, :] = small_rows(acc)
        for e in range(STEMS):
            s = last_ref[e]
            value = stem[jnp.maximum(s, 0), STEM_ROWS : STEM_ROWS + 8, :]
            first.sm[0, 16 + 2 * e : 18 + 2 * e, :] = jnp.where(s >= 0, value, 0.0)[0:2]
        second.run(SCATTER_END)
        for layer, g, phase in scatter_last():
            if phase == 0 and g >= 0:
                gather_group(g)
            (first, second)[layer].run(((g, phase),))
        write_proprio(gprops, gprop_ref)
        second.close()
        first.close()


def backward_scatter(steps, scalars, ins, outs, g1, s1):
    lead = (4, 2, 2, 2, ROWS, D)
    samples = scalars[0].shape[0]
    smem = pl.BlockSpec(memory_space=pltpu.SMEM)
    any_spec = pl.BlockSpec(memory_space=pl.ANY)
    outs = outs + [((LAYERS, ROWS, D), F32, 0), ((LAYERS, SMALL, D), F32, 0)]
    per_layer = [
        pltpu.VMEM((4, 2, 2, ROWS, D), BF16),
        pltpu.VMEM((4, 2, 2, ROWS, D), BF16),
        pltpu.VMEM((4, 2, ROWS, D), BF16),
        pltpu.VMEM((4, ROWS, D), BF16),
        pltpu.VMEM((3, ROWS, D), BF16),
        pltpu.VMEM((4, SMALL, D), F32),
        pltpu.VMEM((3, SMALL, D), F32),
        pltpu.VMEM((4, SMALL, D), F32),
        pltpu.SemaphoreType.DMA((2 * len(SCATTER_GROUPS), 4, 3)),
        pltpu.SemaphoreType.DMA((2 * len(SCATTER_GROUPS), 4, 3)),
        pltpu.SemaphoreType.DMA((4, 3)),
        pltpu.SemaphoreType.DMA((4, 3)),
    ]
    return pl.pallas_call(
        backward_scatter_kernel,
        grid=(steps,),
        in_specs=[smem] * 3 + [blocked(a.shape, n) if n else whole(a.shape) for a, n in ins]
        + [any_spec, whole(s1.shape)],
        out_specs=[blocked(s, n) if n else whole(s) for s, _, n in outs],
        out_shape=[jax.ShapeDtypeStruct(s, d) for s, d, _ in outs],
        scratch_shapes=[pltpu.VMEM((PROP, STEPS * samples), F32)] + acc_shapes(samples)
        + [
            pltpu.VMEM((STEMS, 48, D), BF16),
            pltpu.VMEM((4, 2, 2, ROWS, D), BF16),
            pltpu.SemaphoreType.DMA(()),
        ]
        + per_layer * LAYERS,
        compiler_params=pltpu.CompilerParams(
            dimension_semantics=("arbitrary",), vmem_limit_bytes=VMEM_LIMIT, collective_id=1,
            has_side_effects=True,
        ),
    )(*scalars, *[a for a, _ in ins], g1.reshape(lead), s1)


def unpack_kernel(mats, small, gtok_in, gfeat_in, gtok, gfeat, att, up, down, stem, q, pin, vec, mb, sb):
    gtok[...] = gtok_in[...]
    gfeat[...] = gfeat_in[...]
    pl.when(pl.program_id(0) == 0)(
        lambda: split_gradients(mats, small, att, up, down, stem, q, pin, vec, mb, sb)
    )


def split_gradients(mats, small, att, up, down, stem, q, pin, vec, mb, sb):
    for layer in range(LAYERS):
        for j in range(4):
            stem[layer, :, j * D : (j + 1) * D] = mats[layer, j * D : (j + 1) * D, :]
        q[layer] = mats[layer, R_Q:R_PIN, :]
        pin[layer] = mats[layer, R_PIN:R_ATT, :]
        att[layer] = mats[layer, R_ATT:R_UP, :]
        up[layer] = mats[layer, R_UP:R_DOWN, :]
        down[layer] = mats[layer, R_DOWN:ROWS, :]
        vec[layer] = small[layer, 0:8, :]
        for i in range(4):
            mb[layer : layer + 1, i * D : (i + 1) * D] = small[layer, 8 + i : 9 + i, :]
        sb[layer] = small[layer, 16:SMALL, :]


def unpack(mats, small, gtok, gfeat):
    outs = [
        (LAYERS, 16, D), (LAYERS, 16, D), (LAYERS, 16, D), (LAYERS, D, 4 * D), (LAYERS, SQ, D),
        (LAYERS, PROP, D), (LAYERS, 8, D), (LAYERS, FF), (LAYERS, 2 * STEMS, D),
    ]
    steps = 4
    moved_through = [blocked(a.shape, a.shape[0] // steps) for a in (gtok, gfeat)]
    return pl.pallas_call(
        unpack_kernel,
        grid=(steps,),
        out_shape=[jax.ShapeDtypeStruct(s, F32) for s in [gtok.shape, gfeat.shape] + outs],
        in_specs=[whole(mats.shape), whole(small.shape)] + moved_through,
        out_specs=moved_through + [whole(s) for s in outs],
    )(mats, small, gtok, gfeat)


def pack(attn, up, down, stem, queries, pin):
    gathered = [lax.all_gather(a, "fsdp", axis=1, tiled=True) for a in (attn, up, down, stem, queries, pin)]
    attn, up, down, stem, queries, pin = gathered
    stem = stem.reshape(LAYERS, STEMS, D, 4, D).transpose(0, 1, 3, 2, 4).reshape(LAYERS, STEMS, 4 * D, D)
    parts = [stem] + [a.reshape(LAYERS, STEMS, -1, D) for a in (queries, pin, attn, up, down)]
    return jnp.concatenate(parts, 2)


def unpack_blocks(grad):
    lead = grad.shape[:-2]
    stem = grad[..., : 4 * D, :].reshape(lead + (4, D, D))
    stem = jnp.swapaxes(stem, -3, -2).reshape(lead + (D, 4 * D))
    return (
        grad[..., R_ATT:R_UP, :], grad[..., R_UP:R_DOWN, :], grad[..., R_DOWN:ROWS, :],
        stem, grad[..., R_Q:R_PIN, :], grad[..., R_PIN:R_ATT, :],
    )


def body(n, tokens, features, proprio, embodiment, trunk_attn, feedforward_up_weight, mlp_down,
         stem_mats, stem_queries, prop_in, trunk_vectors, mlp_bias, stem_bias, cotangent):
    shards = (trunk_attn, feedforward_up_weight, mlp_down, stem_mats, stem_queries, prop_in)
    out, gtok, gfeat, gprop, mats, small = compute(
        tokens, features, proprio, embodiment, shards, trunk_vectors, mlp_bias, stem_bias,
        cotangent, None if n == 32 else pack(*shards),
    )
    if n == 32:
        return (out, gtok, gfeat, gprop, *mats, small.reshape(LAYERS, STEMS, 2, D))
    mats = [
        lax.psum_scatter(a.reshape(LAYERS, -1, a.shape[-1]), "fsdp", scatter_dimension=1, tiled=True)
        for a in unpack_blocks(mats.astype(F32))
    ]
    small = lax.psum(small, "fsdp")
    gvec = small[:, :8]
    gmb = small[:, 8:12].reshape(LAYERS, FF)
    gsb = small[:, 16:].reshape(LAYERS, STEMS, 2, D)
    return (out, gtok, gfeat, gprop, *mats, gvec, gmb, gsb)


def solution(mesh):
    n = mesh.shape["fsdp"]
    return jax.shard_map(
        functools.partial(body, n),
        mesh=mesh,
        in_specs=(
            P("fsdp"), P("fsdp"), P("fsdp"), P("fsdp"),
            P(None, "fsdp"), P(None, "fsdp"), P(None, "fsdp"), P(None, "fsdp"), P(None, "fsdp"),
            P(None, "fsdp"), P(), P(), P(), P("fsdp"),
        ),
        out_specs=(
            P("fsdp"), P("fsdp"), P("fsdp"), P("fsdp"),
            P(None, "fsdp"), P(None, "fsdp"), P(None, "fsdp"), P(None, "fsdp"), P(None, "fsdp"),
            P(None, "fsdp"), P(), P(), P(),
        ),
        check_vma=False,
    )
```

```python
import functools
import math

import jax
import jax.numpy as jnp
from jax import lax
from jax.experimental import pallas as pl
from jax.experimental.pallas import tpu as pltpu
from jax.sharding import PartitionSpec as P

D = 128
HEADS = 8
HD = 16
FF = 512
SQ = 16
FR = 49
CR = 112
PROP = 32
STEMS = 32
STEPS = 2
LAYERS = 2
TOK = 32
SB = 16

R_Q = 3 * D
R_WP = R_Q + SQ
R_PIN = R_WP + D
R_ATT = R_PIN + PROP
R_UP = R_ATT + 16
R_DOWN = R_UP + 16
ROWS = R_DOWN + 16
STEM_ROWS = R_WP
SMALL = 16 + 2 * STEMS

MAT_ROWS = (0, D, 2 * D, R_WP)

F32 = jnp.float32
BF16 = jnp.bfloat16
VMEM_LIMIT = 60 * 1024 * 1024


def dot(a, b):
    return lax.dot_general(a, b, (((1,), (0,)), ((), ())), preferred_element_type=F32)


def dot_nt(a, b):
    return lax.dot_general(a, b, (((1,), (1,)), ((), ())), preferred_element_type=F32)


def dot_tn(a, b):
    return lax.dot_general(a, b, (((0,), (0,)), ((), ())), preferred_element_type=F32)


def gelu_parts(x):
    cdf = 0.5 + 0.5 * lax.erf(x * math.sqrt(0.5))
    slope = cdf + x * (jnp.exp(-0.5 * x * x) * (1.0 / math.sqrt(2.0 * math.pi)))
    return x * cdf, slope


def norm_parts(x):
    centred = x - jnp.mean(x, -1, keepdims=True)
    inverse = lax.rsqrt(jnp.mean(centred * centred, -1, keepdims=True) + 1e-05)
    return centred * inverse, inverse


def norm_back(grad, gain, hat, inverse):
    g = grad * gain
    return inverse * (
        g - jnp.mean(g, -1, keepdims=True) - hat * jnp.mean(g * hat, -1, keepdims=True)
    )


def head_mask(rows, value):
    row = lax.broadcasted_iota(jnp.int32, (HEADS * rows, D), 0) // rows
    lane = lax.broadcasted_iota(jnp.int32, (HEADS * rows, D), 1) // HD
    return jnp.where(row == lane, value, 0.0).astype(BF16)


def expand(rows, mask):
    return jnp.concatenate([rows] * HEADS, 0) * mask


def contract(wide, rows):
    lane = lax.broadcasted_iota(jnp.int32, (rows, D), 1) // HD
    out = wide[:rows]
    for head in range(1, HEADS):
        out = jnp.where(lane == head, wide[head * rows : (head + 1) * rows], out)
    return out


def fold(x):
    return jnp.sum(x.reshape(x.shape[0] // 8, 8, x.shape[1]), 0)


def slot(w_ref, e, start, stop):
    if len(w_ref.shape) == 3:
        return w_ref[e, start:stop, :]
    return w_ref[e // 8, (e // 4) % 2, (e // 2) % 2, e % 2, start:stop, :]


def all_slots(w_ref, start, stop):
    index = (slice(None),) * (len(w_ref.shape) - 2)
    return w_ref[index + (slice(start, stop), slice(None))].reshape(STEMS * (stop - start), D)


def trunk_weights(w_ref):
    attn = all_slots(w_ref, R_ATT, R_UP)
    up = all_slots(w_ref, R_UP, R_DOWN)
    down = all_slots(w_ref, R_DOWN, ROWS)
    wqkv = jnp.concatenate([attn[:D], attn[D : 2 * D], attn[2 * D : 3 * D]], 1)
    return wqkv, attn[3 * D :], up, down


def stem_kv_weight(w_ref, e):
    return jnp.concatenate([slot(w_ref, e, 0, D), slot(w_ref, e, D, 2 * D)], 1)


def step_reduce(x, op):
    x = x.reshape(x.shape[0] // 8, 8, x.shape[1])
    out = x[0]
    for i in range(1, x.shape[0]):
        out = op(out, x[i])
    out = op(out, pltpu.roll(out, 4, 0))
    return op(out, pltpu.roll(out, 2, 0))


def step_apply(x, y, op):
    return op(x.reshape(x.shape[0] // 8, 8, x.shape[1]), y[None]).reshape(x.shape)


def step_masks():
    odd = lax.broadcasted_iota(jnp.int32, (CR, D), 0) % 2
    return (odd == 0).astype(BF16), odd.astype(BF16)


def split_steps(p, masks):
    return jnp.concatenate([p * masks[0], p * masks[1]], 1)


def softmax_rows(score):
    top = jnp.max(score, 0, keepdims=True)
    weight = jnp.exp(score - top)
    return weight * (1.0 / jnp.sum(weight, 0, keepdims=True))


def stem_ids(emb_ref, rows, down=False):
    samples = emb_ref.shape[1]
    row = lax.broadcasted_iota(jnp.int32, (rows, samples), 0) // STEPS
    pick = (row == lax.broadcasted_iota(jnp.int32, (rows, samples), 1)).astype(BF16)
    stems = jnp.broadcast_to(emb_ref[...].astype(F32).astype(BF16), (D, samples))
    return dot_nt(stems, pick) if down else dot_nt(pick, stems)


def spread(values, ids):
    values = values.astype(F32)
    return jnp.concatenate([jnp.where(ids == e, values, 0.0).astype(BF16) for e in range(STEMS)], 1)


def sample_rows(samples):
    shape = (samples * STEPS, samples * STEPS)
    row = lax.broadcasted_iota(jnp.int32, shape, 0)
    column = (row % STEPS) * samples + row // STEPS
    return (lax.broadcasted_iota(jnp.int32, shape, 1) == column).astype(BF16)


def spread_down(values, ids):
    values = values.astype(F32)
    return jnp.concatenate([jnp.where(ids == e, values, 0.0).astype(BF16) for e in range(STEMS)], 0)


def spread_proprio(prop_ref, ids, down=False):
    both = jnp.concatenate([prop_ref[t] for t in range(STEPS)], 1)
    group = D // PROP
    tiled = jnp.concatenate([both] * group, 0)
    place_ = sample_rows(prop_ref.shape[2])
    rows = dot_nt(tiled, place_) if down else dot_nt(place_, tiled)
    entry = (lax.broadcasted_iota(jnp.int32, rows.shape, 0 if down else 1) // PROP).astype(F32)
    return jnp.concatenate(
        [jnp.where(ids == entry + float(group * b), rows, 0.0).astype(BF16) for b in range(STEMS // group)],
        0 if down else 1,
    )


def bias_picks(ids):
    lane = lax.broadcasted_iota(jnp.int32, (ids.shape[0], 2 * STEMS), 1).astype(F32)
    twice = 2.0 * ids[:, : 2 * STEMS]
    return (lane == twice).astype(BF16), (lane == twice + 1.0).astype(BF16)


def proprio_forward(emb_ref, prop_ref, w_ref, biases):
    ids = stem_ids(emb_ref, STEPS * emb_ref.shape[1])
    first, second = bias_picks(ids)
    pre = dot(spread_proprio(prop_ref, ids), all_slots(w_ref, R_PIN, R_ATT)) + dot(first, biases)
    act, slope = gelu_parts(pre)
    act = act.astype(BF16)
    return act, slope, dot(spread(act, ids), all_slots(w_ref, R_WP, R_PIN)) + dot(second, biases)


def proprio_backward(emb_ref, prop_ref, w_ref, act, slope, grad_rows):
    ids = stem_ids(emb_ref, STEPS * emb_ref.shape[1])
    first, second = bias_picks(ids)
    low = grad_rows.astype(BF16)
    wp = jnp.concatenate([slot(w_ref, e, R_WP, R_PIN) for e in range(STEMS)], 1)
    pin = jnp.concatenate([slot(w_ref, e, R_PIN, R_ATT) for e in range(STEMS)], 1)
    grad_pre = (dot_nt(spread(low, ids), wp) * slope).astype(BF16)
    down = stem_ids(emb_ref, STEPS * emb_ref.shape[1], True)
    return (
        dot(spread_down(act.astype(F32).T, down), low), dot(spread_proprio(prop_ref, down, True), grad_pre),
        dot_tn(first, grad_pre) + dot_tn(second, low), dot_nt(spread(grad_pre, ids), pin),
    )


def forward_block(es, hidden, feat_ref, prows, w_ref, vec, mb, tick=None):
    kept = {}
    row8 = lax.broadcasted_iota(jnp.int32, (8, D), 0)
    contexts = []
    for j in range(SB):
        rows = feat_ref[j * STEPS * FR : (j + 1) * STEPS * FR, :]
        last = jnp.concatenate([rows[96:98], jnp.zeros((14, D), BF16)], 0).astype(F32)[:8]
        k = j // 4 * 8
        mine = pltpu.roll(prows[k : k + 8], (2 - 2 * (j % 4)) % 8, 0)
        tail = jnp.where(row8 < 2, last, jnp.where(row8 < 4, mine, 0.0))
        tail = jnp.concatenate([tail, jnp.zeros((8, D), F32)], 0).astype(BF16)
        contexts.append(jnp.concatenate([rows[:96], tail], 0))
    kept["ctx"] = contexts
    kvs = [dot(contexts[j], stem_kv_weight(w_ref, e)).astype(BF16) for j, e in enumerate(es)]
    kept["kv"] = kvs
    mask16 = head_mask(SQ, 0.25)
    scores = [
        dot_nt(kvs[j][:, :D], expand(slot(w_ref, e, R_Q, R_WP), mask16)) for j, e in enumerate(es)
    ]
    valid = lax.broadcasted_iota(jnp.int32, (104, D), 0) < STEPS * (FR + 1)
    pad = jnp.zeros((8, D), F32)
    probs = []
    for j in range(SB):
        s = jnp.where(valid, scores[j][:104], -1e30)
        weight = jnp.exp(step_apply(s, step_reduce(s, jnp.maximum), jnp.subtract))
        scale = 1.0 / step_reduce(weight, jnp.add)
        probs.append(jnp.concatenate([step_apply(weight, scale, jnp.multiply), pad], 0))
    kept["prob"] = probs
    masks = step_masks()
    mixes = []
    for j in range(SB):
        wide = dot_tn(split_steps(probs[j].astype(BF16), masks), kvs[j][:, D:])
        mixes += [contract(wide[t * D : (t + 1) * D], SQ).astype(BF16) for t in range(STEPS)]
    mix = jnp.concatenate(mixes, 0)
    kept["mix"] = mix
    if tick is not None:
        tick()
    outs = [
        dot(mix[j * TOK : (j + 1) * TOK], slot(w_ref, e, 2 * D, 3 * D)) for j, e in enumerate(es)
    ]
    first = hidden + jnp.concatenate(outs, 0)
    kept["first"] = first
    wqkv, wout, up, down = trunk_weights(w_ref)
    normed = (norm_parts(first)[0] * vec[0:1] + vec[1:2]).astype(BF16)
    bias = jnp.concatenate([vec[2:3], jnp.zeros((1, D), F32), vec[3:4]], 1)
    qkv = (dot(normed, wqkv) + bias).astype(BF16)
    kept["qkv"] = qkv
    mask32 = head_mask(TOK, 0.25)
    rows = [qkv[j * TOK : (j + 1) * TOK] for j in range(SB)]
    scores = [dot_nt(rows[j][:, D : 2 * D], expand(rows[j][:, :D], mask32)) for j in range(SB)]
    sprobs = [softmax_rows(s) for s in scores]
    smixes = [
        contract(dot_tn(sprobs[j].astype(BF16), rows[j][:, 2 * D :]), TOK).astype(BF16)
        for j in range(SB)
    ]
    kept["sprob"] = sprobs
    smix = jnp.concatenate(smixes, 0)
    kept["smix"] = smix
    second = first + (dot(smix, wout) + vec[4:5])
    kept["second"] = second
    mlp_in = (norm_parts(second)[0] * vec[5:6] + vec[6:7]).astype(BF16)
    act, slope = gelu_parts(dot_nt(mlp_in, up) + mb)
    act = act.astype(BF16)
    kept["act"], kept["slope"] = act, slope
    return second + (dot(act, down) + vec[7:8]), kept


def backward_block(es, grad, kept, w_ref, vec, acc, tick=None):
    wqkv, wout, up, down = trunk_weights(w_ref)
    out_low = grad.astype(BF16)
    acc["vec"][7] += fold(out_low.astype(F32))
    acc["down"][...] += dot_tn(out_low, kept["act"])
    grad_act = dot_nt(out_low, down)
    grad_pre = (grad_act * kept["slope"].astype(F32)).astype(BF16)
    acc["mb"][...] += fold(grad_pre.astype(F32))
    hat, inverse = norm_parts(kept["second"])
    mlp_in = (hat * vec[5:6] + vec[6:7]).astype(BF16)
    acc["up"][...] += dot_tn(mlp_in, grad_pre)
    grad_in = dot(grad_pre, up)
    acc["vec"][5] += fold(grad_in * hat)
    acc["vec"][6] += fold(grad_in)
    grad_second = grad + norm_back(grad_in, vec[5:6], hat, inverse)
    branch = grad_second.astype(BF16)
    acc["vec"][4] += fold(branch.astype(F32))
    acc["wout"][...] += dot_tn(kept["smix"], branch)
    grad_mix = dot_nt(branch, wout).astype(BF16)
    mask32 = head_mask(TOK, 0.25)
    mask32_one = head_mask(TOK, 1.0)
    rows = [kept["qkv"][j * TOK : (j + 1) * TOK] for j in range(SB)]
    wides = [expand(grad_mix[j * TOK : (j + 1) * TOK], mask32_one) for j in range(SB)]
    grad_ps = [dot_nt(rows[j][:, 2 * D :], wides[j]) for j in range(SB)]
    grads_v = [dot(kept["sprob"][j].astype(BF16), wides[j]) for j in range(SB)]
    gss = []
    for j in range(SB):
        p = kept["sprob"][j].astype(F32)
        gss.append((p * (grad_ps[j] - jnp.sum(grad_ps[j] * p, 0, keepdims=True))).astype(BF16))
    grads_q = [contract(dot_tn(gss[j], rows[j][:, D : 2 * D]), TOK) * 0.25 for j in range(SB)]
    grads_k = [dot(gss[j], expand(rows[j][:, :D], mask32)) for j in range(SB)]
    grad_qkv = jnp.concatenate(
        [jnp.concatenate(g, 0).astype(BF16) for g in (grads_q, grads_k, grads_v)], 1
    )
    acc["vec"][2] += fold(grad_qkv[:, :D].astype(F32))
    acc["vec"][3] += fold(grad_qkv[:, 2 * D :].astype(F32))
    hat, inverse = norm_parts(kept["first"])
    normed = (hat * vec[0:1] + vec[1:2]).astype(BF16)
    acc["wqkv"][...] += dot_tn(normed, grad_qkv)
    grad_normed = dot_nt(grad_qkv, wqkv)
    acc["vec"][0] += fold(grad_normed * hat)
    acc["vec"][1] += fold(grad_normed)
    grad_first = grad_second + norm_back(grad_normed, vec[0:1], hat, inverse)
    stem_grad = grad_first.astype(BF16)
    mask16 = head_mask(SQ, 0.25)
    mask16_one = head_mask(SQ, 1.0)
    row8 = lax.broadcasted_iota(jnp.int32, (8, D), 0)
    if tick is not None:
        tick()
    gs_in = [stem_grad[j * TOK : (j + 1) * TOK] for j in range(SB)]
    gmixes = [dot_nt(gs_in[j], slot(w_ref, e, 2 * D, 3 * D)).astype(BF16) for j, e in enumerate(es)]
    grad_wo = [dot_tn(kept["mix"][j * TOK : (j + 1) * TOK], gs_in[j]) for j in range(SB)]
    kvs = [kept["kv"][j] for j in range(SB)]
    probs = [kept["prob"][j] for j in range(SB)]
    wides = [
        jnp.concatenate(
            [expand(gmixes[j][t * SQ : (t + 1) * SQ], mask16_one) for t in range(STEPS)], 0
        )
        for j in range(SB)
    ]
    grad_ps = [dot_nt(kvs[j][:, D:], wides[j]) for j in range(SB)]
    masks = step_masks()
    gvs = [dot(split_steps(probs[j].astype(BF16), masks), wides[j]) for j in range(SB)]
    even = lax.broadcasted_iota(jnp.int32, (104, D), 0) % 2 == 0
    pad = jnp.zeros((8, D), F32)
    gss = []
    for j in range(SB):
        p = probs[j][:104].astype(F32)
        gp = jnp.where(even, grad_ps[j][:104, :D], grad_ps[j][:104, D:])
        gs = p * step_apply(gp, step_reduce(gp * p, jnp.add), jnp.subtract)
        gss.append(jnp.concatenate([gs, pad], 0).astype(BF16))
    gks = [dot(gss[j], expand(slot(w_ref, e, R_Q, R_WP), mask16)) for j, e in enumerate(es)]
    gkvs = [
        jnp.concatenate([gks[j], gvs[j]], 1).astype(BF16) for j in range(SB)
    ]
    grad_contexts = [
        dot_nt(gkvs[j], stem_kv_weight(w_ref, e)).astype(BF16) for j, e in enumerate(es)
    ]
    grad_prows = []
    for k in range(0, SB, 4):
        rows = jnp.zeros((8, D), F32)
        for j in range(k, k + 4):
            tail = pltpu.roll(grad_contexts[j][96:112].astype(F32)[:8], (2 * (j % 4) - 2) % 8, 0)
            rows = jnp.where(row8 // 2 == j % 4, tail, rows)
        grad_prows.append(rows)
    grad_q = [contract(dot_tn(gss[j], kvs[j][:, :D]), SQ) * 0.25 for j in range(SB)]
    grad_wkv = [dot_tn(kept["ctx"][j], gkvs[j]) for j in range(SB)]
    for j, e in enumerate(es):
        acc["add"](
            j, e,
            ((0, grad_wkv[j][:, :D]), (D, grad_wkv[j][:, D:]), (2 * D, grad_wo[j]), (R_Q, grad_q[j])),
        )
    return grad_first, grad_contexts, jnp.concatenate(grad_prows, 0)


ACC = ("stem", "wqkv", "wout", "up", "down", "vec", "mb")


def acc_shapes(entries):
    return [
        pltpu.VMEM((entries, STEM_ROWS, D), F32),
        pltpu.VMEM((D, 3 * D), F32),
        pltpu.VMEM((D, D), F32),
        pltpu.VMEM((D, FF), F32),
        pltpu.VMEM((D, FF), F32),
        pltpu.VMEM((8, 8, D), F32),
        pltpu.VMEM((8, FF), F32),
    ]


def clear(acc):
    for ref in acc.values():
        ref[...] = jnp.zeros(ref.shape, ref.dtype)


def add_in_place(acc):
    def add(j, e, pieces):
        for row, value in pieces:
            acc["stem"][e, row : row + value.shape[0], :] += value

    return {**acc, "add": add}


def trunk_blocks(acc):
    wqkv = acc["wqkv"][...]
    attn = [wqkv[:, :D], wqkv[:, D : 2 * D], wqkv[:, 2 * D :], acc["wout"][...]]
    return (
        jnp.concatenate(attn, 0).astype(BF16).reshape(STEMS, 16, D),
        acc["up"][...].T.astype(BF16).reshape(STEMS, 16, D),
        acc["down"][...].T.astype(BF16).reshape(STEMS, 16, D),
    )


def small_rows(acc):
    mb = jnp.sum(acc["mb"][...], 0, keepdims=True)
    return jnp.concatenate(
        [jnp.sum(acc["vec"][...], 1)] + [mb[:, i * D : (i + 1) * D] for i in range(4)]
        + [jnp.zeros((4, D), F32)], 0
    )


def other_blocks(acc, grads):
    grad_wp, grad_pin = grads
    return (
        (R_WP, grad_wp.astype(BF16).reshape(STEMS, D, D)),
        (R_PIN, grad_pin.astype(BF16).reshape(STEMS, PROP, D)),
    ) + tuple((R_ATT + 16 * i, part) for i, part in enumerate(trunk_blocks(acc)))


def finish(acc, grads, bias, grad_ref, small_ref):
    def stem_out(e, carry):
        grad_ref[e, 0:STEM_ROWS, :] = acc["stem"][e].astype(grad_ref.dtype)
        return carry

    lax.fori_loop(0, STEMS, stem_out, 0)
    for start, part in other_blocks(acc, grads):
        grad_ref[:, start : start + part.shape[1], :] = part
    small_ref[0:16, :] = small_rows(acc)
    small_ref[16:SMALL, :] = bias


SAVED = ("ctx", "kv", "prob", "mix", "first", "qkv", "sprob", "smix", "second", "act", "slope")
PER_SAMPLE = ("ctx", "kv", "prob", "sprob")


def saved_shapes(samples):
    rows = samples * TOK
    return dict(
        ctx=((samples, CR, D), BF16),
        kv=((samples, CR, 2 * D), BF16),
        prob=((samples, CR, D), BF16),
        mix=((rows, D), BF16),
        first=((rows, D), F32),
        qkv=((rows, 3 * D), BF16),
        sprob=((samples, TOK, HEADS * TOK), BF16),
        smix=((rows, D), BF16),
        second=((rows, D), F32),
        act=((rows, FF), BF16),
        slope=((rows, FF), BF16),
    )


def layer_inputs(layer, vec_ref, mb_ref):
    return vec_ref[layer].astype(F32), mb_ref[layer : layer + 1, :].astype(F32)


def start_forward(layer, emb_ref, prop_ref, w_ref, sb_ref, act_ref, slope_ref, rows_ref):
    act_ref[...], slope_ref[...], rows_ref[...] = proprio_forward(emb_ref, prop_ref, w_ref, sb_ref[layer])


def block_rows(step):
    return pl.ds(pl.multiple_of(step * SB * STEPS, SB * STEPS), SB * STEPS)


def save(kept, saved):
    for name, ref in zip(SAVED, saved):
        if name in PER_SAMPLE:
            for j in range(SB):
                ref[j] = kept[name][j].astype(ref.dtype)
        else:
            ref[...] = kept[name].astype(ref.dtype)


def load(saved):
    return {
        name: [ref[j] for j in range(SB)] if name in PER_SAMPLE else ref[...]
        for name, ref in zip(SAVED, saved)
    }


def forward_kernel(
    emb_ref, ids_ref, tok_ref, feat_ref, prop_ref, w_ref, vec_ref, mb_ref, sb_ref, out_ref, act_ref, slope_ref, *rest
):
    saved, rows_ref = rest[:-1], rest[-1]
    step = pl.program_id(0)
    pl.when(step == 0)(
        lambda: start_forward(0, ids_ref, prop_ref, w_ref, sb_ref, act_ref, slope_ref, rows_ref)
    )
    es = [emb_ref[step * SB + j] for j in range(SB)]
    out, kept = forward_block(
        es, tok_ref[...].astype(F32), feat_ref, rows_ref[block_rows(step), :], w_ref,
        *layer_inputs(0, vec_ref, mb_ref)
    )
    out_ref[...] = out
    save(kept, saved)


def link_samples(emb_ref, before_ref, last_ref):
    def unset(e, carry):
        last_ref[e] = -1
        return carry

    def link(s, carry):
        e = emb_ref[s]
        before_ref[s] = last_ref[e]
        last_ref[e] = s
        return carry

    lax.fori_loop(0, STEMS, unset, 0)
    lax.fori_loop(0, before_ref.shape[0], link, 0)


def middle_kernel(
    emb_ref, ids_ref, hid_ref, feat_ref, prop_ref, w_ref, vec_ref, mb_ref, sb_ref, cot_ref,
    out_ref, ghid_ref, gfeat_ref, gprop_ref, gw_ref, gsmall_ref, before_ref, last_ref,
    act_ref, slope_ref, rows_ref, grows_ref, *accs
):
    step = pl.program_id(0)
    acc = dict(zip(ACC, accs))

    @pl.when(step == 0)
    def _():
        clear(acc)
        link_samples(emb_ref, before_ref, last_ref)
        start_forward(1, ids_ref, prop_ref, w_ref, sb_ref, act_ref, slope_ref, rows_ref)

    es = [emb_ref[step * SB + j] for j in range(SB)]
    vec, mb = layer_inputs(1, vec_ref, mb_ref)
    out, kept = forward_block(
        es, hid_ref[...], feat_ref, rows_ref[block_rows(step), :], w_ref, vec, mb
    )
    out_ref[...] = out.astype(BF16)
    ghid, gctx, grows = backward_block(
        es, cot_ref[...].astype(F32), kept, w_ref, vec, add_in_place(acc)
    )
    ghid_ref[...] = ghid
    grows_ref[block_rows(step), :] = grows
    for j in range(SB):
        gfeat_ref[j] = gctx[j]

    @pl.when(step == pl.num_programs(0) - 1)
    def _():
        *grads, bias, gprop_ref[...] = proprio_backward(
            ids_ref, prop_ref, w_ref, act_ref[...], slope_ref[...], grows_ref[...]
        )
        finish(acc, grads, bias, gw_ref, gsmall_ref)


def write_features(gctx, gfeat1_ref, gfeat_ref):
    for j in range(0, SB, 4):
        totals = [gctx[i].astype(F32) + gfeat1_ref[i].astype(F32) for i in range(j, j + 4)]
        gfeat_ref[j * STEPS * FR : (j + 4) * STEPS * FR, :] = jnp.concatenate(
            [total[: STEPS * FR] for total in totals], 0
        )


def write_proprio(rows, gprop_ref):
    samples = gprop_ref.shape[2]
    place_ = sample_rows(samples)
    high = rows.astype(BF16)
    rest = rows - high.astype(F32)
    middle = rest.astype(BF16)
    low = (rest - middle.astype(F32)).astype(BF16)
    out = dot_tn(high, place_) + (dot_tn(middle, place_) + dot_tn(low, place_))
    for t in range(STEPS):
        gprop_ref[t] = out[:, t * samples : (t + 1) * samples]


def backward_kernel(
    emb_ref, ids_ref, grad_ref, prop_ref, w_ref, vec_ref, gfeat1_ref, gprop1_ref, act_ref, slope_ref, *rest
):
    n = len(SAVED)
    saved = rest[:n]
    gtok_ref, gfeat_ref, gprop_ref, gw_ref, gsmall_ref, grows_ref = rest[n : n + 6]
    acc = dict(zip(ACC, rest[n + 6 :]))
    step = pl.program_id(0)
    pl.when(step == 0)(lambda: clear(acc))
    es = [emb_ref[step * SB + j] for j in range(SB)]
    vec = vec_ref[0].astype(F32)
    ghid, gctx, grows = backward_block(es, grad_ref[...], load(saved), w_ref, vec, add_in_place(acc))
    gtok_ref[...] = ghid
    grows_ref[block_rows(step), :] = grows
    write_features(gctx, gfeat1_ref, gfeat_ref)

    @pl.when(step == pl.num_programs(0) - 1)
    def _():
        *grads, bias, gprop = proprio_backward(
            ids_ref, prop_ref, w_ref, act_ref[...], slope_ref[...], grows_ref[...]
        )
        finish(acc, grads, bias, gw_ref, gsmall_ref)
        write_proprio(gprop + gprop1_ref[...], gprop_ref)


def blocked(shape, per_step):
    block = (per_step,) + tuple(shape[1:])
    zeros = (0,) * (len(shape) - 1)
    return pl.BlockSpec(block, lambda i, *_: (i,) + zeros)


def whole(shape):
    zeros = (0,) * len(shape)
    return pl.BlockSpec(tuple(shape), lambda i, *_: zeros, pipeline_mode=pl.Buffered(1))


def call(kernel, steps, emb, ins, outs, scratch):
    return pl.pallas_call(
        kernel,
        grid_spec=pltpu.PrefetchScalarGridSpec(
            num_scalar_prefetch=1,
            grid=(steps,),
            in_specs=[blocked(a.shape, n) if n else whole(a.shape) for a, n in ins],
            out_specs=[
                pl.BlockSpec(memory_space=pltpu.SMEM) if n is None else blocked(s, n) if n else whole(s)
                for s, _, n in outs
            ],
            scratch_shapes=scratch,
        ),
        out_shape=[jax.ShapeDtypeStruct(s, d) for s, d, _ in outs],
        compiler_params=pltpu.CompilerParams(
            dimension_semantics=("arbitrary",), vmem_limit_bytes=VMEM_LIMIT
        ),
    )(emb, *[a for a, _ in ins])


def compute(tokens, features, proprio, emb, shards, vecs, mbs, sbs, cot, weights=None):
    samples = emb.shape[0]
    steps = samples // SB
    rows = samples * TOK
    rb = SB * TOK
    tok = tokens.reshape(rows, D)
    feat = jnp.swapaxes(features, 1, 2).reshape(samples * FR * STEPS, D)
    prop = proprio.transpose(1, 2, 0)
    ids = emb.reshape(1, samples)
    sbs = sbs.reshape(LAYERS, 2 * STEMS, D)
    fb = SB * FR * STEPS
    prows = (STEPS * samples, D)
    shapes = saved_shapes(samples)
    per = lambda s: s[0] // steps
    forward_ins = [(ids, 0), (tok, rb), (feat, fb), (prop, 0), (vecs, 0), (mbs, 0), (sbs, 0)]
    forward_outs = [((rows, D), F32, rb), (prows, BF16, 0), (prows, F32, 0)] + [
        (shapes[n][0], shapes[n][1], per(shapes[n][0])) for n in SAVED
    ]
    if weights is None:
        hidden, act, slope, w0, w1, *saved = gather_forward(steps, emb, forward_ins, forward_outs, shards)
    else:
        w0, w1 = weights
        forward_ins = forward_ins[:4] + [(w0, 0)] + forward_ins[4:]
        hidden, act, slope, *saved = call(
            forward_kernel, steps, emb, forward_ins, forward_outs, [pltpu.VMEM(prows, F32)]
        )
    grad_outs = [((STEMS, ROWS, D), BF16, 0), ((SMALL, D), F32, 0)]
    out, ghid, gfeat1, gprop1, *grads1, before, last = call(
        middle_kernel, steps, emb,
        [(ids, 0), (hidden, rb), (feat, fb), (prop, 0), (w1, 0), (vecs, 0), (mbs, 0), (sbs, 0),
         (cot.reshape(rows, D), rb)],
        [((rows, D), BF16, rb), ((rows, D), F32, rb), ((samples, CR, D), BF16, SB),
         ((STEPS * samples, PROP), F32, 0)] + grad_outs
        + [((samples,), jnp.int32, None), ((STEMS,), jnp.int32, None)],
        [pltpu.VMEM(prows, BF16)] + [pltpu.VMEM(prows, F32)] * 3 + acc_shapes(STEMS),
    )
    backward_ins = (
        [(ids, 0), (ghid, rb), (prop, 0), (w0, 0), (vecs, 0), (gfeat1, SB), (gprop1, 0), (act, 0), (slope, 0)]
        + [(a, per(a.shape)) for a in saved]
    )
    backward_outs = [
        ((rows, D), F32, rb), ((samples * FR * STEPS, D), F32, fb), ((STEPS, PROP, samples), F32, 0)
    ]
    if weights is None:
        gtok, gfeat, gprop, mats, small = backward_scatter(
            steps, (emb, before, last), backward_ins, backward_outs, *grads1
        )
        gtok, gfeat, *mats, small = unpack(mats, small, gtok, gfeat)
    else:
        gtok, gfeat, gprop, *grads0 = call(
            backward_kernel, steps, emb, backward_ins, backward_outs + grad_outs,
            [pltpu.VMEM(prows, F32)] + acc_shapes(STEMS),
        )
        mats, small = (jnp.stack(pair) for pair in zip(grads0, grads1))
    gfeat = jnp.swapaxes(gfeat.reshape(samples, FR, STEPS, D), 1, 2)
    return (
        out.reshape(tokens.shape), gtok.reshape(tokens.shape), gfeat, gprop.transpose(2, 0, 1),
        mats, small
    )


def chunks_of(layer, bounds):
    groups = []
    for start, stop in zip(bounds[:-1], bounds[1:]):
        half = (stop - start) // 32 * 16
        groups.append(
            [(layer, start, half, ("z", "x", "y")), (layer, start + half, stop - start - half, ("z", "y", "x"))]
        )
    return groups


SIZES = {"z": 4, "y": 2, "x": 2, "c": 2}
AXES = ("z", "y", "x", "c")
MESH = pl.DeviceIdType.MESH


def place():
    me = lax.axis_index("fsdp")
    return {"z": me // 8, "y": (me // 4) % 2, "x": (me // 2) % 2, "c": me % 2}


def number(at):
    return ((at["z"] * 2 + at["y"]) * 2 + at["x"]) * 2 + at["c"]


def moved(at, axis, by):
    out = dict(at)
    out[axis] = (at[axis] + by) % SIZES[axis]
    return out


def greet(at):
    barrier = pltpu.get_barrier_semaphore()
    count = 0
    for axis in AXES:
        for by in range(1, SIZES[axis]):
            pl.semaphore_signal(
                barrier, inc=1, device_id=(number(moved(at, axis, by)),), device_id_type=MESH
            )
            count += 1
    pl.semaphore_wait(barrier, count)


def block(ref, at, done, row, count):
    index = tuple(pl.ds(0, SIZES[a]) if a in done else pl.ds(at[a], 1) for a in AXES)
    return ref.at[index + (pl.ds(row, count), slice(None))]


class Gather:
    def __init__(self, at, outs, groups, send_sem, recv_sem):
        self.at, self.outs, self.groups = at, outs, groups
        self.send_sem, self.recv_sem = send_sem, recv_sem

    def copies(self, g, phase, arriving):
        for i, (layer, row, count, order) in enumerate(self.groups[g]):
            order = order + ("c",)
            axis, done = order[phase], order[:phase]
            for by in range(1, SIZES[axis]):
                whose = moved(self.at, axis, -by) if arriving else self.at
                ref = block(self.outs[layer], whose, done, row, count)
                sem = (2 * g + i, AXES.index(axis), by - 1)
                yield pltpu.make_async_remote_copy(
                    ref, ref, self.send_sem.at[sem], self.recv_sem.at[sem],
                    device_id=(number(moved(self.at, axis, by)),), device_id_type=MESH,
                )

    def start(self, g, phase):
        for copy in self.copies(g, phase, False):
            copy.start()

    def land(self, g, phase):
        for copy in self.copies(g, phase, True):
            copy.wait_recv()

    def run(self, moves):
        for g, phase in moves:
            if phase > 0:
                self.land(g, phase - 1)
            if phase < 4:
                self.start(g, phase)

    def close(self):
        for g in range(len(self.groups)):
            for phase in range(4):
                for copy in self.copies(g, phase, False):
                    copy.wait_send()


BOUNDS = (0, 160, 320, 480, ROWS)
HALVES = (0, 320, ROWS)
GATHER_GROUPS = chunks_of(0, BOUNDS) + chunks_of(1, HALVES)
GATHER_FIRST = (
    (0, 0), (1, 0), (0, 1), (2, 0), (1, 1), (0, 2), (3, 0), (2, 1), (1, 2), (0, 3), (4, 0), (3, 1), (2, 2),
    (5, 0), (1, 3), (0, 4), (3, 2), (2, 3), (1, 4), (4, 1), (3, 3), (2, 4), (5, 1), (3, 4),
)
GATHER_LATER = ((), ((4, 2),), (), ((5, 2),), (), (), ((4, 3),), ())
GATHER_END = ((5, 3), (4, 4), (5, 4))


def place_own(at, shards, outs, local_sem):
    att, up, down, stem, q, pin = shards
    copies = []
    for layer in range(LAYERS):
        own = outs[layer].at[at["z"], at["y"], at["x"], at["c"]]
        pieces = [
            (stem.at[layer, :, pl.ds(j * D, D)], row, D) for j, row in enumerate(MAT_ROWS)
        ] + [
            (q.at[layer], R_Q, SQ), (pin.at[layer], R_PIN, PROP), (att.at[layer], R_ATT, 16),
            (up.at[layer], R_UP, 16), (down.at[layer], R_DOWN, 16),
        ]
        for i, (piece, row, count) in enumerate(pieces):
            copies.append(
                pltpu.make_async_copy(piece, own.at[pl.ds(row, count), :], local_sem.at[layer, i])
            )
    return copies


def gather_forward_kernel(emb_ref, ids_ref, tok_ref, feat_ref, prop_ref, vec_ref, mb_ref, sb_ref, *rest):
    shards, (out_ref, act_ref, slope_ref, g0, g1), rest = rest[:6], rest[6:11], rest[11:]
    saved, (rows_ref, w_ref, local_sem, send_sem, recv_sem, keep_sem) = rest[:-6], rest[-6:]
    step = pl.program_id(0)
    at = place()
    move = Gather(at, (w_ref, g1), GATHER_GROUPS, send_sem, recv_sem)
    keep = pltpu.make_async_copy(w_ref, g0, keep_sem)

    @pl.when(step == 0)
    def _():
        local = place_own(at, shards, (w_ref, g1), local_sem)
        for copy in local:
            copy.start()
        greet(at)
        for copy in local:
            copy.wait()
        move.run(GATHER_FIRST)
        keep.start()
        start_forward(0, ids_ref, prop_ref, w_ref, sb_ref, act_ref, slope_ref, rows_ref)

    def moves_at(half):
        for i in range(len(GATHER_LATER) // 2):
            pl.when(step == i)(functools.partial(move.run, GATHER_LATER[2 * i + half]))

    moves_at(0)
    es = [emb_ref[step * SB + j] for j in range(SB)]
    out, kept = forward_block(
        es, tok_ref[...].astype(F32), feat_ref, rows_ref[block_rows(step), :], w_ref,
        *layer_inputs(0, vec_ref, mb_ref), tick=lambda: moves_at(1)
    )
    out_ref[...] = out
    save(kept, saved)

    @pl.when(step == pl.num_programs(0) - 1)
    def _():
        move.run(GATHER_END)
        keep.wait()
        move.close()


def gather_forward(steps, emb, ins, outs, shards):
    assert 2 * steps == len(GATHER_LATER)
    lead = (4, 2, 2, 2, ROWS, D)
    any_spec = pl.BlockSpec(memory_space=pl.ANY)
    smem = pl.BlockSpec(memory_space=pltpu.SMEM)
    weights = jax.ShapeDtypeStruct(lead, BF16)
    ins = ins + [(a, 0) for a in shards]
    specs = [blocked(s, n) if n else whole(s) for s, _, n in outs]
    shapes = [jax.ShapeDtypeStruct(s, d) for s, d, _ in outs]
    groups = 2 * len(GATHER_GROUPS)
    res = pl.pallas_call(
        gather_forward_kernel,
        grid=(steps,),
        in_specs=[smem] + [blocked(a.shape, n) if n else whole(a.shape) for a, n in ins],
        out_specs=specs[:3] + [any_spec, any_spec] + specs[3:],
        out_shape=shapes[:3] + [weights, weights] + shapes[3:],
        scratch_shapes=[
            pltpu.VMEM(outs[2][0], F32),
            pltpu.VMEM(lead, BF16),
            pltpu.SemaphoreType.DMA((LAYERS, 9)),
            pltpu.SemaphoreType.DMA((groups, 4, 3)),
            pltpu.SemaphoreType.DMA((groups, 4, 3)),
            pltpu.SemaphoreType.DMA(()),
        ],
        compiler_params=pltpu.CompilerParams(
            dimension_semantics=("arbitrary",), vmem_limit_bytes=VMEM_LIMIT, collective_id=0,
            has_side_effects=True,
        ),
    )(emb, *[a for a, _ in ins])
    hidden, act, slope, w0, w1, *saved = res
    return (hidden, act, slope, w0.reshape(STEMS, ROWS, D), w1.reshape(STEMS, ROWS, D), *saved)


class Scatter:
    def __init__(self, at, groups, source, acc, lands, out, small, sems):
        self.at, self.groups, self.source, self.acc, self.lands, self.out = at, groups, source, acc, lands, out
        self.send_sem, self.recv_sem, self.small_send, self.small_recv = sems
        self.sm, self.smr, self.smz, self.small_out = small

    def order(self, chunk):
        return ("c",) + chunk[3][::-1]

    def left(self, chunk, phase):
        return [a for a in AXES if a not in self.order(chunk)[: phase + 1]]

    def copies(self, g, phase):
        for i, chunk in enumerate(self.groups[g]):
            _, row, count, _ = chunk
            axis, left = self.order(chunk)[phase], self.left(chunk, phase)
            for by in range(1, SIZES[axis]):
                to = moved(self.at, axis, by)
                src = []
                for a in "zyx":
                    spot = to if a == axis else self.at
                    src.append(pl.ds(0, SIZES[a]) if a in left else spot[a])
                dst = [by - 1] if axis == "z" else [pl.ds(0, SIZES[a]) for a in left]
                source = self.source(to["c"]) if phase == 0 else self.acc
                rows = (pl.ds(row, count), slice(None))
                sem = (2 * g + i, AXES.index(axis), by - 1)
                yield pltpu.make_async_remote_copy(
                    source.at[tuple(src) + rows], self.lands[phase].at[tuple(dst) + rows],
                    self.send_sem.at[sem], self.recv_sem.at[sem],
                    device_id=(number(to),), device_id_type=MESH,
                )

    def add(self, g, phase):
        for chunk in self.groups[g]:
            _, row, count, _ = chunk
            axis, left = self.order(chunk)[phase], self.left(chunk, phase)
            rows = (pl.ds(row, count), slice(None))
            keep = tuple(slice(None) if a in left else self.at[a] for a in "zyx") + rows
            value = self.acc[keep].astype(F32)
            if axis == "z":
                for by in range(SIZES["z"] - 1):
                    value = value + self.lands[3][(by,) + rows].astype(F32)
                self.out[rows] = value
            else:
                land = (slice(None),) * len(left) + rows
                self.acc[keep] = (value + self.lands[phase][land].astype(F32)).astype(BF16)

    def small_copies(self, phase, arriving):
        axis = "cxyz"[phase]
        for by in range(1, SIZES[axis]):
            whose = moved(self.at, axis, -by) if arriving else self.at
            dst = self.smz.at[whose["z"]] if axis == "z" else self.smr.at[phase]
            yield pltpu.make_async_remote_copy(
                self.sm.at[phase], dst, self.small_send.at[phase, by - 1], self.small_recv.at[phase, by - 1],
                device_id=(number(moved(self.at, axis, by)),), device_id_type=MESH,
            )

    def small_add(self, phase):
        if phase < 3:
            self.sm[phase + 1] = self.sm[phase] + self.smr[phase]
        else:
            self.smz[self.at["z"]] = self.sm[phase]
            self.small_out[...] = (self.smz[0] + self.smz[1]) + (self.smz[2] + self.smz[3])

    def run(self, moves):
        for g, phase in moves:
            if phase > 0:
                for copy in self.small_copies(phase - 1, True) if g < 0 else self.copies(g, phase - 1):
                    copy.wait_recv()
                self.small_add(phase - 1) if g < 0 else self.add(g, phase - 1)
            if phase < 4:
                for copy in self.small_copies(phase, False) if g < 0 else self.copies(g, phase):
                    copy.start()

    def close(self):
        for phase in range(4):
            for g in range(len(self.groups)):
                for copy in self.copies(g, phase):
                    copy.wait_send()
            for copy in self.small_copies(phase, False):
                copy.wait_send()


SCATTER_GROUPS = (chunks_of(0, BOUNDS), chunks_of(1, HALVES))
SCATTER_BESIDE = (
    ((1, 0), (0, 0), (-1, 0)),
    ((-1, 1),),
    ((0, 1), (-1, 2)),
    ((1, 1), (-1, 3)),
    ((-1, 4),),
    ((0, 2),),
    ((1, 2),),
    (),
)
SCATTER_END = (
    (0, 0, 0), (0, -1, 0), (1, 0, 3), (0, 1, 0), (0, 0, 1), (0, -1, 1), (0, 2, 0), (1, 1, 3), (0, 1, 1), (0, 0, 2),
    (0, -1, 2), (0, 3, 0), (0, 2, 1), (1, 0, 4), (0, 1, 2), (1, 1, 4), (0, 0, 3), (0, -1, 3), (0, 3, 1), (0, 2, 2),
    (0, 1, 3), (0, 0, 4), (0, -1, 4), (0, 3, 2), (0, 2, 3), (0, 1, 4), (0, 3, 3), (0, 2, 4), (0, 3, 4),
)


def backward_scatter_kernel(
    emb_ref, before_ref, last_ref, ids_ref, grad_ref, prop_ref, w_ref, vec_ref, gfeat1_ref, gprop1_ref,
    act_ref, slope_ref, *rest
):
    n = len(SAVED)
    saved, (g1, s1), rest = rest[:n], rest[n : n + 2], rest[n + 2 :]
    (gtok_ref, gfeat_ref, gprop_ref, mats_ref, small_ref, grows_ref), rest = rest[:6], rest[6:]
    acc, rest = dict(zip(ACC, rest[: len(ACC)])), rest[len(ACC) :]
    others, sbuf, own_sem = rest[:3]
    per_layer = rest[3:]
    step = pl.program_id(0)
    samples = before_ref.shape[0]
    at = place()

    def scatter_of(layer):
        accum, r0, r1, r2, r3, sm, smr, smz, *sems = per_layer[12 * layer : 12 * (layer + 1)]
        source = (lambda c: g1.at[:, :, :, c]) if layer else (lambda c: sbuf)
        return Scatter(
            at, SCATTER_GROUPS[layer], source, accum, (r0, r1, r2, r3), mats_ref.at[layer],
            (sm, smr, smz, small_ref.at[layer]), sems,
        )

    first, second = scatter_of(0), scatter_of(1)
    own = pltpu.make_async_copy(g1.at[:, :, :, at["c"]], second.acc, own_sem)

    @pl.when(step == 0)
    def _():
        own.start()
        greet(at)
        for name in ACC[1:]:
            acc[name][...] = jnp.zeros(acc[name].shape, F32)
        second.sm[0] = s1[...]
        own.wait()
        second.run(SCATTER_BESIDE[0])

    def moves_at(half):
        for i in range(len(SCATTER_BESIDE) // 2):
            if 2 * i + half:
                pl.when(step == i)(functools.partial(second.run, SCATTER_BESIDE[2 * i + half]))

    moves_at(0)
    es = [emb_ref[step * SB + j] for j in range(SB)]
    befores = [before_ref[step * SB + j] for j in range(SB)]
    stem = acc["stem"]

    def add(j, e, pieces):
        for row, value in pieces:
            old = stem[jnp.maximum(befores[j], 0), row : row + value.shape[0], :]
            stem[step * SB + j, row : row + value.shape[0], :] = value + jnp.where(befores[j] >= 0, old, 0.0)

    ghid, gctx, grows = backward_block(
        es, grad_ref[...], load(saved), w_ref, vec_ref[0].astype(F32), {**acc, "add": add},
        lambda: moves_at(1)
    )
    gtok_ref[...] = ghid
    grows_ref[block_rows(step), :] = grows
    write_features(gctx, gfeat1_ref, gfeat_ref)

    def gather_group(g):
        start, stop = BOUNDS[g], BOUNDS[g + 1]

        def line(z, carry):
            for i in range(4):
                spot = (z, i // 2, i % 2)
                for ref, c in ((first.acc, at["c"]), (sbuf, 1 - at["c"])):
                    e = 8 * z + 2 * i + c
                    s = last_ref[e]
                    if start < STEM_ROWS:
                        end = min(stop, STEM_ROWS)
                        value = stem[jnp.maximum(s, 0), start:end, :]
                        ref[spot + (slice(start, end), slice(None))] = jnp.where(s >= 0, value, 0.0).astype(BF16)
                    if stop > STEM_ROWS:
                        begin = max(start, STEM_ROWS)
                        ref[spot + (slice(begin, stop), slice(None))] = others[
                            e, begin - STEM_ROWS : stop - STEM_ROWS, :
                        ]
            return carry

        lax.fori_loop(0, SIZES["z"], line, 0)

    @pl.when(step == pl.num_programs(0) - 1)
    def _():
        *grads, bias, gprop = proprio_backward(
            ids_ref, prop_ref, w_ref, act_ref[...], slope_ref[...], grows_ref[...]
        )
        for row, part in other_blocks(acc, grads):
            row -= STEM_ROWS
            others[:, row : row + part.shape[1], :] = part
        first.sm[0, 0:16, :] = small_rows(acc)
        first.sm[0, 16:SMALL, :] = bias
        for layer, g, phase in SCATTER_END:
            if phase == 0 and g >= 0:
                gather_group(g)
            (first, second)[layer].run(((g, phase),))
        write_proprio(gprop + gprop1_ref[...], gprop_ref)
        second.close()
        first.close()


def backward_scatter(steps, scalars, ins, outs, g1, s1):
    lead = (4, 2, 2, 2, ROWS, D)
    samples = scalars[0].shape[0]
    smem = pl.BlockSpec(memory_space=pltpu.SMEM)
    any_spec = pl.BlockSpec(memory_space=pl.ANY)
    outs = outs + [((LAYERS, ROWS, D), F32, 0), ((LAYERS, SMALL, D), F32, 0)]
    per_layer = [
        pltpu.VMEM((4, 2, 2, ROWS, D), BF16),
        pltpu.VMEM((4, 2, 2, ROWS, D), BF16),
        pltpu.VMEM((4, 2, ROWS, D), BF16),
        pltpu.VMEM((4, ROWS, D), BF16),
        pltpu.VMEM((3, ROWS, D), BF16),
        pltpu.VMEM((4, SMALL, D), F32),
        pltpu.VMEM((3, SMALL, D), F32),
        pltpu.VMEM((4, SMALL, D), F32),
        pltpu.SemaphoreType.DMA((2 * len(BOUNDS), 4, 3)),
        pltpu.SemaphoreType.DMA((2 * len(BOUNDS), 4, 3)),
        pltpu.SemaphoreType.DMA((4, 3)),
        pltpu.SemaphoreType.DMA((4, 3)),
    ]
    return pl.pallas_call(
        backward_scatter_kernel,
        grid=(steps,),
        in_specs=[smem] * 3 + [blocked(a.shape, n) if n else whole(a.shape) for a, n in ins]
        + [any_spec, whole(s1.shape)],
        out_specs=[blocked(s, n) if n else whole(s) for s, _, n in outs],
        out_shape=[jax.ShapeDtypeStruct(s, d) for s, d, _ in outs],
        scratch_shapes=[pltpu.VMEM((STEPS * samples, D), F32)] + acc_shapes(samples)
        + [
            pltpu.VMEM((STEMS, ROWS - STEM_ROWS, D), BF16),
            pltpu.VMEM((4, 2, 2, ROWS, D), BF16),
            pltpu.SemaphoreType.DMA(()),
        ]
        + per_layer * LAYERS,
        compiler_params=pltpu.CompilerParams(
            dimension_semantics=("arbitrary",), vmem_limit_bytes=VMEM_LIMIT, collective_id=1,
            has_side_effects=True,
        ),
    )(*scalars, *[a for a, _ in ins], g1.reshape(lead), s1)


def unpack_kernel(mats, small, gtok_in, gfeat_in, gtok, gfeat, att, up, down, stem, q, pin, vec, mb, sb):
    gtok[...] = gtok_in[...]
    gfeat[...] = gfeat_in[...]
    pl.when(pl.program_id(0) == 0)(
        lambda: split_gradients(mats, small, att, up, down, stem, q, pin, vec, mb, sb)
    )


def split_gradients(mats, small, att, up, down, stem, q, pin, vec, mb, sb):
    for layer in range(LAYERS):
        for j, row in enumerate(MAT_ROWS):
            stem[layer, :, j * D : (j + 1) * D] = mats[layer, row : row + D, :]
        q[layer] = mats[layer, R_Q:R_WP, :]
        pin[layer] = mats[layer, R_PIN:R_ATT, :]
        att[layer] = mats[layer, R_ATT:R_UP, :]
        up[layer] = mats[layer, R_UP:R_DOWN, :]
        down[layer] = mats[layer, R_DOWN:ROWS, :]
        vec[layer] = small[layer, 0:8, :]
        for i in range(4):
            mb[layer : layer + 1, i * D : (i + 1) * D] = small[layer, 8 + i : 9 + i, :]
        sb[layer] = small[layer, 16:SMALL, :]


def unpack(mats, small, gtok, gfeat):
    outs = [
        (LAYERS, 16, D), (LAYERS, 16, D), (LAYERS, 16, D), (LAYERS, D, 4 * D), (LAYERS, SQ, D),
        (LAYERS, PROP, D), (LAYERS, 8, D), (LAYERS, FF), (LAYERS, 2 * STEMS, D),
    ]
    steps = 4
    moved_through = [blocked(a.shape, a.shape[0] // steps) for a in (gtok, gfeat)]
    return pl.pallas_call(
        unpack_kernel,
        grid=(steps,),
        out_shape=[jax.ShapeDtypeStruct(s, F32) for s in [gtok.shape, gfeat.shape] + outs],
        in_specs=[whole(mats.shape), whole(small.shape)] + moved_through,
        out_specs=moved_through + [whole(s) for s in outs],
    )(mats, small, gtok, gfeat)


def pack(attn, up, down, stem, queries, pin):
    gathered = [lax.all_gather(a, "fsdp", axis=1, tiled=True) for a in (attn, up, down, stem, queries, pin)]
    attn, up, down, stem, queries, pin = gathered
    stem = stem.reshape(LAYERS, STEMS, D, 4, D).transpose(0, 1, 3, 2, 4).reshape(LAYERS, STEMS, 4 * D, D)
    queries, *parts = [a.reshape(LAYERS, STEMS, -1, D) for a in (queries, pin, attn, up, down)]
    return jnp.concatenate([stem[:, :, : 3 * D], queries, stem[:, :, 3 * D :], *parts], 2)


def unpack_blocks(grad):
    stem = jnp.concatenate([grad[..., row : row + D, :] for row in MAT_ROWS], -1)
    return (
        grad[..., R_ATT:R_UP, :], grad[..., R_UP:R_DOWN, :], grad[..., R_DOWN:ROWS, :],
        stem, grad[..., R_Q:R_WP, :], grad[..., R_PIN:R_ATT, :],
    )


def body(n, tokens, features, proprio, embodiment, trunk_attn, feedforward_up_weight, mlp_down,
         stem_mats, stem_queries, prop_in, trunk_vectors, mlp_bias, stem_bias, cotangent):
    shards = (trunk_attn, feedforward_up_weight, mlp_down, stem_mats, stem_queries, prop_in)
    out, gtok, gfeat, gprop, mats, small = compute(
        tokens, features, proprio, embodiment, shards, trunk_vectors, mlp_bias, stem_bias,
        cotangent, None if n == 32 else pack(*shards),
    )
    if n == 32:
        return (out, gtok, gfeat, gprop, *mats, small.reshape(LAYERS, STEMS, 2, D))
    mats = [
        lax.psum_scatter(a.reshape(LAYERS, -1, a.shape[-1]), "fsdp", scatter_dimension=1, tiled=True)
        for a in unpack_blocks(mats.astype(F32))
    ]
    small = lax.psum(small, "fsdp")
    gvec = small[:, :8]
    gmb = small[:, 8:12].reshape(LAYERS, FF)
    gsb = small[:, 16:].reshape(LAYERS, STEMS, 2, D)
    return (out, gtok, gfeat, gprop, *mats, gvec, gmb, gsb)


def solution(mesh):
    n = mesh.shape["fsdp"]
    return jax.shard_map(
        functools.partial(body, n),
        mesh=mesh,
        in_specs=(
            P("fsdp"), P("fsdp"), P("fsdp"), P("fsdp"),
            P(None, "fsdp"), P(None, "fsdp"), P(None, "fsdp"), P(None, "fsdp"), P(None, "fsdp"),
            P(None, "fsdp"), P(), P(), P(), P("fsdp"),
        ),
        out_specs=(
            P("fsdp"), P("fsdp"), P("fsdp"), P("fsdp"),
            P(None, "fsdp"), P(None, "fsdp"), P(None, "fsdp"), P(None, "fsdp"), P(None, "fsdp"),
            P(None, "fsdp"), P(), P(), P(),
        ),
        check_vma=False,
    )
```

```python
import functools
import math

import jax
import jax.numpy as jnp
from jax import lax
from jax.experimental import pallas as pl
from jax.experimental.pallas import tpu as pltpu
from jax.sharding import PartitionSpec as P

D = 128
HEADS = 8
HD = 16
FF = 512
SQ = 16
FR = 49
CR = 112
PROP = 32
STEMS = 32
STEPS = 2
LAYERS = 2
TOK = 32
SB = 16

R_Q = 3 * D
R_WP = R_Q + SQ
R_PIN = R_WP + D
R_ATT = R_PIN + PROP
R_UP = R_ATT + 16
R_DOWN = R_UP + 16
ROWS = R_DOWN + 16
STEM_ROWS = R_WP
SMALL = 16 + 2 * STEMS

MAT_ROWS = (0, D, 2 * D, R_WP)

F32 = jnp.float32
BF16 = jnp.bfloat16
VMEM_LIMIT = 60 * 1024 * 1024


def dot(a, b):
    return lax.dot_general(a, b, (((1,), (0,)), ((), ())), preferred_element_type=F32)


def dot_nt(a, b):
    return lax.dot_general(a, b, (((1,), (1,)), ((), ())), preferred_element_type=F32)


def dot_tn(a, b):
    return lax.dot_general(a, b, (((0,), (0,)), ((), ())), preferred_element_type=F32)


def gelu_parts(x):
    cdf = 0.5 + 0.5 * lax.erf(x * math.sqrt(0.5))
    slope = cdf + x * (jnp.exp(-0.5 * x * x) * (1.0 / math.sqrt(2.0 * math.pi)))
    return x * cdf, slope


def norm_parts(x):
    centred = x - jnp.mean(x, -1, keepdims=True)
    inverse = lax.rsqrt(jnp.mean(centred * centred, -1, keepdims=True) + 1e-05)
    return centred * inverse, inverse


def norm_back(grad, gain, hat, inverse):
    g = grad * gain
    return inverse * (
        g - jnp.mean(g, -1, keepdims=True) - hat * jnp.mean(g * hat, -1, keepdims=True)
    )


def head_mask(rows, value):
    row = lax.broadcasted_iota(jnp.int32, (HEADS * rows, D), 0) // rows
    lane = lax.broadcasted_iota(jnp.int32, (HEADS * rows, D), 1) // HD
    return jnp.where(row == lane, value, 0.0).astype(BF16)


def expand(rows, mask):
    return jnp.concatenate([rows] * HEADS, 0) * mask


def contract(wide, rows):
    lane = lax.broadcasted_iota(jnp.int32, (rows, D), 1) // HD
    out = wide[:rows]
    for head in range(1, HEADS):
        out = jnp.where(lane == head, wide[head * rows : (head + 1) * rows], out)
    return out


def fold(x):
    return jnp.sum(x.reshape(x.shape[0] // 8, 8, x.shape[1]), 0)


def slot(w_ref, e, start, stop):
    if len(w_ref.shape) == 3:
        return w_ref[e, start:stop, :]
    return w_ref[e // 8, (e // 4) % 2, (e // 2) % 2, e % 2, start:stop, :]


def all_slots(w_ref, start, stop):
    index = (slice(None),) * (len(w_ref.shape) - 2)
    return w_ref[index + (slice(start, stop), slice(None))].reshape(STEMS * (stop - start), D)


def trunk_weights(w_ref):
    attn = all_slots(w_ref, R_ATT, R_UP)
    up = all_slots(w_ref, R_UP, R_DOWN)
    down = all_slots(w_ref, R_DOWN, ROWS)
    wqkv = jnp.concatenate([attn[:D], attn[D : 2 * D], attn[2 * D : 3 * D]], 1)
    return wqkv, attn[3 * D :], up, down


def stem_kv_weight(w_ref, e):
    return jnp.concatenate([slot(w_ref, e, 0, D), slot(w_ref, e, D, 2 * D)], 1)


def step_reduce(x, op):
    x = x.reshape(x.shape[0] // 8, 8, x.shape[1])
    out = x[0]
    for i in range(1, x.shape[0]):
        out = op(out, x[i])
    out = op(out, pltpu.roll(out, 4, 0))
    return op(out, pltpu.roll(out, 2, 0))


def step_apply(x, y, op):
    return op(x.reshape(x.shape[0] // 8, 8, x.shape[1]), y[None]).reshape(x.shape)


def step_masks():
    odd = lax.broadcasted_iota(jnp.int32, (CR, D), 0) % 2
    return (odd == 0).astype(BF16), odd.astype(BF16)


def split_steps(p, masks):
    return jnp.concatenate([p * masks[0], p * masks[1]], 1)


def softmax_rows(score):
    top = jnp.max(score, 0, keepdims=True)
    weight = jnp.exp(score - top)
    return weight * (1.0 / jnp.sum(weight, 0, keepdims=True))


def stem_ids(emb_ref, rows, down=False):
    samples = emb_ref.shape[1]
    row = lax.broadcasted_iota(jnp.int32, (rows, samples), 0) // STEPS
    pick = (row == lax.broadcasted_iota(jnp.int32, (rows, samples), 1)).astype(BF16)
    stems = jnp.broadcast_to(emb_ref[...].astype(F32).astype(BF16), (D, samples))
    return dot_nt(stems, pick) if down else dot_nt(pick, stems)


def spread(values, ids):
    values = values.astype(F32)
    return jnp.concatenate([jnp.where(ids == e, values, 0.0).astype(BF16) for e in range(STEMS)], 1)


def sample_rows(samples):
    shape = (samples * STEPS, samples * STEPS)
    row = lax.broadcasted_iota(jnp.int32, shape, 0)
    column = (row % STEPS) * samples + row // STEPS
    return (lax.broadcasted_iota(jnp.int32, shape, 1) == column).astype(BF16)


def spread_down(values, ids):
    values = values.astype(F32)
    return jnp.concatenate([jnp.where(ids == e, values, 0.0).astype(BF16) for e in range(STEMS)], 0)


def spread_proprio(prop_ref, ids, down=False):
    both = jnp.concatenate([prop_ref[t] for t in range(STEPS)], 1)
    group = D // PROP
    tiled = jnp.concatenate([both] * group, 0)
    place_ = sample_rows(prop_ref.shape[2])
    rows = dot_nt(tiled, place_) if down else dot_nt(place_, tiled)
    entry = (lax.broadcasted_iota(jnp.int32, rows.shape, 0 if down else 1) // PROP).astype(F32)
    return jnp.concatenate(
        [jnp.where(ids == entry + float(group * b), rows, 0.0).astype(BF16) for b in range(STEMS // group)],
        0 if down else 1,
    )


def bias_picks(ids):
    lane = lax.broadcasted_iota(jnp.int32, (ids.shape[0], 2 * STEMS), 1).astype(F32)
    twice = 2.0 * ids[:, : 2 * STEMS]
    return (lane == twice).astype(BF16), (lane == twice + 1.0).astype(BF16)


def proprio_forward(emb_ref, prop_ref, w_ref, biases):
    ids = stem_ids(emb_ref, STEPS * emb_ref.shape[1])
    first, second = bias_picks(ids)
    pre = dot(spread_proprio(prop_ref, ids), all_slots(w_ref, R_PIN, R_ATT)) + dot(first, biases)
    act, slope = gelu_parts(pre)
    act = act.astype(BF16)
    return act, slope, dot(spread(act, ids), all_slots(w_ref, R_WP, R_PIN)) + dot(second, biases)


def proprio_backward(emb_ref, prop_ref, w_ref, act, slope, grad_rows):
    ids = stem_ids(emb_ref, STEPS * emb_ref.shape[1])
    first, second = bias_picks(ids)
    low = grad_rows.astype(BF16)
    wp = jnp.concatenate([slot(w_ref, e, R_WP, R_PIN) for e in range(STEMS)], 1)
    pin = jnp.concatenate([slot(w_ref, e, R_PIN, R_ATT) for e in range(STEMS)], 1)
    grad_pre = (dot_nt(spread(low, ids), wp) * slope).astype(BF16)
    down = stem_ids(emb_ref, STEPS * emb_ref.shape[1], True)
    return (
        dot(spread_down(act.astype(F32).T, down), low), dot(spread_proprio(prop_ref, down, True), grad_pre),
        dot_tn(first, grad_pre) + dot_tn(second, low), dot_nt(spread(grad_pre, ids), pin),
    )


def forward_block(es, hidden, feat_ref, prows, w_ref, vec, mb, tick=None):
    kept = {}
    row8 = lax.broadcasted_iota(jnp.int32, (8, D), 0)
    contexts = []
    for j in range(SB):
        rows = feat_ref[j * STEPS * FR : (j + 1) * STEPS * FR, :]
        last = jnp.concatenate([rows[96:98], jnp.zeros((14, D), BF16)], 0).astype(F32)[:8]
        k = j // 4 * 8
        mine = pltpu.roll(prows[k : k + 8], (2 - 2 * (j % 4)) % 8, 0)
        tail = jnp.where(row8 < 2, last, jnp.where(row8 < 4, mine, 0.0))
        tail = jnp.concatenate([tail, jnp.zeros((8, D), F32)], 0).astype(BF16)
        contexts.append(jnp.concatenate([rows[:96], tail], 0))
    kept["ctx"] = contexts
    kvs = [dot(contexts[j], stem_kv_weight(w_ref, e)).astype(BF16) for j, e in enumerate(es)]
    kept["kv"] = kvs
    mask16 = head_mask(SQ, 0.25)
    scores = [
        dot_nt(kvs[j][:, :D], expand(slot(w_ref, e, R_Q, R_WP), mask16)) for j, e in enumerate(es)
    ]
    valid = lax.broadcasted_iota(jnp.int32, (104, D), 0) < STEPS * (FR + 1)
    pad = jnp.zeros((8, D), F32)
    probs = []
    for j in range(SB):
        s = jnp.where(valid, scores[j][:104], -1e30)
        weight = jnp.exp(step_apply(s, step_reduce(s, jnp.maximum), jnp.subtract))
        scale = 1.0 / step_reduce(weight, jnp.add)
        probs.append(jnp.concatenate([step_apply(weight, scale, jnp.multiply), pad], 0))
    kept["prob"] = probs
    masks = step_masks()
    mixes = []
    for j in range(SB):
        wide = dot_tn(split_steps(probs[j].astype(BF16), masks), kvs[j][:, D:])
        mixes += [contract(wide[t * D : (t + 1) * D], SQ).astype(BF16) for t in range(STEPS)]
    mix = jnp.concatenate(mixes, 0)
    kept["mix"] = mix
    if tick is not None:
        tick()
    outs = [
        dot(mix[j * TOK : (j + 1) * TOK], slot(w_ref, e, 2 * D, 3 * D)) for j, e in enumerate(es)
    ]
    first = hidden + jnp.concatenate(outs, 0)
    kept["first"] = first
    wqkv, wout, up, down = trunk_weights(w_ref)
    normed = (norm_parts(first)[0] * vec[0:1] + vec[1:2]).astype(BF16)
    bias = jnp.concatenate([vec[2:3], jnp.zeros((1, D), F32), vec[3:4]], 1)
    qkv = (dot(normed, wqkv) + bias).astype(BF16)
    kept["qkv"] = qkv
    mask32 = head_mask(TOK, 0.25)
    rows = [qkv[j * TOK : (j + 1) * TOK] for j in range(SB)]
    scores = [dot_nt(rows[j][:, D : 2 * D], expand(rows[j][:, :D], mask32)) for j in range(SB)]
    sprobs = [softmax_rows(s) for s in scores]
    smixes = [
        contract(dot_tn(sprobs[j].astype(BF16), rows[j][:, 2 * D :]), TOK).astype(BF16)
        for j in range(SB)
    ]
    kept["sprob"] = sprobs
    smix = jnp.concatenate(smixes, 0)
    kept["smix"] = smix
    second = first + (dot(smix, wout) + vec[4:5])
    kept["second"] = second
    mlp_in = (norm_parts(second)[0] * vec[5:6] + vec[6:7]).astype(BF16)
    act, slope = gelu_parts(dot_nt(mlp_in, up) + mb)
    act = act.astype(BF16)
    kept["act"], kept["slope"] = act, slope
    return second + (dot(act, down) + vec[7:8]), kept


def backward_block(es, grad, kept, w_ref, vec, acc, tick=None):
    wqkv, wout, up, down = trunk_weights(w_ref)
    out_low = grad.astype(BF16)
    acc["vec"][7] += fold(out_low.astype(F32))
    acc["down"][...] += dot_tn(out_low, kept["act"])
    grad_act = dot_nt(out_low, down)
    grad_pre = (grad_act * kept["slope"].astype(F32)).astype(BF16)
    acc["mb"][...] += fold(grad_pre.astype(F32))
    hat, inverse = norm_parts(kept["second"])
    mlp_in = (hat * vec[5:6] + vec[6:7]).astype(BF16)
    acc["up"][...] += dot_tn(mlp_in, grad_pre)
    grad_in = dot(grad_pre, up)
    acc["vec"][5] += fold(grad_in * hat)
    acc["vec"][6] += fold(grad_in)
    grad_second = grad + norm_back(grad_in, vec[5:6], hat, inverse)
    branch = grad_second.astype(BF16)
    acc["vec"][4] += fold(branch.astype(F32))
    acc["wout"][...] += dot_tn(kept["smix"], branch)
    grad_mix = dot_nt(branch, wout).astype(BF16)
    mask32 = head_mask(TOK, 0.25)
    mask32_one = head_mask(TOK, 1.0)
    rows = [kept["qkv"][j * TOK : (j + 1) * TOK] for j in range(SB)]
    wides = [expand(grad_mix[j * TOK : (j + 1) * TOK], mask32_one) for j in range(SB)]
    grad_ps = [dot_nt(rows[j][:, 2 * D :], wides[j]) for j in range(SB)]
    grads_v = [dot(kept["sprob"][j].astype(BF16), wides[j]) for j in range(SB)]
    gss = []
    for j in range(SB):
        p = kept["sprob"][j].astype(F32)
        gss.append((p * (grad_ps[j] - jnp.sum(grad_ps[j] * p, 0, keepdims=True))).astype(BF16))
    grads_q = [contract(dot_tn(gss[j], rows[j][:, D : 2 * D]), TOK) * 0.25 for j in range(SB)]
    grads_k = [dot(gss[j], expand(rows[j][:, :D], mask32)) for j in range(SB)]
    grad_qkv = jnp.concatenate(
        [jnp.concatenate(g, 0).astype(BF16) for g in (grads_q, grads_k, grads_v)], 1
    )
    acc["vec"][2] += fold(grad_qkv[:, :D].astype(F32))
    acc["vec"][3] += fold(grad_qkv[:, 2 * D :].astype(F32))
    hat, inverse = norm_parts(kept["first"])
    normed = (hat * vec[0:1] + vec[1:2]).astype(BF16)
    acc["wqkv"][...] += dot_tn(normed, grad_qkv)
    grad_normed = dot_nt(grad_qkv, wqkv)
    acc["vec"][0] += fold(grad_normed * hat)
    acc["vec"][1] += fold(grad_normed)
    grad_first = grad_second + norm_back(grad_normed, vec[0:1], hat, inverse)
    stem_grad = grad_first.astype(BF16)
    mask16 = head_mask(SQ, 0.25)
    mask16_one = head_mask(SQ, 1.0)
    row8 = lax.broadcasted_iota(jnp.int32, (8, D), 0)
    if tick is not None:
        tick()
    gs_in = [stem_grad[j * TOK : (j + 1) * TOK] for j in range(SB)]
    gmixes = [dot_nt(gs_in[j], slot(w_ref, e, 2 * D, 3 * D)).astype(BF16) for j, e in enumerate(es)]
    grad_wo = [dot_tn(kept["mix"][j * TOK : (j + 1) * TOK], gs_in[j]) for j in range(SB)]
    kvs = [kept["kv"][j] for j in range(SB)]
    probs = [kept["prob"][j] for j in range(SB)]
    wides = [
        jnp.concatenate(
            [expand(gmixes[j][t * SQ : (t + 1) * SQ], mask16_one) for t in range(STEPS)], 0
        )
        for j in range(SB)
    ]
    grad_ps = [dot_nt(kvs[j][:, D:], wides[j]) for j in range(SB)]
    masks = step_masks()
    gvs = [dot(split_steps(probs[j].astype(BF16), masks), wides[j]) for j in range(SB)]
    even = lax.broadcasted_iota(jnp.int32, (104, D), 0) % 2 == 0
    pad = jnp.zeros((8, D), F32)
    gss = []
    for j in range(SB):
        p = probs[j][:104].astype(F32)
        gp = jnp.where(even, grad_ps[j][:104, :D], grad_ps[j][:104, D:])
        gs = p * step_apply(gp, step_reduce(gp * p, jnp.add), jnp.subtract)
        gss.append(jnp.concatenate([gs, pad], 0).astype(BF16))
    gks = [dot(gss[j], expand(slot(w_ref, e, R_Q, R_WP), mask16)) for j, e in enumerate(es)]
    gkvs = [
        jnp.concatenate([gks[j], gvs[j]], 1).astype(BF16) for j in range(SB)
    ]
    grad_contexts = [
        dot_nt(gkvs[j], stem_kv_weight(w_ref, e)).astype(BF16) for j, e in enumerate(es)
    ]
    grad_prows = []
    for k in range(0, SB, 4):
        rows = jnp.zeros((8, D), F32)
        for j in range(k, k + 4):
            tail = pltpu.roll(grad_contexts[j][96:112].astype(F32)[:8], (2 * (j % 4) - 2) % 8, 0)
            rows = jnp.where(row8 // 2 == j % 4, tail, rows)
        grad_prows.append(rows)
    grad_q = [contract(dot_tn(gss[j], kvs[j][:, :D]), SQ) * 0.25 for j in range(SB)]
    grad_wkv = [dot_tn(kept["ctx"][j], gkvs[j]) for j in range(SB)]
    for j, e in enumerate(es):
        acc["add"](
            j, e,
            ((0, grad_wkv[j][:, :D]), (D, grad_wkv[j][:, D:]), (2 * D, grad_wo[j]), (R_Q, grad_q[j])),
        )
    return grad_first, grad_contexts, jnp.concatenate(grad_prows, 0)


ACC = ("stem", "wqkv", "wout", "up", "down", "vec", "mb")


def acc_shapes(entries):
    return [
        pltpu.VMEM((entries, STEM_ROWS, D), F32),
        pltpu.VMEM((D, 3 * D), F32),
        pltpu.VMEM((D, D), F32),
        pltpu.VMEM((D, FF), F32),
        pltpu.VMEM((D, FF), F32),
        pltpu.VMEM((8, 8, D), F32),
        pltpu.VMEM((8, FF), F32),
    ]


def clear(acc):
    for ref in acc.values():
        ref[...] = jnp.zeros(ref.shape, ref.dtype)


def add_in_place(acc):
    def add(j, e, pieces):
        for row, value in pieces:
            acc["stem"][e, row : row + value.shape[0], :] += value

    return {**acc, "add": add}


def trunk_blocks(acc):
    wqkv = acc["wqkv"][...]
    attn = [wqkv[:, :D], wqkv[:, D : 2 * D], wqkv[:, 2 * D :], acc["wout"][...]]
    return (
        jnp.concatenate(attn, 0).astype(BF16).reshape(STEMS, 16, D),
        acc["up"][...].T.astype(BF16).reshape(STEMS, 16, D),
        acc["down"][...].T.astype(BF16).reshape(STEMS, 16, D),
    )


def small_rows(acc):
    mb = jnp.sum(acc["mb"][...], 0, keepdims=True)
    return jnp.concatenate(
        [jnp.sum(acc["vec"][...], 1)] + [mb[:, i * D : (i + 1) * D] for i in range(4)]
        + [jnp.zeros((4, D), F32)], 0
    )


def other_blocks(acc, grads):
    grad_wp, grad_pin = grads
    return (
        (R_WP, grad_wp.astype(BF16).reshape(STEMS, D, D)),
        (R_PIN, grad_pin.astype(BF16).reshape(STEMS, PROP, D)),
    ) + tuple((R_ATT + 16 * i, part) for i, part in enumerate(trunk_blocks(acc)))


def finish(acc, grads, bias, grad_ref, small_ref):
    def stem_out(e, carry):
        grad_ref[e, 0:STEM_ROWS, :] = acc["stem"][e].astype(grad_ref.dtype)
        return carry

    lax.fori_loop(0, STEMS, stem_out, 0)
    for start, part in other_blocks(acc, grads):
        grad_ref[:, start : start + part.shape[1], :] = part
    small_ref[0:16, :] = small_rows(acc)
    small_ref[16:SMALL, :] = bias


SAVED = ("ctx", "kv", "prob", "mix", "first", "qkv", "sprob", "smix", "second", "act", "slope")
PER_SAMPLE = ("ctx", "kv", "prob", "sprob")


def saved_shapes(samples):
    rows = samples * TOK
    return dict(
        ctx=((samples, CR, D), BF16),
        kv=((samples, CR, 2 * D), BF16),
        prob=((samples, CR, D), BF16),
        mix=((rows, D), BF16),
        first=((rows, D), F32),
        qkv=((rows, 3 * D), BF16),
        sprob=((samples, TOK, HEADS * TOK), BF16),
        smix=((rows, D), BF16),
        second=((rows, D), F32),
        act=((rows, FF), BF16),
        slope=((rows, FF), BF16),
    )


def layer_inputs(layer, vec_ref, mb_ref):
    return vec_ref[layer].astype(F32), mb_ref[layer : layer + 1, :].astype(F32)


def start_forward(layer, emb_ref, prop_ref, w_ref, sb_ref, act_ref, slope_ref, rows_ref):
    act_ref[...], slope_ref[...], rows_ref[...] = proprio_forward(emb_ref, prop_ref, w_ref, sb_ref[layer])


def block_rows(step):
    return pl.ds(pl.multiple_of(step * SB * STEPS, SB * STEPS), SB * STEPS)


def save(kept, saved):
    for name, ref in zip(SAVED, saved):
        if name in PER_SAMPLE:
            for j in range(SB):
                ref[j] = kept[name][j].astype(ref.dtype)
        else:
            ref[...] = kept[name].astype(ref.dtype)


def load(saved):
    return {
        name: [ref[j] for j in range(SB)] if name in PER_SAMPLE else ref[...]
        for name, ref in zip(SAVED, saved)
    }


def forward_kernel(
    emb_ref, ids_ref, tok_ref, feat_ref, prop_ref, w_ref, vec_ref, mb_ref, sb_ref, out_ref, act_ref, slope_ref, *rest
):
    saved, rows_ref = rest[:-1], rest[-1]
    step = pl.program_id(0)
    pl.when(step == 0)(
        lambda: start_forward(0, ids_ref, prop_ref, w_ref, sb_ref, act_ref, slope_ref, rows_ref)
    )
    es = [emb_ref[step * SB + j] for j in range(SB)]
    out, kept = forward_block(
        es, tok_ref[...].astype(F32), feat_ref, rows_ref[block_rows(step), :], w_ref,
        *layer_inputs(0, vec_ref, mb_ref)
    )
    out_ref[...] = out
    save(kept, saved)


def link_samples(emb_ref, before_ref, last_ref):
    def unset(e, carry):
        last_ref[e] = -1
        return carry

    def link(s, carry):
        e = emb_ref[s]
        before_ref[s] = last_ref[e]
        last_ref[e] = s
        return carry

    lax.fori_loop(0, STEMS, unset, 0)
    lax.fori_loop(0, before_ref.shape[0], link, 0)


def middle_kernel(
    emb_ref, ids_ref, hid_ref, feat_ref, prop_ref, w_ref, vec_ref, mb_ref, sb_ref, cot_ref,
    out_ref, ghid_ref, gfeat_ref, gprop_ref, gw_ref, gsmall_ref, before_ref, last_ref,
    act_ref, slope_ref, rows_ref, grows_ref, *accs
):
    step = pl.program_id(0)
    acc = dict(zip(ACC, accs))

    @pl.when(step == 0)
    def _():
        clear(acc)
        link_samples(emb_ref, before_ref, last_ref)
        start_forward(1, ids_ref, prop_ref, w_ref, sb_ref, act_ref, slope_ref, rows_ref)

    es = [emb_ref[step * SB + j] for j in range(SB)]
    vec, mb = layer_inputs(1, vec_ref, mb_ref)
    out, kept = forward_block(
        es, hid_ref[...], feat_ref, rows_ref[block_rows(step), :], w_ref, vec, mb
    )
    out_ref[...] = out.astype(BF16)
    ghid, gctx, grows = backward_block(
        es, cot_ref[...].astype(F32), kept, w_ref, vec, add_in_place(acc)
    )
    ghid_ref[...] = ghid
    grows_ref[block_rows(step), :] = grows
    for j in range(SB):
        gfeat_ref[j] = gctx[j]

    @pl.when(step == pl.num_programs(0) - 1)
    def _():
        *grads, bias, gprop_ref[...] = proprio_backward(
            ids_ref, prop_ref, w_ref, act_ref[...], slope_ref[...], grows_ref[...]
        )
        finish(acc, grads, bias, gw_ref, gsmall_ref)


def write_features(gctx, gfeat1_ref, gfeat_ref):
    for j in range(0, SB, 4):
        totals = [gctx[i].astype(F32) + gfeat1_ref[i].astype(F32) for i in range(j, j + 4)]
        gfeat_ref[j * STEPS * FR : (j + 4) * STEPS * FR, :] = jnp.concatenate(
            [total[: STEPS * FR] for total in totals], 0
        )


def write_proprio(rows, gprop_ref):
    samples = gprop_ref.shape[2]
    place_ = sample_rows(samples)
    high = rows.astype(BF16)
    rest = rows - high.astype(F32)
    middle = rest.astype(BF16)
    low = (rest - middle.astype(F32)).astype(BF16)
    out = dot_tn(high, place_) + (dot_tn(middle, place_) + dot_tn(low, place_))
    for t in range(STEPS):
        gprop_ref[t] = out[:, t * samples : (t + 1) * samples]


def backward_kernel(
    emb_ref, ids_ref, grad_ref, prop_ref, w_ref, vec_ref, gfeat1_ref, gprop1_ref, act_ref, slope_ref, *rest
):
    n = len(SAVED)
    saved = rest[:n]
    gtok_ref, gfeat_ref, gprop_ref, gw_ref, gsmall_ref, grows_ref = rest[n : n + 6]
    acc = dict(zip(ACC, rest[n + 6 :]))
    step = pl.program_id(0)
    pl.when(step == 0)(lambda: clear(acc))
    es = [emb_ref[step * SB + j] for j in range(SB)]
    vec = vec_ref[0].astype(F32)
    ghid, gctx, grows = backward_block(es, grad_ref[...], load(saved), w_ref, vec, add_in_place(acc))
    gtok_ref[...] = ghid
    grows_ref[block_rows(step), :] = grows
    write_features(gctx, gfeat1_ref, gfeat_ref)

    @pl.when(step == pl.num_programs(0) - 1)
    def _():
        *grads, bias, gprop = proprio_backward(
            ids_ref, prop_ref, w_ref, act_ref[...], slope_ref[...], grows_ref[...]
        )
        finish(acc, grads, bias, gw_ref, gsmall_ref)
        write_proprio(gprop + gprop1_ref[...], gprop_ref)


def blocked(shape, per_step):
    block = (per_step,) + tuple(shape[1:])
    zeros = (0,) * (len(shape) - 1)
    return pl.BlockSpec(block, lambda i, *_: (i,) + zeros)


def whole(shape):
    zeros = (0,) * len(shape)
    return pl.BlockSpec(tuple(shape), lambda i, *_: zeros, pipeline_mode=pl.Buffered(1))


def call(kernel, steps, emb, ins, outs, scratch):
    return pl.pallas_call(
        kernel,
        grid_spec=pltpu.PrefetchScalarGridSpec(
            num_scalar_prefetch=1,
            grid=(steps,),
            in_specs=[blocked(a.shape, n) if n else whole(a.shape) for a, n in ins],
            out_specs=[
                pl.BlockSpec(memory_space=pltpu.SMEM) if n is None else blocked(s, n) if n else whole(s)
                for s, _, n in outs
            ],
            scratch_shapes=scratch,
        ),
        out_shape=[jax.ShapeDtypeStruct(s, d) for s, d, _ in outs],
        compiler_params=pltpu.CompilerParams(
            dimension_semantics=("arbitrary",), vmem_limit_bytes=VMEM_LIMIT
        ),
    )(emb, *[a for a, _ in ins])


def compute(tokens, features, proprio, emb, shards, vecs, mbs, sbs, cot, weights=None):
    samples = emb.shape[0]
    steps = samples // SB
    rows = samples * TOK
    rb = SB * TOK
    tok = tokens.reshape(rows, D)
    feat = jnp.swapaxes(features, 1, 2).reshape(samples * FR * STEPS, D)
    prop = proprio.transpose(1, 2, 0)
    ids = emb.reshape(1, samples)
    sbs = sbs.reshape(LAYERS, 2 * STEMS, D)
    fb = SB * FR * STEPS
    prows = (STEPS * samples, D)
    shapes = saved_shapes(samples)
    per = lambda s: s[0] // steps
    forward_ins = [(ids, 0), (tok, rb), (feat, fb), (prop, 0), (vecs, 0), (mbs, 0), (sbs, 0)]
    forward_outs = [((rows, D), F32, rb), (prows, BF16, 0), (prows, F32, 0)] + [
        (shapes[n][0], shapes[n][1], per(shapes[n][0])) for n in SAVED
    ]
    if weights is None:
        hidden, act, slope, w0, w1, *saved = gather_forward(steps, emb, forward_ins, forward_outs, shards)
    else:
        w0, w1 = weights
        forward_ins = forward_ins[:4] + [(w0, 0)] + forward_ins[4:]
        hidden, act, slope, *saved = call(
            forward_kernel, steps, emb, forward_ins, forward_outs, [pltpu.VMEM(prows, F32)]
        )
    grad_outs = [((STEMS, ROWS, D), BF16, 0), ((SMALL, D), F32, 0)]
    out, ghid, gfeat1, gprop1, *grads1, before, last = call(
        middle_kernel, steps, emb,
        [(ids, 0), (hidden, rb), (feat, fb), (prop, 0), (w1, 0), (vecs, 0), (mbs, 0), (sbs, 0),
         (cot.reshape(rows, D), rb)],
        [((rows, D), BF16, rb), ((rows, D), F32, rb), ((samples, CR, D), BF16, SB),
         ((STEPS * samples, PROP), F32, 0)] + grad_outs
        + [((samples,), jnp.int32, None), ((STEMS,), jnp.int32, None)],
        [pltpu.VMEM(prows, BF16)] + [pltpu.VMEM(prows, F32)] * 3 + acc_shapes(STEMS),
    )
    backward_ins = (
        [(ids, 0), (ghid, rb), (prop, 0), (w0, 0), (vecs, 0), (gfeat1, SB), (gprop1, 0), (act, 0), (slope, 0)]
        + [(a, per(a.shape)) for a in saved]
    )
    backward_outs = [
        ((rows, D), F32, rb), ((samples * FR * STEPS, D), F32, fb), ((STEPS, PROP, samples), F32, 0)
    ]
    if weights is None:
        gtok, gfeat, gprop, mats, small = backward_scatter(
            steps, (emb, before, last), backward_ins, backward_outs, *grads1
        )
        gtok, gfeat, *mats, small = unpack(mats, small, gtok, gfeat)
    else:
        gtok, gfeat, gprop, *grads0 = call(
            backward_kernel, steps, emb, backward_ins, backward_outs + grad_outs,
            [pltpu.VMEM(prows, F32)] + acc_shapes(STEMS),
        )
        mats, small = (jnp.stack(pair) for pair in zip(grads0, grads1))
    gfeat = jnp.swapaxes(gfeat.reshape(samples, FR, STEPS, D), 1, 2)
    return (
        out.reshape(tokens.shape), gtok.reshape(tokens.shape), gfeat, gprop.transpose(2, 0, 1),
        mats, small
    )


def chunks_of(layer, bounds):
    groups = []
    for start, stop in zip(bounds[:-1], bounds[1:]):
        half = (stop - start) // 32 * 16
        groups.append(
            [(layer, start, half, ("z", "x", "y")), (layer, start + half, stop - start - half, ("z", "y", "x"))]
        )
    return groups


SIZES = {"z": 4, "y": 2, "x": 2, "c": 2}
AXES = ("z", "y", "x", "c")
MESH = pl.DeviceIdType.MESH


def place():
    me = lax.axis_index("fsdp")
    return {"z": me // 8, "y": (me // 4) % 2, "x": (me // 2) % 2, "c": me % 2}


def number(at):
    return ((at["z"] * 2 + at["y"]) * 2 + at["x"]) * 2 + at["c"]


def moved(at, axis, by):
    out = dict(at)
    out[axis] = (at[axis] + by) % SIZES[axis]
    return out


def greet(at):
    barrier = pltpu.get_barrier_semaphore()
    count = 0
    for axis in AXES:
        for by in range(1, SIZES[axis]):
            pl.semaphore_signal(
                barrier, inc=1, device_id=(number(moved(at, axis, by)),), device_id_type=MESH
            )
            count += 1
    pl.semaphore_wait(barrier, count)


def block(ref, at, done, row, count):
    index = tuple(pl.ds(0, SIZES[a]) if a in done else pl.ds(at[a], 1) for a in AXES)
    return ref.at[index + (pl.ds(row, count), slice(None))]


class Gather:
    def __init__(self, at, outs, groups, send_sem, recv_sem):
        self.at, self.outs, self.groups = at, outs, groups
        self.send_sem, self.recv_sem = send_sem, recv_sem

    def copies(self, g, phase, arriving):
        for i, (layer, row, count, order) in enumerate(self.groups[g]):
            order = order + ("c",)
            axis, done = order[phase], order[:phase]
            for by in range(1, SIZES[axis]):
                whose = moved(self.at, axis, -by) if arriving else self.at
                ref = block(self.outs[layer], whose, done, row, count)
                sem = (2 * g + i, AXES.index(axis), by - 1)
                yield pltpu.make_async_remote_copy(
                    ref, ref, self.send_sem.at[sem], self.recv_sem.at[sem],
                    device_id=(number(moved(self.at, axis, by)),), device_id_type=MESH,
                )

    def start(self, g, phase):
        for copy in self.copies(g, phase, False):
            copy.start()

    def land(self, g, phase):
        for copy in self.copies(g, phase, True):
            copy.wait_recv()

    def run(self, moves):
        for g, phase in moves:
            if phase > 0:
                self.land(g, phase - 1)
            if phase < 4:
                self.start(g, phase)

    def close(self):
        for g in range(len(self.groups)):
            for phase in range(4):
                for copy in self.copies(g, phase, False):
                    copy.wait_send()


BOUNDS = (0, 160, 320, 480, ROWS)
HALVES = (0, 320, ROWS)
THIRDS = (0, 256, 448, ROWS)
GATHER_GROUPS = chunks_of(0, BOUNDS) + chunks_of(1, THIRDS)
GATHER_FIRST = (
    (0, 0), (1, 0), (0, 1), (2, 0), (1, 1), (0, 2), (3, 0), (2, 1), (1, 2), (0, 3), (4, 0), (3, 1), (2, 2),
    (5, 0), (1, 3), (0, 4), (3, 2), (2, 3), (1, 4), (6, 0), (4, 1), (3, 3), (2, 4), (5, 1), (3, 4),
)
GATHER_LATER = ((), ((4, 2), (6, 1)), (), ((5, 2),), ((6, 2),), ((4, 3),), (), ((5, 3),))
GATHER_END = ((6, 3), (4, 4), (5, 4), (6, 4))


def place_own(at, shards, outs, local_sem):
    att, up, down, stem, q, pin = shards
    copies = []
    for layer in range(LAYERS):
        own = outs[layer].at[at["z"], at["y"], at["x"], at["c"]]
        pieces = [
            (stem.at[layer, :, pl.ds(j * D, D)], row, D) for j, row in enumerate(MAT_ROWS)
        ] + [
            (q.at[layer], R_Q, SQ), (pin.at[layer], R_PIN, PROP), (att.at[layer], R_ATT, 16),
            (up.at[layer], R_UP, 16), (down.at[layer], R_DOWN, 16),
        ]
        for i, (piece, row, count) in enumerate(pieces):
            copies.append(
                pltpu.make_async_copy(piece, own.at[pl.ds(row, count), :], local_sem.at[layer, i])
            )
    return copies


def gather_forward_kernel(emb_ref, ids_ref, tok_ref, feat_ref, prop_ref, vec_ref, mb_ref, sb_ref, *rest):
    shards, (out_ref, act_ref, slope_ref, g0, g1), rest = rest[:6], rest[6:11], rest[11:]
    saved, (rows_ref, w_ref, local_sem, send_sem, recv_sem, keep_sem) = rest[:-6], rest[-6:]
    step = pl.program_id(0)
    at = place()
    move = Gather(at, (w_ref, g1), GATHER_GROUPS, send_sem, recv_sem)
    keep = pltpu.make_async_copy(w_ref, g0, keep_sem)

    @pl.when(step == 0)
    def _():
        local = place_own(at, shards, (w_ref, g1), local_sem)
        for copy in local:
            copy.start()
        greet(at)
        for copy in local:
            copy.wait()
        move.run(GATHER_FIRST)
        keep.start()
        start_forward(0, ids_ref, prop_ref, w_ref, sb_ref, act_ref, slope_ref, rows_ref)

    def moves_at(half):
        for i in range(len(GATHER_LATER) // 2):
            pl.when(step == i)(functools.partial(move.run, GATHER_LATER[2 * i + half]))

    moves_at(0)
    es = [emb_ref[step * SB + j] for j in range(SB)]
    out, kept = forward_block(
        es, tok_ref[...].astype(F32), feat_ref, rows_ref[block_rows(step), :], w_ref,
        *layer_inputs(0, vec_ref, mb_ref), tick=lambda: moves_at(1)
    )
    out_ref[...] = out
    save(kept, saved)

    @pl.when(step == pl.num_programs(0) - 1)
    def _():
        move.run(GATHER_END)
        keep.wait()
        move.close()


def gather_forward(steps, emb, ins, outs, shards):
    assert 2 * steps == len(GATHER_LATER)
    lead = (4, 2, 2, 2, ROWS, D)
    any_spec = pl.BlockSpec(memory_space=pl.ANY)
    smem = pl.BlockSpec(memory_space=pltpu.SMEM)
    weights = jax.ShapeDtypeStruct(lead, BF16)
    ins = ins + [(a, 0) for a in shards]
    specs = [blocked(s, n) if n else whole(s) for s, _, n in outs]
    shapes = [jax.ShapeDtypeStruct(s, d) for s, d, _ in outs]
    groups = 2 * len(GATHER_GROUPS)
    res = pl.pallas_call(
        gather_forward_kernel,
        grid=(steps,),
        in_specs=[smem] + [blocked(a.shape, n) if n else whole(a.shape) for a, n in ins],
        out_specs=specs[:3] + [any_spec, any_spec] + specs[3:],
        out_shape=shapes[:3] + [weights, weights] + shapes[3:],
        scratch_shapes=[
            pltpu.VMEM(outs[2][0], F32),
            pltpu.VMEM(lead, BF16),
            pltpu.SemaphoreType.DMA((LAYERS, 9)),
            pltpu.SemaphoreType.DMA((groups, 4, 3)),
            pltpu.SemaphoreType.DMA((groups, 4, 3)),
            pltpu.SemaphoreType.DMA(()),
        ],
        compiler_params=pltpu.CompilerParams(
            dimension_semantics=("arbitrary",), vmem_limit_bytes=VMEM_LIMIT, collective_id=0,
            has_side_effects=True,
        ),
    )(emb, *[a for a, _ in ins])
    hidden, act, slope, w0, w1, *saved = res
    return (hidden, act, slope, w0.reshape(STEMS, ROWS, D), w1.reshape(STEMS, ROWS, D), *saved)


class Scatter:
    def __init__(self, at, groups, source, acc, lands, out, small, sems):
        self.at, self.groups, self.source, self.acc, self.lands, self.out = at, groups, source, acc, lands, out
        self.send_sem, self.recv_sem, self.small_send, self.small_recv = sems
        self.sm, self.smr, self.smz, self.small_out = small

    def order(self, chunk):
        return ("c",) + chunk[3][::-1]

    def left(self, chunk, phase):
        return [a for a in AXES if a not in self.order(chunk)[: phase + 1]]

    def copies(self, g, phase):
        for i, chunk in enumerate(self.groups[g]):
            _, row, count, _ = chunk
            axis, left = self.order(chunk)[phase], self.left(chunk, phase)
            for by in range(1, SIZES[axis]):
                to = moved(self.at, axis, by)
                src = []
                for a in "zyx":
                    spot = to if a == axis else self.at
                    src.append(pl.ds(0, SIZES[a]) if a in left else spot[a])
                dst = [by - 1] if axis == "z" else [pl.ds(0, SIZES[a]) for a in left]
                source = self.source(to["c"]) if phase == 0 else self.acc
                rows = (pl.ds(row, count), slice(None))
                sem = (2 * g + i, AXES.index(axis), by - 1)
                yield pltpu.make_async_remote_copy(
                    source.at[tuple(src) + rows], self.lands[phase].at[tuple(dst) + rows],
                    self.send_sem.at[sem], self.recv_sem.at[sem],
                    device_id=(number(to),), device_id_type=MESH,
                )

    def add(self, g, phase):
        for chunk in self.groups[g]:
            _, row, count, _ = chunk
            axis, left = self.order(chunk)[phase], self.left(chunk, phase)
            rows = (pl.ds(row, count), slice(None))
            keep = tuple(slice(None) if a in left else self.at[a] for a in "zyx") + rows
            value = self.acc[keep].astype(F32)
            if axis == "z":
                for by in range(SIZES["z"] - 1):
                    value = value + self.lands[3][(by,) + rows].astype(F32)
                self.out[rows] = value
            else:
                land = (slice(None),) * len(left) + rows
                self.acc[keep] = (value + self.lands[phase][land].astype(F32)).astype(BF16)

    def small_copies(self, phase, arriving):
        axis = "cxyz"[phase]
        for by in range(1, SIZES[axis]):
            whose = moved(self.at, axis, -by) if arriving else self.at
            dst = self.smz.at[whose["z"]] if axis == "z" else self.smr.at[phase]
            yield pltpu.make_async_remote_copy(
                self.sm.at[phase], dst, self.small_send.at[phase, by - 1], self.small_recv.at[phase, by - 1],
                device_id=(number(moved(self.at, axis, by)),), device_id_type=MESH,
            )

    def small_add(self, phase):
        if phase < 3:
            self.sm[phase + 1] = self.sm[phase] + self.smr[phase]
        else:
            self.smz[self.at["z"]] = self.sm[phase]
            self.small_out[...] = (self.smz[0] + self.smz[1]) + (self.smz[2] + self.smz[3])

    def run(self, moves):
        for g, phase in moves:
            if phase > 0:
                for copy in self.small_copies(phase - 1, True) if g < 0 else self.copies(g, phase - 1):
                    copy.wait_recv()
                self.small_add(phase - 1) if g < 0 else self.add(g, phase - 1)
            if phase < 4:
                for copy in self.small_copies(phase, False) if g < 0 else self.copies(g, phase):
                    copy.start()

    def close(self):
        for phase in range(4):
            for g in range(len(self.groups)):
                for copy in self.copies(g, phase):
                    copy.wait_send()
            for copy in self.small_copies(phase, False):
                copy.wait_send()


SCATTER_GROUPS = (chunks_of(0, BOUNDS), chunks_of(1, HALVES))
SCATTER_BESIDE = (
    ((-1, 0), (0, 0), (1, 0)),
    ((-1, 1),),
    ((-1, 2), (0, 1), (1, 1)),
    ((-1, 3),),
    ((-1, 4),),
    ((0, 2),),
    (),
    ((1, 2),),
)
PROPRIO = None
SCATTER_END = (
    (0, 0, 0), (1, 0, 3), (0, 1, 0), (0, 0, 1), PROPRIO, (0, -1, 0), (0, 2, 0), (0, 1, 1), (0, -1, 1), (1, 1, 3),
    (0, 0, 2), (0, 3, 0), (0, 2, 1), (0, -1, 2), (0, 1, 2), (0, 0, 3), (0, 3, 1), (0, 2, 2), (0, -1, 3), (1, 0, 4),
    (0, 1, 3), (0, 0, 4), (0, 3, 2), (1, 1, 4), (0, 2, 3), (0, 1, 4), (0, 3, 3), (0, 2, 4), (0, -1, 4), (0, 3, 4),
)


def backward_scatter_kernel(
    emb_ref, before_ref, last_ref, ids_ref, grad_ref, prop_ref, w_ref, vec_ref, gfeat1_ref, gprop1_ref,
    act_ref, slope_ref, *rest
):
    n = len(SAVED)
    saved, (g1, s1), rest = rest[:n], rest[n : n + 2], rest[n + 2 :]
    (gtok_ref, gfeat_ref, gprop_ref, mats_ref, small_ref, grows_ref), rest = rest[:6], rest[6:]
    acc, rest = dict(zip(ACC, rest[: len(ACC)])), rest[len(ACC) :]
    others, sbuf, own_sem = rest[:3]
    per_layer = rest[3:]
    step = pl.program_id(0)
    samples = before_ref.shape[0]
    at = place()

    def scatter_of(layer):
        accum, r0, r1, r2, r3, sm, smr, smz, *sems = per_layer[12 * layer : 12 * (layer + 1)]
        source = (lambda c: g1.at[:, :, :, c]) if layer else (lambda c: sbuf)
        return Scatter(
            at, SCATTER_GROUPS[layer], source, accum, (r0, r1, r2, r3), mats_ref.at[layer],
            (sm, smr, smz, small_ref.at[layer]), sems,
        )

    first, second = scatter_of(0), scatter_of(1)
    own = pltpu.make_async_copy(g1.at[:, :, :, at["c"]], second.acc, own_sem)

    @pl.when(step == 0)
    def _():
        own.start()
        greet(at)
        for name in ACC[1:]:
            acc[name][...] = jnp.zeros(acc[name].shape, F32)
        second.sm[0] = s1[...]
        own.wait()
        second.run(SCATTER_BESIDE[0])

    def moves_at(half):
        for i in range(len(SCATTER_BESIDE) // 2):
            if 2 * i + half:
                pl.when(step == i)(functools.partial(second.run, SCATTER_BESIDE[2 * i + half]))

    moves_at(0)
    es = [emb_ref[step * SB + j] for j in range(SB)]
    befores = [before_ref[step * SB + j] for j in range(SB)]
    stem = acc["stem"]

    def add(j, e, pieces):
        for row, value in pieces:
            old = stem[jnp.maximum(befores[j], 0), row : row + value.shape[0], :]
            stem[step * SB + j, row : row + value.shape[0], :] = value + jnp.where(befores[j] >= 0, old, 0.0)

    ghid, gctx, grows = backward_block(
        es, grad_ref[...], load(saved), w_ref, vec_ref[0].astype(F32), {**acc, "add": add},
        lambda: moves_at(1)
    )
    gtok_ref[...] = ghid
    grows_ref[block_rows(step), :] = grows
    write_features(gctx, gfeat1_ref, gfeat_ref)

    def gather_group(g):
        start, stop = BOUNDS[g], BOUNDS[g + 1]

        def line(z, carry):
            for i in range(4):
                spot = (z, i // 2, i % 2)
                for ref, c in ((first.acc, at["c"]), (sbuf, 1 - at["c"])):
                    e = 8 * z + 2 * i + c
                    s = last_ref[e]
                    if start < STEM_ROWS:
                        end = min(stop, STEM_ROWS)
                        value = stem[jnp.maximum(s, 0), start:end, :]
                        ref[spot + (slice(start, end), slice(None))] = jnp.where(s >= 0, value, 0.0).astype(BF16)
                    if stop > STEM_ROWS:
                        begin = max(start, STEM_ROWS)
                        ref[spot + (slice(begin, stop), slice(None))] = others[
                            e, begin - STEM_ROWS : stop - STEM_ROWS, :
                        ]
            return carry

        lax.fori_loop(0, SIZES["z"], line, 0)

    @pl.when(step == pl.num_programs(0) - 1)
    def _():
        for move in SCATTER_END:
            if move is PROPRIO:
                *grads, bias, gprop = proprio_backward(
                    ids_ref, prop_ref, w_ref, act_ref[...], slope_ref[...], grows_ref[...]
                )
                for row, part in other_blocks(acc, grads):
                    row -= STEM_ROWS
                    others[:, row : row + part.shape[1], :] = part
                first.sm[0, 0:16, :] = small_rows(acc)
                first.sm[0, 16:SMALL, :] = bias
                write_proprio(gprop + gprop1_ref[...], gprop_ref)
                continue
            layer, g, phase = move
            if layer == 0 and phase == 0 and g >= 0:
                gather_group(g)
            (first, second)[layer].run(((g, phase),))
        second.close()
        first.close()


def backward_scatter(steps, scalars, ins, outs, g1, s1):
    lead = (4, 2, 2, 2, ROWS, D)
    samples = scalars[0].shape[0]
    smem = pl.BlockSpec(memory_space=pltpu.SMEM)
    any_spec = pl.BlockSpec(memory_space=pl.ANY)
    outs = outs + [((LAYERS, ROWS, D), F32, 0), ((LAYERS, SMALL, D), F32, 0)]
    per_layer = [
        pltpu.VMEM((4, 2, 2, ROWS, D), BF16),
        pltpu.VMEM((4, 2, 2, ROWS, D), BF16),
        pltpu.VMEM((4, 2, ROWS, D), BF16),
        pltpu.VMEM((4, ROWS, D), BF16),
        pltpu.VMEM((3, ROWS, D), BF16),
        pltpu.VMEM((4, SMALL, D), F32),
        pltpu.VMEM((3, SMALL, D), F32),
        pltpu.VMEM((4, SMALL, D), F32),
        pltpu.SemaphoreType.DMA((2 * len(BOUNDS), 4, 3)),
        pltpu.SemaphoreType.DMA((2 * len(BOUNDS), 4, 3)),
        pltpu.SemaphoreType.DMA((4, 3)),
        pltpu.SemaphoreType.DMA((4, 3)),
    ]
    return pl.pallas_call(
        backward_scatter_kernel,
        grid=(steps,),
        in_specs=[smem] * 3 + [blocked(a.shape, n) if n else whole(a.shape) for a, n in ins]
        + [any_spec, whole(s1.shape)],
        out_specs=[blocked(s, n) if n else whole(s) for s, _, n in outs],
        out_shape=[jax.ShapeDtypeStruct(s, d) for s, d, _ in outs],
        scratch_shapes=[pltpu.VMEM((STEPS * samples, D), F32)] + acc_shapes(samples)
        + [
            pltpu.VMEM((STEMS, ROWS - STEM_ROWS, D), BF16),
            pltpu.VMEM((4, 2, 2, ROWS, D), BF16),
            pltpu.SemaphoreType.DMA(()),
        ]
        + per_layer * LAYERS,
        compiler_params=pltpu.CompilerParams(
            dimension_semantics=("arbitrary",), vmem_limit_bytes=VMEM_LIMIT, collective_id=1,
            has_side_effects=True,
        ),
    )(*scalars, *[a for a, _ in ins], g1.reshape(lead), s1)


def unpack_kernel(mats, small, gtok_in, gfeat_in, gtok, gfeat, att, up, down, stem, q, pin, vec, mb, sb):
    gtok[...] = gtok_in[...]
    gfeat[...] = gfeat_in[...]
    pl.when(pl.program_id(0) == 0)(
        lambda: split_gradients(mats, small, att, up, down, stem, q, pin, vec, mb, sb)
    )


def split_gradients(mats, small, att, up, down, stem, q, pin, vec, mb, sb):
    for layer in range(LAYERS):
        for j, row in enumerate(MAT_ROWS):
            stem[layer, :, j * D : (j + 1) * D] = mats[layer, row : row + D, :]
        q[layer] = mats[layer, R_Q:R_WP, :]
        pin[layer] = mats[layer, R_PIN:R_ATT, :]
        att[layer] = mats[layer, R_ATT:R_UP, :]
        up[layer] = mats[layer, R_UP:R_DOWN, :]
        down[layer] = mats[layer, R_DOWN:ROWS, :]
        vec[layer] = small[layer, 0:8, :]
        for i in range(4):
            mb[layer : layer + 1, i * D : (i + 1) * D] = small[layer, 8 + i : 9 + i, :]
        sb[layer] = small[layer, 16:SMALL, :]


def unpack(mats, small, gtok, gfeat):
    outs = [
        (LAYERS, 16, D), (LAYERS, 16, D), (LAYERS, 16, D), (LAYERS, D, 4 * D), (LAYERS, SQ, D),
        (LAYERS, PROP, D), (LAYERS, 8, D), (LAYERS, FF), (LAYERS, 2 * STEMS, D),
    ]
    steps = 4
    moved_through = [blocked(a.shape, a.shape[0] // steps) for a in (gtok, gfeat)]
    return pl.pallas_call(
        unpack_kernel,
        grid=(steps,),
        out_shape=[jax.ShapeDtypeStruct(s, F32) for s in [gtok.shape, gfeat.shape] + outs],
        in_specs=[whole(mats.shape), whole(small.shape)] + moved_through,
        out_specs=moved_through + [whole(s) for s in outs],
    )(mats, small, gtok, gfeat)


def pack(attn, up, down, stem, queries, pin):
    gathered = [lax.all_gather(a, "fsdp", axis=1, tiled=True) for a in (attn, up, down, stem, queries, pin)]
    attn, up, down, stem, queries, pin = gathered
    stem = stem.reshape(LAYERS, STEMS, D, 4, D).transpose(0, 1, 3, 2, 4).reshape(LAYERS, STEMS, 4 * D, D)
    queries, *parts = [a.reshape(LAYERS, STEMS, -1, D) for a in (queries, pin, attn, up, down)]
    return jnp.concatenate([stem[:, :, : 3 * D], queries, stem[:, :, 3 * D :], *parts], 2)


def unpack_blocks(grad):
    stem = jnp.concatenate([grad[..., row : row + D, :] for row in MAT_ROWS], -1)
    return (
        grad[..., R_ATT:R_UP, :], grad[..., R_UP:R_DOWN, :], grad[..., R_DOWN:ROWS, :],
        stem, grad[..., R_Q:R_WP, :], grad[..., R_PIN:R_ATT, :],
    )


def body(n, tokens, features, proprio, embodiment, trunk_attn, feedforward_up_weight, mlp_down,
         stem_mats, stem_queries, prop_in, trunk_vectors, mlp_bias, stem_bias, cotangent):
    shards = (trunk_attn, feedforward_up_weight, mlp_down, stem_mats, stem_queries, prop_in)
    out, gtok, gfeat, gprop, mats, small = compute(
        tokens, features, proprio, embodiment, shards, trunk_vectors, mlp_bias, stem_bias,
        cotangent, None if n == 32 else pack(*shards),
    )
    if n == 32:
        return (out, gtok, gfeat, gprop, *mats, small.reshape(LAYERS, STEMS, 2, D))
    mats = [
        lax.psum_scatter(a.reshape(LAYERS, -1, a.shape[-1]), "fsdp", scatter_dimension=1, tiled=True)
        for a in unpack_blocks(mats.astype(F32))
    ]
    small = lax.psum(small, "fsdp")
    gvec = small[:, :8]
    gmb = small[:, 8:12].reshape(LAYERS, FF)
    gsb = small[:, 16:].reshape(LAYERS, STEMS, 2, D)
    return (out, gtok, gfeat, gprop, *mats, gvec, gmb, gsb)


def solution(mesh):
    n = mesh.shape["fsdp"]
    return jax.shard_map(
        functools.partial(body, n),
        mesh=mesh,
        in_specs=(
            P("fsdp"), P("fsdp"), P("fsdp"), P("fsdp"),
            P(None, "fsdp"), P(None, "fsdp"), P(None, "fsdp"), P(None, "fsdp"), P(None, "fsdp"),
            P(None, "fsdp"), P(), P(), P(), P("fsdp"),
        ),
        out_specs=(
            P("fsdp"), P("fsdp"), P("fsdp"), P("fsdp"),
            P(None, "fsdp"), P(None, "fsdp"), P(None, "fsdp"), P(None, "fsdp"), P(None, "fsdp"),
            P(None, "fsdp"), P(), P(), P(),
        ),
        check_vma=False,
    )
```

```python
import functools
import math

import jax
import jax.numpy as jnp
from jax import lax
from jax.experimental import pallas as pl
from jax.experimental.pallas import tpu as pltpu
from jax.sharding import PartitionSpec as P

D = 128
HEADS = 8
HD = 16
FF = 512
SQ = 16
FR = 49
CR = 112
PROP = 32
STEMS = 32
STEPS = 2
LAYERS = 2
TOK = 32
SB = 16

R_Q = 3 * D
R_WP = R_Q + SQ
R_PIN = R_WP + D
R_ATT = R_PIN + PROP
R_UP = R_ATT + 16
R_DOWN = R_UP + 16
ROWS = R_DOWN + 16
STEM_ROWS = R_WP
SMALL = 16 + 2 * STEMS

MAT_ROWS = (0, D, 2 * D, R_WP)

F32 = jnp.float32
BF16 = jnp.bfloat16
VMEM_LIMIT = 60 * 1024 * 1024


def dot(a, b):
    return lax.dot_general(a, b, (((1,), (0,)), ((), ())), preferred_element_type=F32)


def dot_nt(a, b):
    return lax.dot_general(a, b, (((1,), (1,)), ((), ())), preferred_element_type=F32)


def dot_tn(a, b):
    return lax.dot_general(a, b, (((0,), (0,)), ((), ())), preferred_element_type=F32)


def gelu_parts(x):
    cdf = 0.5 + 0.5 * lax.erf(x * math.sqrt(0.5))
    slope = cdf + x * (jnp.exp(-0.5 * x * x) * (1.0 / math.sqrt(2.0 * math.pi)))
    return x * cdf, slope


def norm_parts(x):
    centred = x - jnp.mean(x, -1, keepdims=True)
    inverse = lax.rsqrt(jnp.mean(centred * centred, -1, keepdims=True) + 1e-05)
    return centred * inverse, inverse


def norm_back(grad, gain, hat, inverse):
    g = grad * gain
    return inverse * (
        g - jnp.mean(g, -1, keepdims=True) - hat * jnp.mean(g * hat, -1, keepdims=True)
    )


def head_mask(rows, value):
    row = lax.broadcasted_iota(jnp.int32, (HEADS * rows, D), 0) // rows
    lane = lax.broadcasted_iota(jnp.int32, (HEADS * rows, D), 1) // HD
    return jnp.where(row == lane, value, 0.0).astype(BF16)


def expand(rows, mask):
    return jnp.concatenate([rows] * HEADS, 0) * mask


def contract(wide, rows):
    lane = lax.broadcasted_iota(jnp.int32, (rows, D), 1) // HD
    out = wide[:rows]
    for head in range(1, HEADS):
        out = jnp.where(lane == head, wide[head * rows : (head + 1) * rows], out)
    return out


def fold(x):
    return jnp.sum(x.reshape(x.shape[0] // 8, 8, x.shape[1]), 0)


def slot(w_ref, e, start, stop):
    if len(w_ref.shape) == 3:
        return w_ref[e, start:stop, :]
    return w_ref[e // 8, (e // 4) % 2, (e // 2) % 2, e % 2, start:stop, :]


def all_slots(w_ref, start, stop):
    index = (slice(None),) * (len(w_ref.shape) - 2)
    return w_ref[index + (slice(start, stop), slice(None))].reshape(STEMS * (stop - start), D)


def trunk_weights(w_ref):
    attn = all_slots(w_ref, R_ATT, R_UP)
    up = all_slots(w_ref, R_UP, R_DOWN)
    down = all_slots(w_ref, R_DOWN, ROWS)
    wqkv = jnp.concatenate([attn[:D], attn[D : 2 * D], attn[2 * D : 3 * D]], 1)
    return wqkv, attn[3 * D :], up, down


def stem_kv_weight(w_ref, e):
    return jnp.concatenate([slot(w_ref, e, 0, D), slot(w_ref, e, D, 2 * D)], 1)


def step_reduce(x, op):
    x = x.reshape(x.shape[0] // 8, 8, x.shape[1])
    out = x[0]
    for i in range(1, x.shape[0]):
        out = op(out, x[i])
    out = op(out, pltpu.roll(out, 4, 0))
    return op(out, pltpu.roll(out, 2, 0))


def step_apply(x, y, op):
    return op(x.reshape(x.shape[0] // 8, 8, x.shape[1]), y[None]).reshape(x.shape)


def step_masks():
    odd = lax.broadcasted_iota(jnp.int32, (CR, D), 0) % 2
    return (odd == 0).astype(BF16), odd.astype(BF16)


def split_steps(p, masks):
    return jnp.concatenate([p * masks[0], p * masks[1]], 1)


def softmax_rows(score):
    top = jnp.max(score, 0, keepdims=True)
    weight = jnp.exp(score - top)
    return weight * (1.0 / jnp.sum(weight, 0, keepdims=True))


def stem_ids(emb_ref, rows, down=False):
    samples = emb_ref.shape[1]
    row = lax.broadcasted_iota(jnp.int32, (rows, samples), 0) // STEPS
    pick = (row == lax.broadcasted_iota(jnp.int32, (rows, samples), 1)).astype(BF16)
    stems = jnp.broadcast_to(emb_ref[...].astype(F32).astype(BF16), (D, samples))
    return dot_nt(stems, pick) if down else dot_nt(pick, stems)


def spread(values, ids):
    values = values.astype(F32)
    return jnp.concatenate([jnp.where(ids == e, values, 0.0).astype(BF16) for e in range(STEMS)], 1)


def sample_rows(samples):
    shape = (samples * STEPS, samples * STEPS)
    row = lax.broadcasted_iota(jnp.int32, shape, 0)
    column = (row % STEPS) * samples + row // STEPS
    return (lax.broadcasted_iota(jnp.int32, shape, 1) == column).astype(BF16)


def spread_down(values, ids):
    values = values.astype(F32)
    return jnp.concatenate([jnp.where(ids == e, values, 0.0).astype(BF16) for e in range(STEMS)], 0)


def spread_proprio(prop_ref, ids, down=False):
    both = jnp.concatenate([prop_ref[t] for t in range(STEPS)], 1)
    group = D // PROP
    tiled = jnp.concatenate([both] * group, 0)
    place_ = sample_rows(prop_ref.shape[2])
    rows = dot_nt(tiled, place_) if down else dot_nt(place_, tiled)
    entry = (lax.broadcasted_iota(jnp.int32, rows.shape, 0 if down else 1) // PROP).astype(F32)
    return jnp.concatenate(
        [jnp.where(ids == entry + float(group * b), rows, 0.0).astype(BF16) for b in range(STEMS // group)],
        0 if down else 1,
    )


def bias_picks(ids):
    lane = lax.broadcasted_iota(jnp.int32, (ids.shape[0], 2 * STEMS), 1).astype(F32)
    twice = 2.0 * ids[:, : 2 * STEMS]
    return (lane == twice).astype(BF16), (lane == twice + 1.0).astype(BF16)


def proprio_forward(emb_ref, prop_ref, w_ref, biases):
    ids = stem_ids(emb_ref, STEPS * emb_ref.shape[1])
    first, second = bias_picks(ids)
    pre = dot(spread_proprio(prop_ref, ids), all_slots(w_ref, R_PIN, R_ATT)) + dot(first, biases)
    act, slope = gelu_parts(pre)
    act = act.astype(BF16)
    return act, slope, dot(spread(act, ids), all_slots(w_ref, R_WP, R_PIN)) + dot(second, biases)


def proprio_backward(emb_ref, prop_ref, w_ref, act, slope, grad_rows):
    ids = stem_ids(emb_ref, STEPS * emb_ref.shape[1])
    first, second = bias_picks(ids)
    low = grad_rows.astype(BF16)
    wp = jnp.concatenate([slot(w_ref, e, R_WP, R_PIN) for e in range(STEMS)], 1)
    pin = jnp.concatenate([slot(w_ref, e, R_PIN, R_ATT) for e in range(STEMS)], 1)
    grad_pre = (dot_nt(spread(low, ids), wp) * slope).astype(BF16)
    down = stem_ids(emb_ref, STEPS * emb_ref.shape[1], True)
    return (
        dot(spread_down(act.astype(F32).T, down), low), dot(spread_proprio(prop_ref, down, True), grad_pre),
        dot_tn(first, grad_pre) + dot_tn(second, low), dot_nt(spread(grad_pre, ids), pin),
    )


def forward_block(es, hidden, feat_ref, prows, w_ref, vec, mb, tick=None):
    kept = {}
    row8 = lax.broadcasted_iota(jnp.int32, (8, D), 0)
    contexts = []
    for j in range(SB):
        rows = feat_ref[j * STEPS * FR : (j + 1) * STEPS * FR, :]
        last = jnp.concatenate([rows[96:98], jnp.zeros((14, D), BF16)], 0).astype(F32)[:8]
        k = j // 4 * 8
        mine = pltpu.roll(prows[k : k + 8], (2 - 2 * (j % 4)) % 8, 0)
        tail = jnp.where(row8 < 2, last, jnp.where(row8 < 4, mine, 0.0))
        tail = jnp.concatenate([tail, jnp.zeros((8, D), F32)], 0).astype(BF16)
        contexts.append(jnp.concatenate([rows[:96], tail], 0))
    kept["ctx"] = contexts
    kvs = [dot(contexts[j], stem_kv_weight(w_ref, e)).astype(BF16) for j, e in enumerate(es)]
    kept["kv"] = kvs
    mask16 = head_mask(SQ, 0.25)
    scores = [
        dot_nt(kvs[j][:, :D], expand(slot(w_ref, e, R_Q, R_WP), mask16)) for j, e in enumerate(es)
    ]
    valid = lax.broadcasted_iota(jnp.int32, (104, D), 0) < STEPS * (FR + 1)
    pad = jnp.zeros((8, D), F32)
    probs = []
    for j in range(SB):
        s = jnp.where(valid, scores[j][:104], -1e30)
        weight = jnp.exp(step_apply(s, step_reduce(s, jnp.maximum), jnp.subtract))
        scale = 1.0 / step_reduce(weight, jnp.add)
        probs.append(jnp.concatenate([step_apply(weight, scale, jnp.multiply), pad], 0))
    kept["prob"] = probs
    masks = step_masks()
    mixes = []
    for j in range(SB):
        wide = dot_tn(split_steps(probs[j].astype(BF16), masks), kvs[j][:, D:])
        mixes += [contract(wide[t * D : (t + 1) * D], SQ).astype(BF16) for t in range(STEPS)]
    mix = jnp.concatenate(mixes, 0)
    kept["mix"] = mix
    if tick is not None:
        tick()
    outs = [
        dot(mix[j * TOK : (j + 1) * TOK], slot(w_ref, e, 2 * D, 3 * D)) for j, e in enumerate(es)
    ]
    first = hidden + jnp.concatenate(outs, 0)
    kept["first"] = first
    wqkv, wout, up, down = trunk_weights(w_ref)
    normed = (norm_parts(first)[0] * vec[0:1] + vec[1:2]).astype(BF16)
    bias = jnp.concatenate([vec[2:3], jnp.zeros((1, D), F32), vec[3:4]], 1)
    qkv = (dot(normed, wqkv) + bias).astype(BF16)
    kept["qkv"] = qkv
    mask32 = head_mask(TOK, 0.25)
    rows = [qkv[j * TOK : (j + 1) * TOK] for j in range(SB)]
    scores = [dot_nt(rows[j][:, D : 2 * D], expand(rows[j][:, :D], mask32)) for j in range(SB)]
    sprobs = [softmax_rows(s) for s in scores]
    smixes = [
        contract(dot_tn(sprobs[j].astype(BF16), rows[j][:, 2 * D :]), TOK).astype(BF16)
        for j in range(SB)
    ]
    kept["sprob"] = sprobs
    smix = jnp.concatenate(smixes, 0)
    kept["smix"] = smix
    second = first + (dot(smix, wout) + vec[4:5])
    kept["second"] = second
    mlp_in = (norm_parts(second)[0] * vec[5:6] + vec[6:7]).astype(BF16)
    act, slope = gelu_parts(dot_nt(mlp_in, up) + mb)
    act = act.astype(BF16)
    kept["act"], kept["slope"] = act, slope
    return second + (dot(act, down) + vec[7:8]), kept


def backward_block(es, grad, kept, w_ref, vec, acc, tick=None):
    wqkv, wout, up, down = trunk_weights(w_ref)
    out_low = grad.astype(BF16)
    acc["vec"][7] += fold(out_low.astype(F32))
    acc["down"][...] += dot_tn(out_low, kept["act"])
    grad_act = dot_nt(out_low, down)
    grad_pre = (grad_act * kept["slope"].astype(F32)).astype(BF16)
    acc["mb"][...] += fold(grad_pre.astype(F32))
    hat, inverse = norm_parts(kept["second"])
    mlp_in = (hat * vec[5:6] + vec[6:7]).astype(BF16)
    acc["up"][...] += dot_tn(mlp_in, grad_pre)
    grad_in = dot(grad_pre, up)
    acc["vec"][5] += fold(grad_in * hat)
    acc["vec"][6] += fold(grad_in)
    grad_second = grad + norm_back(grad_in, vec[5:6], hat, inverse)
    branch = grad_second.astype(BF16)
    acc["vec"][4] += fold(branch.astype(F32))
    acc["wout"][...] += dot_tn(kept["smix"], branch)
    grad_mix = dot_nt(branch, wout).astype(BF16)
    mask32 = head_mask(TOK, 0.25)
    mask32_one = head_mask(TOK, 1.0)
    rows = [kept["qkv"][j * TOK : (j + 1) * TOK] for j in range(SB)]
    wides = [expand(grad_mix[j * TOK : (j + 1) * TOK], mask32_one) for j in range(SB)]
    grad_ps = [dot_nt(rows[j][:, 2 * D :], wides[j]) for j in range(SB)]
    grads_v = [dot(kept["sprob"][j].astype(BF16), wides[j]) for j in range(SB)]
    gss = []
    for j in range(SB):
        p = kept["sprob"][j].astype(F32)
        gss.append((p * (grad_ps[j] - jnp.sum(grad_ps[j] * p, 0, keepdims=True))).astype(BF16))
    grads_q = [contract(dot_tn(gss[j], rows[j][:, D : 2 * D]), TOK) * 0.25 for j in range(SB)]
    grads_k = [dot(gss[j], expand(rows[j][:, :D], mask32)) for j in range(SB)]
    grad_qkv = jnp.concatenate(
        [jnp.concatenate(g, 0).astype(BF16) for g in (grads_q, grads_k, grads_v)], 1
    )
    acc["vec"][2] += fold(grad_qkv[:, :D].astype(F32))
    acc["vec"][3] += fold(grad_qkv[:, 2 * D :].astype(F32))
    hat, inverse = norm_parts(kept["first"])
    normed = (hat * vec[0:1] + vec[1:2]).astype(BF16)
    acc["wqkv"][...] += dot_tn(normed, grad_qkv)
    grad_normed = dot_nt(grad_qkv, wqkv)
    acc["vec"][0] += fold(grad_normed * hat)
    acc["vec"][1] += fold(grad_normed)
    grad_first = grad_second + norm_back(grad_normed, vec[0:1], hat, inverse)
    stem_grad = grad_first.astype(BF16)
    mask16 = head_mask(SQ, 0.25)
    mask16_one = head_mask(SQ, 1.0)
    row8 = lax.broadcasted_iota(jnp.int32, (8, D), 0)
    if tick is not None:
        tick()
    gs_in = [stem_grad[j * TOK : (j + 1) * TOK] for j in range(SB)]
    gmixes = [dot_nt(gs_in[j], slot(w_ref, e, 2 * D, 3 * D)).astype(BF16) for j, e in enumerate(es)]
    grad_wo = [dot_tn(kept["mix"][j * TOK : (j + 1) * TOK], gs_in[j]) for j in range(SB)]
    kvs = [kept["kv"][j] for j in range(SB)]
    probs = [kept["prob"][j] for j in range(SB)]
    wides = [
        jnp.concatenate(
            [expand(gmixes[j][t * SQ : (t + 1) * SQ], mask16_one) for t in range(STEPS)], 0
        )
        for j in range(SB)
    ]
    grad_ps = [dot_nt(kvs[j][:, D:], wides[j]) for j in range(SB)]
    masks = step_masks()
    gvs = [dot(split_steps(probs[j].astype(BF16), masks), wides[j]) for j in range(SB)]
    even = lax.broadcasted_iota(jnp.int32, (104, D), 0) % 2 == 0
    pad = jnp.zeros((8, D), F32)
    gss = []
    for j in range(SB):
        p = probs[j][:104].astype(F32)
        gp = jnp.where(even, grad_ps[j][:104, :D], grad_ps[j][:104, D:])
        gs = p * step_apply(gp, step_reduce(gp * p, jnp.add), jnp.subtract)
        gss.append(jnp.concatenate([gs, pad], 0).astype(BF16))
    gks = [dot(gss[j], expand(slot(w_ref, e, R_Q, R_WP), mask16)) for j, e in enumerate(es)]
    gkvs = [
        jnp.concatenate([gks[j], gvs[j]], 1).astype(BF16) for j in range(SB)
    ]
    grad_contexts = [
        dot_nt(gkvs[j], stem_kv_weight(w_ref, e)).astype(BF16) for j, e in enumerate(es)
    ]
    grad_prows = []
    for k in range(0, SB, 4):
        rows = jnp.zeros((8, D), F32)
        for j in range(k, k + 4):
            tail = pltpu.roll(grad_contexts[j][96:112].astype(F32)[:8], (2 * (j % 4) - 2) % 8, 0)
            rows = jnp.where(row8 // 2 == j % 4, tail, rows)
        grad_prows.append(rows)
    grad_q = [contract(dot_tn(gss[j], kvs[j][:, :D]), SQ) * 0.25 for j in range(SB)]
    grad_wkv = [dot_tn(kept["ctx"][j], gkvs[j]) for j in range(SB)]
    for j, e in enumerate(es):
        acc["add"](
            j, e,
            ((0, grad_wkv[j][:, :D]), (D, grad_wkv[j][:, D:]), (2 * D, grad_wo[j]), (R_Q, grad_q[j])),
        )
    return grad_first, grad_contexts, jnp.concatenate(grad_prows, 0)


ACC = ("stem", "wqkv", "wout", "up", "down", "vec", "mb")


def acc_shapes(entries):
    return [
        pltpu.VMEM((entries, STEM_ROWS, D), F32),
        pltpu.VMEM((D, 3 * D), F32),
        pltpu.VMEM((D, D), F32),
        pltpu.VMEM((D, FF), F32),
        pltpu.VMEM((D, FF), F32),
        pltpu.VMEM((8, 8, D), F32),
        pltpu.VMEM((8, FF), F32),
    ]


def clear(acc):
    for ref in acc.values():
        ref[...] = jnp.zeros(ref.shape, ref.dtype)


def add_in_place(acc):
    def add(j, e, pieces):
        for row, value in pieces:
            acc["stem"][e, row : row + value.shape[0], :] += value

    return {**acc, "add": add}


def trunk_blocks(acc):
    wqkv = acc["wqkv"][...]
    attn = [wqkv[:, :D], wqkv[:, D : 2 * D], wqkv[:, 2 * D :], acc["wout"][...]]
    return (
        jnp.concatenate(attn, 0).astype(BF16).reshape(STEMS, 16, D),
        acc["up"][...].T.astype(BF16).reshape(STEMS, 16, D),
        acc["down"][...].T.astype(BF16).reshape(STEMS, 16, D),
    )


def small_rows(acc):
    mb = jnp.sum(acc["mb"][...], 0, keepdims=True)
    return jnp.concatenate(
        [jnp.sum(acc["vec"][...], 1)] + [mb[:, i * D : (i + 1) * D] for i in range(4)]
        + [jnp.zeros((4, D), F32)], 0
    )


def other_blocks(acc, grads):
    grad_wp, grad_pin = grads
    return (
        (R_WP, grad_wp.astype(BF16).reshape(STEMS, D, D)),
        (R_PIN, grad_pin.astype(BF16).reshape(STEMS, PROP, D)),
    ) + tuple((R_ATT + 16 * i, part) for i, part in enumerate(trunk_blocks(acc)))


def finish(acc, grads, bias, grad_ref, small_ref):
    def stem_out(e, carry):
        grad_ref[e, 0:STEM_ROWS, :] = acc["stem"][e].astype(grad_ref.dtype)
        return carry

    lax.fori_loop(0, STEMS, stem_out, 0)
    for start, part in other_blocks(acc, grads):
        grad_ref[:, start : start + part.shape[1], :] = part
    small_ref[0:16, :] = small_rows(acc)
    small_ref[16:SMALL, :] = bias


SAVED = ("ctx", "kv", "prob", "mix", "first", "qkv", "sprob", "smix", "second", "act", "slope")
PER_SAMPLE = ("ctx", "kv", "prob", "sprob")


def saved_shapes(samples):
    rows = samples * TOK
    return dict(
        ctx=((samples, CR, D), BF16),
        kv=((samples, CR, 2 * D), BF16),
        prob=((samples, CR, D), BF16),
        mix=((rows, D), BF16),
        first=((rows, D), F32),
        qkv=((rows, 3 * D), BF16),
        sprob=((samples, TOK, HEADS * TOK), BF16),
        smix=((rows, D), BF16),
        second=((rows, D), F32),
        act=((rows, FF), BF16),
        slope=((rows, FF), BF16),
    )


def layer_inputs(layer, vec_ref, mb_ref):
    return vec_ref[layer].astype(F32), mb_ref[layer : layer + 1, :].astype(F32)


def start_forward(layer, emb_ref, prop_ref, w_ref, sb_ref, act_ref, slope_ref, rows_ref):
    act_ref[...], slope_ref[...], rows_ref[...] = proprio_forward(emb_ref, prop_ref, w_ref, sb_ref[layer])


def block_rows(step):
    return pl.ds(pl.multiple_of(step * SB * STEPS, SB * STEPS), SB * STEPS)


def save(kept, saved):
    for name, ref in zip(SAVED, saved):
        if name in PER_SAMPLE:
            for j in range(SB):
                ref[j] = kept[name][j].astype(ref.dtype)
        else:
            ref[...] = kept[name].astype(ref.dtype)


def load(saved):
    return {
        name: [ref[j] for j in range(SB)] if name in PER_SAMPLE else ref[...]
        for name, ref in zip(SAVED, saved)
    }


def forward_kernel(
    emb_ref, ids_ref, tok_ref, feat_ref, prop_ref, w_ref, vec_ref, mb_ref, sb_ref, out_ref, act_ref, slope_ref, *rest
):
    saved, rows_ref = rest[:-1], rest[-1]
    step = pl.program_id(0)
    pl.when(step == 0)(
        lambda: start_forward(0, ids_ref, prop_ref, w_ref, sb_ref, act_ref, slope_ref, rows_ref)
    )
    es = [emb_ref[step * SB + j] for j in range(SB)]
    out, kept = forward_block(
        es, tok_ref[...].astype(F32), feat_ref, rows_ref[block_rows(step), :], w_ref,
        *layer_inputs(0, vec_ref, mb_ref)
    )
    out_ref[...] = out
    save(kept, saved)


def link_samples(emb_ref, before_ref, last_ref):
    def unset(e, carry):
        last_ref[e] = -1
        return carry

    def link(s, carry):
        e = emb_ref[s]
        before_ref[s] = last_ref[e]
        last_ref[e] = s
        return carry

    lax.fori_loop(0, STEMS, unset, 0)
    lax.fori_loop(0, before_ref.shape[0], link, 0)


def middle_kernel(
    emb_ref, ids_ref, hid_ref, feat_ref, prop_ref, w_ref, vec_ref, mb_ref, sb_ref, cot_ref,
    out_ref, ghid_ref, gfeat_ref, gprop_ref, gw_ref, gsmall_ref, before_ref, last_ref,
    act_ref, slope_ref, rows_ref, grows_ref, *accs
):
    step = pl.program_id(0)
    acc = dict(zip(ACC, accs))

    @pl.when(step == 0)
    def _():
        clear(acc)
        link_samples(emb_ref, before_ref, last_ref)
        start_forward(1, ids_ref, prop_ref, w_ref, sb_ref, act_ref, slope_ref, rows_ref)

    es = [emb_ref[step * SB + j] for j in range(SB)]
    vec, mb = layer_inputs(1, vec_ref, mb_ref)
    out, kept = forward_block(
        es, hid_ref[...], feat_ref, rows_ref[block_rows(step), :], w_ref, vec, mb
    )
    out_ref[...] = out.astype(BF16)
    ghid, gctx, grows = backward_block(
        es, cot_ref[...].astype(F32), kept, w_ref, vec, add_in_place(acc)
    )
    ghid_ref[...] = ghid
    grows_ref[block_rows(step), :] = grows
    for j in range(SB):
        gfeat_ref[j] = gctx[j]

    @pl.when(step == pl.num_programs(0) - 1)
    def _():
        *grads, bias, gprop_ref[...] = proprio_backward(
            ids_ref, prop_ref, w_ref, act_ref[...], slope_ref[...], grows_ref[...]
        )
        finish(acc, grads, bias, gw_ref, gsmall_ref)


def write_features(gctx, gfeat1_ref, gfeat_ref):
    for j in range(0, SB, 4):
        totals = [gctx[i].astype(F32) + gfeat1_ref[i].astype(F32) for i in range(j, j + 4)]
        gfeat_ref[j * STEPS * FR : (j + 4) * STEPS * FR, :] = jnp.concatenate(
            [total[: STEPS * FR] for total in totals], 0
        )


def write_proprio(rows, gprop_ref):
    samples = gprop_ref.shape[2]
    place_ = sample_rows(samples)
    high = rows.astype(BF16)
    rest = rows - high.astype(F32)
    middle = rest.astype(BF16)
    low = (rest - middle.astype(F32)).astype(BF16)
    out = dot_tn(high, place_) + (dot_tn(middle, place_) + dot_tn(low, place_))
    for t in range(STEPS):
        gprop_ref[t] = out[:, t * samples : (t + 1) * samples]


def backward_kernel(
    emb_ref, ids_ref, grad_ref, prop_ref, w_ref, vec_ref, gfeat1_ref, gprop1_ref, act_ref, slope_ref, *rest
):
    n = len(SAVED)
    saved = rest[:n]
    gtok_ref, gfeat_ref, gprop_ref, gw_ref, gsmall_ref, grows_ref = rest[n : n + 6]
    acc = dict(zip(ACC, rest[n + 6 :]))
    step = pl.program_id(0)
    pl.when(step == 0)(lambda: clear(acc))
    es = [emb_ref[step * SB + j] for j in range(SB)]
    vec = vec_ref[0].astype(F32)
    ghid, gctx, grows = backward_block(es, grad_ref[...], load(saved), w_ref, vec, add_in_place(acc))
    gtok_ref[...] = ghid
    grows_ref[block_rows(step), :] = grows
    write_features(gctx, gfeat1_ref, gfeat_ref)

    @pl.when(step == pl.num_programs(0) - 1)
    def _():
        *grads, bias, gprop = proprio_backward(
            ids_ref, prop_ref, w_ref, act_ref[...], slope_ref[...], grows_ref[...]
        )
        finish(acc, grads, bias, gw_ref, gsmall_ref)
        write_proprio(gprop + gprop1_ref[...], gprop_ref)


def blocked(shape, per_step):
    block = (per_step,) + tuple(shape[1:])
    zeros = (0,) * (len(shape) - 1)
    return pl.BlockSpec(block, lambda i, *_: (i,) + zeros)


def whole(shape):
    zeros = (0,) * len(shape)
    return pl.BlockSpec(tuple(shape), lambda i, *_: zeros, pipeline_mode=pl.Buffered(1))


def call(kernel, steps, emb, ins, outs, scratch):
    return pl.pallas_call(
        kernel,
        grid_spec=pltpu.PrefetchScalarGridSpec(
            num_scalar_prefetch=1,
            grid=(steps,),
            in_specs=[blocked(a.shape, n) if n else whole(a.shape) for a, n in ins],
            out_specs=[
                pl.BlockSpec(memory_space=pltpu.SMEM) if n is None else blocked(s, n) if n else whole(s)
                for s, _, n in outs
            ],
            scratch_shapes=scratch,
        ),
        out_shape=[jax.ShapeDtypeStruct(s, d) for s, d, _ in outs],
        compiler_params=pltpu.CompilerParams(
            dimension_semantics=("arbitrary",), vmem_limit_bytes=VMEM_LIMIT
        ),
    )(emb, *[a for a, _ in ins])


def compute(tokens, features, proprio, emb, shards, vecs, mbs, sbs, cot, weights=None):
    samples = emb.shape[0]
    steps = samples // SB
    rows = samples * TOK
    rb = SB * TOK
    tok = tokens.reshape(rows, D)
    feat = jnp.swapaxes(features, 1, 2).reshape(samples * FR * STEPS, D)
    prop = proprio.transpose(1, 2, 0)
    ids = emb.reshape(1, samples)
    sbs = sbs.reshape(LAYERS, 2 * STEMS, D)
    fb = SB * FR * STEPS
    prows = (STEPS * samples, D)
    shapes = saved_shapes(samples)
    per = lambda s: s[0] // steps
    forward_ins = [(ids, 0), (tok, rb), (feat, fb), (prop, 0), (vecs, 0), (mbs, 0), (sbs, 0)]
    forward_outs = [((rows, D), F32, rb), (prows, BF16, 0), (prows, F32, 0)] + [
        (shapes[n][0], shapes[n][1], per(shapes[n][0])) for n in SAVED
    ]
    if weights is None:
        hidden, act, slope, w0, w1, *saved = gather_forward(steps, emb, forward_ins, forward_outs, shards)
    else:
        w0, w1 = weights
        forward_ins = forward_ins[:4] + [(w0, 0)] + forward_ins[4:]
        hidden, act, slope, *saved = call(
            forward_kernel, steps, emb, forward_ins, forward_outs, [pltpu.VMEM(prows, F32)]
        )
    grad_outs = [((STEMS, ROWS, D), BF16, 0), ((SMALL, D), F32, 0)]
    out, ghid, gfeat1, gprop1, *grads1, before, last = call(
        middle_kernel, steps, emb,
        [(ids, 0), (hidden, rb), (feat, fb), (prop, 0), (w1, 0), (vecs, 0), (mbs, 0), (sbs, 0),
         (cot.reshape(rows, D), rb)],
        [((rows, D), BF16, rb), ((rows, D), F32, rb), ((samples, CR, D), BF16, SB),
         ((STEPS * samples, PROP), F32, 0)] + grad_outs
        + [((samples,), jnp.int32, None), ((STEMS,), jnp.int32, None)],
        [pltpu.VMEM(prows, BF16)] + [pltpu.VMEM(prows, F32)] * 3 + acc_shapes(STEMS),
    )
    backward_ins = (
        [(ids, 0), (ghid, rb), (prop, 0), (w0, 0), (vecs, 0), (gfeat1, SB), (gprop1, 0), (act, 0), (slope, 0)]
        + [(a, per(a.shape)) for a in saved]
    )
    backward_outs = [
        ((rows, D), F32, rb), ((samples * FR * STEPS, D), F32, fb), ((STEPS, PROP, samples), F32, 0)
    ]
    if weights is None:
        gtok, gfeat, gprop, mats, small = backward_scatter(
            steps, (emb, before, last), backward_ins, backward_outs, *grads1
        )
        gtok, gfeat, *mats, small = unpack(mats, small, gtok, gfeat)
    else:
        gtok, gfeat, gprop, *grads0 = call(
            backward_kernel, steps, emb, backward_ins, backward_outs + grad_outs,
            [pltpu.VMEM(prows, F32)] + acc_shapes(STEMS),
        )
        mats, small = (jnp.stack(pair) for pair in zip(grads0, grads1))
    gfeat = jnp.swapaxes(gfeat.reshape(samples, FR, STEPS, D), 1, 2)
    return (
        out.reshape(tokens.shape), gtok.reshape(tokens.shape), gfeat, gprop.transpose(2, 0, 1),
        mats, small
    )


def chunks_of(layer, bounds):
    groups = []
    for start, stop in zip(bounds[:-1], bounds[1:]):
        half = (stop - start) // 32 * 16
        groups.append(
            [(layer, start, half, ("z", "x", "y")), (layer, start + half, stop - start - half, ("z", "y", "x"))]
        )
    return groups


SIZES = {"z": 4, "y": 2, "x": 2, "c": 2}
AXES = ("z", "y", "x", "c")
MESH = pl.DeviceIdType.MESH


def place():
    me = lax.axis_index("fsdp")
    return {"z": me // 8, "y": (me // 4) % 2, "x": (me // 2) % 2, "c": me % 2}


def number(at):
    return ((at["z"] * 2 + at["y"]) * 2 + at["x"]) * 2 + at["c"]


def moved(at, axis, by):
    out = dict(at)
    out[axis] = (at[axis] + by) % SIZES[axis]
    return out


def greet(at):
    barrier = pltpu.get_barrier_semaphore()
    count = 0
    for axis in AXES:
        for by in range(1, SIZES[axis]):
            pl.semaphore_signal(
                barrier, inc=1, device_id=(number(moved(at, axis, by)),), device_id_type=MESH
            )
            count += 1
    pl.semaphore_wait(barrier, count)


def block(ref, at, done, row, count):
    index = tuple(pl.ds(0, SIZES[a]) if a in done else pl.ds(at[a], 1) for a in AXES)
    return ref.at[index + (pl.ds(row, count), slice(None))]


class Gather:
    def __init__(self, at, outs, groups, send_sem, recv_sem):
        self.at, self.outs, self.groups = at, outs, groups
        self.send_sem, self.recv_sem = send_sem, recv_sem

    def copies(self, g, phase, arriving):
        for i, (layer, row, count, order) in enumerate(self.groups[g]):
            order = order + ("c",)
            axis, done = order[phase], order[:phase]
            for by in range(1, SIZES[axis]):
                whose = moved(self.at, axis, -by) if arriving else self.at
                ref = block(self.outs[layer], whose, done, row, count)
                sem = (2 * g + i, AXES.index(axis), by - 1)
                yield pltpu.make_async_remote_copy(
                    ref, ref, self.send_sem.at[sem], self.recv_sem.at[sem],
                    device_id=(number(moved(self.at, axis, by)),), device_id_type=MESH,
                )

    def start(self, g, phase):
        for copy in self.copies(g, phase, False):
            copy.start()

    def land(self, g, phase):
        for copy in self.copies(g, phase, True):
            copy.wait_recv()

    def run(self, moves):
        for g, phase in moves:
            if phase > 0:
                self.land(g, phase - 1)
            if phase < 4:
                self.start(g, phase)

    def close(self):
        for g in range(len(self.groups)):
            for phase in range(4):
                for copy in self.copies(g, phase, False):
                    copy.wait_send()


BOUNDS = (0, 160, 320, 480, ROWS)
HALVES = (0, 320, ROWS)
PROPRIO = None
THIRDS = (0, 256, 448, ROWS)
GATHER_GROUPS = chunks_of(0, BOUNDS)[::-1] + chunks_of(1, THIRDS)
GATHER_FIRST = (
    (0, 0), (1, 0), (0, 1), (2, 0), (1, 1), (0, 2), (3, 0), (2, 1), (1, 2), (0, 3), (4, 0), (3, 1), (2, 2),
    (5, 0), (1, 3), (0, 4), (3, 2), (2, 3), (1, 4), (6, 0), (4, 1), PROPRIO, (3, 3), (2, 4), (5, 1), (3, 4),
)
GATHER_LATER = ((), ((4, 2), (6, 1)), (), ((5, 2),), ((6, 2),), ((4, 3),), (), ((5, 3),))
GATHER_END = ((6, 3), (4, 4), (5, 4), (6, 4))


def place_own(at, shards, outs, local_sem):
    att, up, down, stem, q, pin = shards
    copies = []
    for layer in range(LAYERS):
        own = outs[layer].at[at["z"], at["y"], at["x"], at["c"]]
        pieces = [
            (stem.at[layer, :, pl.ds(j * D, D)], row, D) for j, row in enumerate(MAT_ROWS)
        ] + [
            (q.at[layer], R_Q, SQ), (pin.at[layer], R_PIN, PROP), (att.at[layer], R_ATT, 16),
            (up.at[layer], R_UP, 16), (down.at[layer], R_DOWN, 16),
        ]
        for i, (piece, row, count) in enumerate(pieces):
            copies.append(
                pltpu.make_async_copy(piece, own.at[pl.ds(row, count), :], local_sem.at[layer, i])
            )
    return copies


def gather_forward_kernel(emb_ref, ids_ref, tok_ref, feat_ref, prop_ref, vec_ref, mb_ref, sb_ref, *rest):
    shards, (out_ref, act_ref, slope_ref, g0, g1), rest = rest[:6], rest[6:11], rest[11:]
    saved, (rows_ref, w_ref, local_sem, send_sem, recv_sem, keep_sem) = rest[:-6], rest[-6:]
    step = pl.program_id(0)
    at = place()
    move = Gather(at, (w_ref, g1), GATHER_GROUPS, send_sem, recv_sem)
    keep = pltpu.make_async_copy(w_ref, g0, keep_sem)

    @pl.when(step == 0)
    def _():
        local = place_own(at, shards, (w_ref, g1), local_sem)
        for copy in local:
            copy.start()
        greet(at)
        for copy in local:
            copy.wait()
        for step_ in GATHER_FIRST:
            if step_ is PROPRIO:
                start_forward(0, ids_ref, prop_ref, w_ref, sb_ref, act_ref, slope_ref, rows_ref)
            else:
                move.run((step_,))
        keep.start()

    def moves_at(half):
        for i in range(len(GATHER_LATER) // 2):
            pl.when(step == i)(functools.partial(move.run, GATHER_LATER[2 * i + half]))

    moves_at(0)
    es = [emb_ref[step * SB + j] for j in range(SB)]
    out, kept = forward_block(
        es, tok_ref[...].astype(F32), feat_ref, rows_ref[block_rows(step), :], w_ref,
        *layer_inputs(0, vec_ref, mb_ref), tick=lambda: moves_at(1)
    )
    out_ref[...] = out
    save(kept, saved)

    @pl.when(step == pl.num_programs(0) - 1)
    def _():
        move.run(GATHER_END)
        keep.wait()
        move.close()


def gather_forward(steps, emb, ins, outs, shards):
    assert 2 * steps == len(GATHER_LATER)
    lead = (4, 2, 2, 2, ROWS, D)
    any_spec = pl.BlockSpec(memory_space=pl.ANY)
    smem = pl.BlockSpec(memory_space=pltpu.SMEM)
    weights = jax.ShapeDtypeStruct(lead, BF16)
    ins = ins + [(a, 0) for a in shards]
    specs = [blocked(s, n) if n else whole(s) for s, _, n in outs]
    shapes = [jax.ShapeDtypeStruct(s, d) for s, d, _ in outs]
    groups = 2 * len(GATHER_GROUPS)
    res = pl.pallas_call(
        gather_forward_kernel,
        grid=(steps,),
        in_specs=[smem] + [blocked(a.shape, n) if n else whole(a.shape) for a, n in ins],
        out_specs=specs[:3] + [any_spec, any_spec] + specs[3:],
        out_shape=shapes[:3] + [weights, weights] + shapes[3:],
        scratch_shapes=[
            pltpu.VMEM(outs[2][0], F32),
            pltpu.VMEM(lead, BF16),
            pltpu.SemaphoreType.DMA((LAYERS, 9)),
            pltpu.SemaphoreType.DMA((groups, 4, 3)),
            pltpu.SemaphoreType.DMA((groups, 4, 3)),
            pltpu.SemaphoreType.DMA(()),
        ],
        compiler_params=pltpu.CompilerParams(
            dimension_semantics=("arbitrary",), vmem_limit_bytes=VMEM_LIMIT, collective_id=0,
            has_side_effects=True,
        ),
    )(emb, *[a for a, _ in ins])
    hidden, act, slope, w0, w1, *saved = res
    return (hidden, act, slope, w0.reshape(STEMS, ROWS, D), w1.reshape(STEMS, ROWS, D), *saved)


class Scatter:
    def __init__(self, at, groups, source, acc, lands, out, small, sems):
        self.at, self.groups, self.source, self.acc, self.lands, self.out = at, groups, source, acc, lands, out
        self.send_sem, self.recv_sem, self.small_send, self.small_recv = sems
        self.sm, self.smr, self.smz, self.small_out = small

    def order(self, chunk):
        return ("c",) + chunk[3][::-1]

    def left(self, chunk, phase):
        return [a for a in AXES if a not in self.order(chunk)[: phase + 1]]

    def copies(self, g, phase):
        for i, chunk in enumerate(self.groups[g]):
            _, row, count, _ = chunk
            axis, left = self.order(chunk)[phase], self.left(chunk, phase)
            for by in range(1, SIZES[axis]):
                to = moved(self.at, axis, by)
                src = []
                for a in "zyx":
                    spot = to if a == axis else self.at
                    src.append(pl.ds(0, SIZES[a]) if a in left else spot[a])
                dst = [by - 1] if axis == "z" else [pl.ds(0, SIZES[a]) for a in left]
                source = self.source(to["c"]) if phase == 0 else self.acc
                rows = (pl.ds(row, count), slice(None))
                sem = (2 * g + i, AXES.index(axis), by - 1)
                yield pltpu.make_async_remote_copy(
                    source.at[tuple(src) + rows], self.lands[phase].at[tuple(dst) + rows],
                    self.send_sem.at[sem], self.recv_sem.at[sem],
                    device_id=(number(to),), device_id_type=MESH,
                )

    def add(self, g, phase):
        for chunk in self.groups[g]:
            _, row, count, _ = chunk
            axis, left = self.order(chunk)[phase], self.left(chunk, phase)
            rows = (pl.ds(row, count), slice(None))
            keep = tuple(slice(None) if a in left else self.at[a] for a in "zyx") + rows
            value = self.acc[keep].astype(F32)
            if axis == "z":
                for by in range(SIZES["z"] - 1):
                    value = value + self.lands[3][(by,) + rows].astype(F32)
                self.out[rows] = value
            else:
                land = (slice(None),) * len(left) + rows
                self.acc[keep] = (value + self.lands[phase][land].astype(F32)).astype(BF16)

    def small_copies(self, phase, arriving):
        axis = "cxyz"[phase]
        for by in range(1, SIZES[axis]):
            whose = moved(self.at, axis, -by) if arriving else self.at
            dst = self.smz.at[whose["z"]] if axis == "z" else self.smr.at[phase]
            yield pltpu.make_async_remote_copy(
                self.sm.at[phase], dst, self.small_send.at[phase, by - 1], self.small_recv.at[phase, by - 1],
                device_id=(number(moved(self.at, axis, by)),), device_id_type=MESH,
            )

    def small_add(self, phase):
        if phase < 3:
            self.sm[phase + 1] = self.sm[phase] + self.smr[phase]
        else:
            self.smz[self.at["z"]] = self.sm[phase]
            self.small_out[...] = (self.smz[0] + self.smz[1]) + (self.smz[2] + self.smz[3])

    def run(self, moves):
        for g, phase in moves:
            if phase > 0:
                for copy in self.small_copies(phase - 1, True) if g < 0 else self.copies(g, phase - 1):
                    copy.wait_recv()
                self.small_add(phase - 1) if g < 0 else self.add(g, phase - 1)
            if phase < 4:
                for copy in self.small_copies(phase, False) if g < 0 else self.copies(g, phase):
                    copy.start()

    def close(self):
        for phase in range(4):
            for g in range(len(self.groups)):
                for copy in self.copies(g, phase):
                    copy.wait_send()
            for copy in self.small_copies(phase, False):
                copy.wait_send()


SCATTER_GROUPS = (chunks_of(0, BOUNDS), chunks_of(1, HALVES))
SCATTER_BESIDE = (
    ((-1, 0), (0, 0), (1, 0)),
    ((-1, 1),),
    ((-1, 2), (0, 1), (1, 1)),
    ((-1, 3),),
    ((-1, 4),),
    ((0, 2),),
    (),
    ((1, 2),),
)
SCATTER_END = (
    (0, 0, 0), (1, 0, 3), (0, 1, 0), (0, 0, 1), PROPRIO, (0, -1, 0), (0, 2, 0), (0, 1, 1), (0, -1, 1), (1, 1, 3),
    (0, 0, 2), (0, 3, 0), (0, 2, 1), (0, -1, 2), (0, 1, 2), (0, 0, 3), (0, 3, 1), (0, 2, 2), (0, -1, 3), (1, 0, 4),
    (0, 1, 3), (0, 0, 4), (0, 3, 2), (1, 1, 4), (0, 2, 3), (0, 1, 4), (0, 3, 3), (0, 2, 4), (0, -1, 4), (0, 3, 4),
)


def backward_scatter_kernel(
    emb_ref, before_ref, last_ref, ids_ref, grad_ref, prop_ref, w_ref, vec_ref, gfeat1_ref, gprop1_ref,
    act_ref, slope_ref, *rest
):
    n = len(SAVED)
    saved, (g1, s1), rest = rest[:n], rest[n : n + 2], rest[n + 2 :]
    (gtok_ref, gfeat_ref, gprop_ref, mats_ref, small_ref, grows_ref), rest = rest[:6], rest[6:]
    acc, rest = dict(zip(ACC, rest[: len(ACC)])), rest[len(ACC) :]
    others, sbuf, own_sem = rest[:3]
    per_layer = rest[3:]
    step = pl.program_id(0)
    samples = before_ref.shape[0]
    at = place()

    def scatter_of(layer):
        accum, r0, r1, r2, r3, sm, smr, smz, *sems = per_layer[12 * layer : 12 * (layer + 1)]
        source = (lambda c: g1.at[:, :, :, c]) if layer else (lambda c: sbuf)
        return Scatter(
            at, SCATTER_GROUPS[layer], source, accum, (r0, r1, r2, r3), mats_ref.at[layer],
            (sm, smr, smz, small_ref.at[layer]), sems,
        )

    first, second = scatter_of(0), scatter_of(1)
    own = pltpu.make_async_copy(g1.at[:, :, :, at["c"]], second.acc, own_sem)

    @pl.when(step == 0)
    def _():
        own.start()
        greet(at)
        for name in ACC[1:]:
            acc[name][...] = jnp.zeros(acc[name].shape, F32)
        second.sm[0] = s1[...]
        second.run(SCATTER_BESIDE[0])

    pl.when(step == 1)(own.wait)

    def moves_at(half):
        for i in range(len(SCATTER_BESIDE) // 2):
            if 2 * i + half:
                pl.when(step == i)(functools.partial(second.run, SCATTER_BESIDE[2 * i + half]))

    moves_at(0)
    es = [emb_ref[step * SB + j] for j in range(SB)]
    befores = [before_ref[step * SB + j] for j in range(SB)]
    stem = acc["stem"]

    def add(j, e, pieces):
        for row, value in pieces:
            old = stem[jnp.maximum(befores[j], 0), row : row + value.shape[0], :]
            stem[step * SB + j, row : row + value.shape[0], :] = value + jnp.where(befores[j] >= 0, old, 0.0)

    ghid, gctx, grows = backward_block(
        es, grad_ref[...], load(saved), w_ref, vec_ref[0].astype(F32), {**acc, "add": add},
        lambda: moves_at(1)
    )
    gtok_ref[...] = ghid
    grows_ref[block_rows(step), :] = grows
    write_features(gctx, gfeat1_ref, gfeat_ref)

    def gather_group(g):
        start, stop = BOUNDS[g], BOUNDS[g + 1]

        def line(z, carry):
            for i in range(4):
                spot = (z, i // 2, i % 2)
                for ref, c in ((first.acc, at["c"]), (sbuf, 1 - at["c"])):
                    e = 8 * z + 2 * i + c
                    s = last_ref[e]
                    if start < STEM_ROWS:
                        end = min(stop, STEM_ROWS)
                        value = stem[jnp.maximum(s, 0), start:end, :]
                        ref[spot + (slice(start, end), slice(None))] = jnp.where(s >= 0, value, 0.0).astype(BF16)
                    if stop > STEM_ROWS:
                        begin = max(start, STEM_ROWS)
                        ref[spot + (slice(begin, stop), slice(None))] = others[
                            e, begin - STEM_ROWS : stop - STEM_ROWS, :
                        ]
            return carry

        lax.fori_loop(0, SIZES["z"], line, 0)

    @pl.when(step == pl.num_programs(0) - 1)
    def _():
        for move in SCATTER_END:
            if move is PROPRIO:
                *grads, bias, gprop = proprio_backward(
                    ids_ref, prop_ref, w_ref, act_ref[...], slope_ref[...], grows_ref[...]
                )
                for row, part in other_blocks(acc, grads):
                    row -= STEM_ROWS
                    others[:, row : row + part.shape[1], :] = part
                first.sm[0, 0:16, :] = small_rows(acc)
                first.sm[0, 16:SMALL, :] = bias
                write_proprio(gprop + gprop1_ref[...], gprop_ref)
                continue
            layer, g, phase = move
            if layer == 0 and phase == 0 and g >= 0:
                gather_group(g)
            (first, second)[layer].run(((g, phase),))
        second.close()
        first.close()


def backward_scatter(steps, scalars, ins, outs, g1, s1):
    lead = (4, 2, 2, 2, ROWS, D)
    samples = scalars[0].shape[0]
    smem = pl.BlockSpec(memory_space=pltpu.SMEM)
    any_spec = pl.BlockSpec(memory_space=pl.ANY)
    outs = outs + [((LAYERS, ROWS, D), F32, 0), ((LAYERS, SMALL, D), F32, 0)]
    per_layer = [
        pltpu.VMEM((4, 2, 2, ROWS, D), BF16),
        pltpu.VMEM((4, 2, 2, ROWS, D), BF16),
        pltpu.VMEM((4, 2, ROWS, D), BF16),
        pltpu.VMEM((4, ROWS, D), BF16),
        pltpu.VMEM((3, ROWS, D), BF16),
        pltpu.VMEM((4, SMALL, D), F32),
        pltpu.VMEM((3, SMALL, D), F32),
        pltpu.VMEM((4, SMALL, D), F32),
        pltpu.SemaphoreType.DMA((2 * len(BOUNDS), 4, 3)),
        pltpu.SemaphoreType.DMA((2 * len(BOUNDS), 4, 3)),
        pltpu.SemaphoreType.DMA((4, 3)),
        pltpu.SemaphoreType.DMA((4, 3)),
    ]
    return pl.pallas_call(
        backward_scatter_kernel,
        grid=(steps,),
        in_specs=[smem] * 3 + [blocked(a.shape, n) if n else whole(a.shape) for a, n in ins]
        + [any_spec, whole(s1.shape)],
        out_specs=[blocked(s, n) if n else whole(s) for s, _, n in outs],
        out_shape=[jax.ShapeDtypeStruct(s, d) for s, d, _ in outs],
        scratch_shapes=[pltpu.VMEM((STEPS * samples, D), F32)] + acc_shapes(samples)
        + [
            pltpu.VMEM((STEMS, ROWS - STEM_ROWS, D), BF16),
            pltpu.VMEM((4, 2, 2, ROWS, D), BF16),
            pltpu.SemaphoreType.DMA(()),
        ]
        + per_layer * LAYERS,
        compiler_params=pltpu.CompilerParams(
            dimension_semantics=("arbitrary",), vmem_limit_bytes=VMEM_LIMIT, collective_id=1,
            has_side_effects=True,
        ),
    )(*scalars, *[a for a, _ in ins], g1.reshape(lead), s1)


def unpack_kernel(mats, small, gtok_in, gfeat_in, gtok, gfeat, att, up, down, stem, q, pin, vec, mb, sb):
    gtok[...] = gtok_in[...]
    gfeat[...] = gfeat_in[...]
    pl.when(pl.program_id(0) == 0)(
        lambda: split_gradients(mats, small, att, up, down, stem, q, pin, vec, mb, sb)
    )


def split_gradients(mats, small, att, up, down, stem, q, pin, vec, mb, sb):
    for layer in range(LAYERS):
        for j, row in enumerate(MAT_ROWS):
            stem[layer, :, j * D : (j + 1) * D] = mats[layer, row : row + D, :]
        q[layer] = mats[layer, R_Q:R_WP, :]
        pin[layer] = mats[layer, R_PIN:R_ATT, :]
        att[layer] = mats[layer, R_ATT:R_UP, :]
        up[layer] = mats[layer, R_UP:R_DOWN, :]
        down[layer] = mats[layer, R_DOWN:ROWS, :]
        vec[layer] = small[layer, 0:8, :]
        for i in range(4):
            mb[layer : layer + 1, i * D : (i + 1) * D] = small[layer, 8 + i : 9 + i, :]
        sb[layer] = small[layer, 16:SMALL, :]


def unpack(mats, small, gtok, gfeat):
    outs = [
        (LAYERS, 16, D), (LAYERS, 16, D), (LAYERS, 16, D), (LAYERS, D, 4 * D), (LAYERS, SQ, D),
        (LAYERS, PROP, D), (LAYERS, 8, D), (LAYERS, FF), (LAYERS, 2 * STEMS, D),
    ]
    steps = 2
    moved_through = [blocked(a.shape, a.shape[0] // steps) for a in (gtok, gfeat)]
    return pl.pallas_call(
        unpack_kernel,
        grid=(steps,),
        out_shape=[jax.ShapeDtypeStruct(s, F32) for s in [gtok.shape, gfeat.shape] + outs],
        in_specs=[whole(mats.shape), whole(small.shape)] + moved_through,
        out_specs=moved_through + [whole(s) for s in outs],
        compiler_params=pltpu.CompilerParams(
            dimension_semantics=("arbitrary",), vmem_limit_bytes=VMEM_LIMIT
        ),
    )(mats, small, gtok, gfeat)


def pack(attn, up, down, stem, queries, pin):
    gathered = [lax.all_gather(a, "fsdp", axis=1, tiled=True) for a in (attn, up, down, stem, queries, pin)]
    attn, up, down, stem, queries, pin = gathered
    stem = stem.reshape(LAYERS, STEMS, D, 4, D).transpose(0, 1, 3, 2, 4).reshape(LAYERS, STEMS, 4 * D, D)
    queries, *parts = [a.reshape(LAYERS, STEMS, -1, D) for a in (queries, pin, attn, up, down)]
    return jnp.concatenate([stem[:, :, : 3 * D], queries, stem[:, :, 3 * D :], *parts], 2)


def unpack_blocks(grad):
    stem = jnp.concatenate([grad[..., row : row + D, :] for row in MAT_ROWS], -1)
    return (
        grad[..., R_ATT:R_UP, :], grad[..., R_UP:R_DOWN, :], grad[..., R_DOWN:ROWS, :],
        stem, grad[..., R_Q:R_WP, :], grad[..., R_PIN:R_ATT, :],
    )


def body(n, tokens, features, proprio, embodiment, trunk_attn, feedforward_up_weight, mlp_down,
         stem_mats, stem_queries, prop_in, trunk_vectors, mlp_bias, stem_bias, cotangent):
    shards = (trunk_attn, feedforward_up_weight, mlp_down, stem_mats, stem_queries, prop_in)
    out, gtok, gfeat, gprop, mats, small = compute(
        tokens, features, proprio, embodiment, shards, trunk_vectors, mlp_bias, stem_bias,
        cotangent, None if n == 32 else pack(*shards),
    )
    if n == 32:
        return (out, gtok, gfeat, gprop, *mats, small.reshape(LAYERS, STEMS, 2, D))
    mats = [
        lax.psum_scatter(a.reshape(LAYERS, -1, a.shape[-1]), "fsdp", scatter_dimension=1, tiled=True)
        for a in unpack_blocks(mats.astype(F32))
    ]
    small = lax.psum(small, "fsdp")
    gvec = small[:, :8]
    gmb = small[:, 8:12].reshape(LAYERS, FF)
    gsb = small[:, 16:].reshape(LAYERS, STEMS, 2, D)
    return (out, gtok, gfeat, gprop, *mats, gvec, gmb, gsb)


def solution(mesh):
    n = mesh.shape["fsdp"]
    return jax.shard_map(
        functools.partial(body, n),
        mesh=mesh,
        in_specs=(
            P("fsdp"), P("fsdp"), P("fsdp"), P("fsdp"),
            P(None, "fsdp"), P(None, "fsdp"), P(None, "fsdp"), P(None, "fsdp"), P(None, "fsdp"),
            P(None, "fsdp"), P(), P(), P(), P("fsdp"),
        ),
        out_specs=(
            P("fsdp"), P("fsdp"), P("fsdp"), P("fsdp"),
            P(None, "fsdp"), P(None, "fsdp"), P(None, "fsdp"), P(None, "fsdp"), P(None, "fsdp"),
            P(None, "fsdp"), P(), P(), P(),
        ),
        check_vma=False,
    )
```

```python
import functools
import math

import jax
import jax.numpy as jnp
from jax import lax
from jax.experimental import pallas as pl
from jax.experimental.pallas import tpu as pltpu
from jax.sharding import PartitionSpec as P

D = 128
HEADS = 8
HD = 16
FF = 512
SQ = 16
FR = 49
CR = 112
PROP = 32
STEMS = 32
STEPS = 2
LAYERS = 2
TOK = 32
SB = 16

R_Q = 3 * D
R_WP = R_Q + SQ
R_PIN = R_WP + D
R_ATT = R_PIN + PROP
R_UP = R_ATT + 16
R_DOWN = R_UP + 16
ROWS = R_DOWN + 16
STEM_ROWS = R_WP
SMALL = 16 + 2 * STEMS

MAT_ROWS = (0, D, 2 * D, R_WP)

F32 = jnp.float32
BF16 = jnp.bfloat16
VMEM_LIMIT = 60 * 1024 * 1024


def dot(a, b):
    return lax.dot_general(a, b, (((1,), (0,)), ((), ())), preferred_element_type=F32)


def dot_nt(a, b):
    return lax.dot_general(a, b, (((1,), (1,)), ((), ())), preferred_element_type=F32)


def dot_tn(a, b):
    return lax.dot_general(a, b, (((0,), (0,)), ((), ())), preferred_element_type=F32)


def gelu_parts(x):
    cdf = 0.5 + 0.5 * lax.erf(x * math.sqrt(0.5))
    slope = cdf + x * (jnp.exp(-0.5 * x * x) * (1.0 / math.sqrt(2.0 * math.pi)))
    return x * cdf, slope


def norm_parts(x):
    centred = x - jnp.mean(x, -1, keepdims=True)
    inverse = lax.rsqrt(jnp.mean(centred * centred, -1, keepdims=True) + 1e-05)
    return centred * inverse, inverse


def norm_back(grad, gain, hat, inverse):
    g = grad * gain
    return inverse * (
        g - jnp.mean(g, -1, keepdims=True) - hat * jnp.mean(g * hat, -1, keepdims=True)
    )


def head_mask(rows, value):
    row = lax.broadcasted_iota(jnp.int32, (HEADS * rows, D), 0) // rows
    lane = lax.broadcasted_iota(jnp.int32, (HEADS * rows, D), 1) // HD
    return jnp.where(row == lane, value, 0.0).astype(BF16)


def expand(rows, mask):
    return jnp.concatenate([rows] * HEADS, 0) * mask


def contract(wide, rows):
    lane = lax.broadcasted_iota(jnp.int32, (rows, D), 1) // HD
    out = wide[:rows]
    for head in range(1, HEADS):
        out = jnp.where(lane == head, wide[head * rows : (head + 1) * rows], out)
    return out


def fold(x):
    return jnp.sum(x.reshape(x.shape[0] // 8, 8, x.shape[1]), 0)


def slot(w_ref, e, start, stop):
    if len(w_ref.shape) == 3:
        return w_ref[e, start:stop, :]
    return w_ref[e // 8, (e // 4) % 2, (e // 2) % 2, e % 2, start:stop, :]


def all_slots(w_ref, start, stop):
    index = (slice(None),) * (len(w_ref.shape) - 2)
    return w_ref[index + (slice(start, stop), slice(None))].reshape(STEMS * (stop - start), D)


def trunk_weights(w_ref):
    attn = all_slots(w_ref, R_ATT, R_UP)
    up = all_slots(w_ref, R_UP, R_DOWN)
    down = all_slots(w_ref, R_DOWN, ROWS)
    wqkv = jnp.concatenate([attn[:D], attn[D : 2 * D], attn[2 * D : 3 * D]], 1)
    return wqkv, attn[3 * D :], up, down


def stem_kv_weight(w_ref, e):
    return jnp.concatenate([slot(w_ref, e, 0, D), slot(w_ref, e, D, 2 * D)], 1)


def step_reduce(x, op):
    x = x.reshape(x.shape[0] // 8, 8, x.shape[1])
    out = x[0]
    for i in range(1, x.shape[0]):
        out = op(out, x[i])
    out = op(out, pltpu.roll(out, 4, 0))
    return op(out, pltpu.roll(out, 2, 0))


def step_apply(x, y, op):
    return op(x.reshape(x.shape[0] // 8, 8, x.shape[1]), y[None]).reshape(x.shape)


def step_masks():
    odd = lax.broadcasted_iota(jnp.int32, (CR, D), 0) % 2
    return (odd == 0).astype(BF16), odd.astype(BF16)


def split_steps(p, masks):
    return jnp.concatenate([p * masks[0], p * masks[1]], 1)


def softmax_rows(score):
    top = jnp.max(score, 0, keepdims=True)
    weight = jnp.exp(score - top)
    return weight * (1.0 / jnp.sum(weight, 0, keepdims=True))


def stem_ids(emb_ref, rows, down=False):
    samples = emb_ref.shape[1]
    row = lax.broadcasted_iota(jnp.int32, (rows, samples), 0) // STEPS
    pick = (row == lax.broadcasted_iota(jnp.int32, (rows, samples), 1)).astype(BF16)
    stems = jnp.broadcast_to(emb_ref[...].astype(F32).astype(BF16), (D, samples))
    return dot_nt(stems, pick) if down else dot_nt(pick, stems)


def spread(values, ids):
    values = values.astype(F32)
    return jnp.concatenate([jnp.where(ids == e, values, 0.0).astype(BF16) for e in range(STEMS)], 1)


def sample_rows(samples):
    shape = (samples * STEPS, samples * STEPS)
    row = lax.broadcasted_iota(jnp.int32, shape, 0)
    column = (row % STEPS) * samples + row // STEPS
    return (lax.broadcasted_iota(jnp.int32, shape, 1) == column).astype(BF16)


def spread_down(values, ids):
    values = values.astype(F32)
    return jnp.concatenate([jnp.where(ids == e, values, 0.0).astype(BF16) for e in range(STEMS)], 0)


def spread_proprio(prop_ref, ids, down=False):
    both = jnp.concatenate([prop_ref[t] for t in range(STEPS)], 1)
    group = D // PROP
    tiled = jnp.concatenate([both] * group, 0)
    place_ = sample_rows(prop_ref.shape[2])
    rows = dot_nt(tiled, place_) if down else dot_nt(place_, tiled)
    entry = (lax.broadcasted_iota(jnp.int32, rows.shape, 0 if down else 1) // PROP).astype(F32)
    return jnp.concatenate(
        [jnp.where(ids == entry + float(group * b), rows, 0.0).astype(BF16) for b in range(STEMS // group)],
        0 if down else 1,
    )


def bias_picks(ids):
    lane = lax.broadcasted_iota(jnp.int32, (ids.shape[0], 2 * STEMS), 1).astype(F32)
    twice = 2.0 * ids[:, : 2 * STEMS]
    return (lane == twice).astype(BF16), (lane == twice + 1.0).astype(BF16)


def proprio_forward(emb_ref, prop_ref, w_ref, biases):
    ids = stem_ids(emb_ref, STEPS * emb_ref.shape[1])
    first, second = bias_picks(ids)
    pre = dot(spread_proprio(prop_ref, ids), all_slots(w_ref, R_PIN, R_ATT)) + dot(first, biases)
    act, slope = gelu_parts(pre)
    act = act.astype(BF16)
    return act, slope, dot(spread(act, ids), all_slots(w_ref, R_WP, R_PIN)) + dot(second, biases)


def proprio_backward(emb_ref, prop_ref, w_ref, act, slope, grad_rows):
    ids = stem_ids(emb_ref, STEPS * emb_ref.shape[1])
    first, second = bias_picks(ids)
    low = grad_rows.astype(BF16)
    wp = jnp.concatenate([slot(w_ref, e, R_WP, R_PIN) for e in range(STEMS)], 1)
    pin = jnp.concatenate([slot(w_ref, e, R_PIN, R_ATT) for e in range(STEMS)], 1)
    grad_pre = (dot_nt(spread(low, ids), wp) * slope).astype(BF16)
    down = stem_ids(emb_ref, STEPS * emb_ref.shape[1], True)
    return (
        dot(spread_down(act.astype(F32).T, down), low), dot(spread_proprio(prop_ref, down, True), grad_pre),
        dot_tn(first, grad_pre) + dot_tn(second, low), dot_nt(spread(grad_pre, ids), pin),
    )


def forward_block(es, hidden, feat_ref, prows, w_ref, vec, mb, tick=None):
    kept = {}
    row8 = lax.broadcasted_iota(jnp.int32, (8, D), 0)
    contexts = []
    for j in range(SB):
        rows = feat_ref[j * STEPS * FR : (j + 1) * STEPS * FR, :]
        last = jnp.concatenate([rows[96:98], jnp.zeros((14, D), BF16)], 0).astype(F32)[:8]
        k = j // 4 * 8
        mine = pltpu.roll(prows[k : k + 8], (2 - 2 * (j % 4)) % 8, 0)
        tail = jnp.where(row8 < 2, last, jnp.where(row8 < 4, mine, 0.0))
        tail = jnp.concatenate([tail, jnp.zeros((8, D), F32)], 0).astype(BF16)
        contexts.append(jnp.concatenate([rows[:96], tail], 0))
    kept["ctx"] = contexts
    kvs = [dot(contexts[j], stem_kv_weight(w_ref, e)).astype(BF16) for j, e in enumerate(es)]
    kept["kv"] = kvs
    mask16 = head_mask(SQ, 0.25)
    scores = [
        dot_nt(kvs[j][:, :D], expand(slot(w_ref, e, R_Q, R_WP), mask16)) for j, e in enumerate(es)
    ]
    valid = lax.broadcasted_iota(jnp.int32, (104, D), 0) < STEPS * (FR + 1)
    pad = jnp.zeros((8, D), F32)
    probs = []
    for j in range(SB):
        s = jnp.where(valid, scores[j][:104], -1e30)
        weight = jnp.exp(step_apply(s, step_reduce(s, jnp.maximum), jnp.subtract))
        scale = 1.0 / step_reduce(weight, jnp.add)
        probs.append(jnp.concatenate([step_apply(weight, scale, jnp.multiply), pad], 0))
    kept["prob"] = probs
    masks = step_masks()
    mixes = []
    for j in range(SB):
        wide = dot_tn(split_steps(probs[j].astype(BF16), masks), kvs[j][:, D:])
        mixes += [contract(wide[t * D : (t + 1) * D], SQ).astype(BF16) for t in range(STEPS)]
    mix = jnp.concatenate(mixes, 0)
    kept["mix"] = mix
    if tick is not None:
        tick()
    outs = [
        dot(mix[j * TOK : (j + 1) * TOK], slot(w_ref, e, 2 * D, 3 * D)) for j, e in enumerate(es)
    ]
    first = hidden + jnp.concatenate(outs, 0)
    kept["first"] = first
    wqkv, wout, up, down = trunk_weights(w_ref)
    normed = (norm_parts(first)[0] * vec[0:1] + vec[1:2]).astype(BF16)
    bias = jnp.concatenate([vec[2:3], jnp.zeros((1, D), F32), vec[3:4]], 1)
    qkv = (dot(normed, wqkv) + bias).astype(BF16)
    kept["qkv"] = qkv
    mask32 = head_mask(TOK, 0.25)
    rows = [qkv[j * TOK : (j + 1) * TOK] for j in range(SB)]
    scores = [dot_nt(rows[j][:, D : 2 * D], expand(rows[j][:, :D], mask32)) for j in range(SB)]
    sprobs = [softmax_rows(s) for s in scores]
    smixes = [
        contract(dot_tn(sprobs[j].astype(BF16), rows[j][:, 2 * D :]), TOK).astype(BF16)
        for j in range(SB)
    ]
    kept["sprob"] = sprobs
    smix = jnp.concatenate(smixes, 0)
    kept["smix"] = smix
    second = first + (dot(smix, wout) + vec[4:5])
    kept["second"] = second
    mlp_in = (norm_parts(second)[0] * vec[5:6] + vec[6:7]).astype(BF16)
    act, slope = gelu_parts(dot_nt(mlp_in, up) + mb)
    act = act.astype(BF16)
    kept["act"], kept["slope"] = act, slope
    return second + (dot(act, down) + vec[7:8]), kept


def backward_block(es, grad, kept, w_ref, vec, acc, tick=None):
    wqkv, wout, up, down = trunk_weights(w_ref)
    out_low = grad.astype(BF16)
    acc["vec"][7] += fold(out_low.astype(F32))
    acc["down"][...] += dot_tn(out_low, kept["act"])
    grad_act = dot_nt(out_low, down)
    grad_pre = (grad_act * kept["slope"].astype(F32)).astype(BF16)
    acc["mb"][...] += fold(grad_pre.astype(F32))
    hat, inverse = norm_parts(kept["second"])
    mlp_in = (hat * vec[5:6] + vec[6:7]).astype(BF16)
    acc["up"][...] += dot_tn(mlp_in, grad_pre)
    grad_in = dot(grad_pre, up)
    acc["vec"][5] += fold(grad_in * hat)
    acc["vec"][6] += fold(grad_in)
    grad_second = grad + norm_back(grad_in, vec[5:6], hat, inverse)
    branch = grad_second.astype(BF16)
    acc["vec"][4] += fold(branch.astype(F32))
    acc["wout"][...] += dot_tn(kept["smix"], branch)
    grad_mix = dot_nt(branch, wout).astype(BF16)
    mask32 = head_mask(TOK, 0.25)
    mask32_one = head_mask(TOK, 1.0)
    rows = [kept["qkv"][j * TOK : (j + 1) * TOK] for j in range(SB)]
    wides = [expand(grad_mix[j * TOK : (j + 1) * TOK], mask32_one) for j in range(SB)]
    grad_ps = [dot_nt(rows[j][:, 2 * D :], wides[j]) for j in range(SB)]
    grads_v = [dot(kept["sprob"][j].astype(BF16), wides[j]) for j in range(SB)]
    gss = []
    for j in range(SB):
        p = kept["sprob"][j].astype(F32)
        gss.append((p * (grad_ps[j] - jnp.sum(grad_ps[j] * p, 0, keepdims=True))).astype(BF16))
    grads_q = [contract(dot_tn(gss[j], rows[j][:, D : 2 * D]), TOK) * 0.25 for j in range(SB)]
    grads_k = [dot(gss[j], expand(rows[j][:, :D], mask32)) for j in range(SB)]
    grad_qkv = jnp.concatenate(
        [jnp.concatenate(g, 0).astype(BF16) for g in (grads_q, grads_k, grads_v)], 1
    )
    acc["vec"][2] += fold(grad_qkv[:, :D].astype(F32))
    acc["vec"][3] += fold(grad_qkv[:, 2 * D :].astype(F32))
    hat, inverse = norm_parts(kept["first"])
    normed = (hat * vec[0:1] + vec[1:2]).astype(BF16)
    acc["wqkv"][...] += dot_tn(normed, grad_qkv)
    grad_normed = dot_nt(grad_qkv, wqkv)
    acc["vec"][0] += fold(grad_normed * hat)
    acc["vec"][1] += fold(grad_normed)
    grad_first = grad_second + norm_back(grad_normed, vec[0:1], hat, inverse)
    stem_grad = grad_first.astype(BF16)
    mask16 = head_mask(SQ, 0.25)
    mask16_one = head_mask(SQ, 1.0)
    row8 = lax.broadcasted_iota(jnp.int32, (8, D), 0)
    if tick is not None:
        tick()
    gs_in = [stem_grad[j * TOK : (j + 1) * TOK] for j in range(SB)]
    gmixes = [dot_nt(gs_in[j], slot(w_ref, e, 2 * D, 3 * D)).astype(BF16) for j, e in enumerate(es)]
    grad_wo = [dot_tn(kept["mix"][j * TOK : (j + 1) * TOK], gs_in[j]) for j in range(SB)]
    kvs = [kept["kv"][j] for j in range(SB)]
    probs = [kept["prob"][j] for j in range(SB)]
    wides = [
        jnp.concatenate(
            [expand(gmixes[j][t * SQ : (t + 1) * SQ], mask16_one) for t in range(STEPS)], 0
        )
        for j in range(SB)
    ]
    grad_ps = [dot_nt(kvs[j][:, D:], wides[j]) for j in range(SB)]
    masks = step_masks()
    gvs = [dot(split_steps(probs[j].astype(BF16), masks), wides[j]) for j in range(SB)]
    even = lax.broadcasted_iota(jnp.int32, (104, D), 0) % 2 == 0
    pad = jnp.zeros((8, D), F32)
    gss = []
    for j in range(SB):
        p = probs[j][:104].astype(F32)
        gp = jnp.where(even, grad_ps[j][:104, :D], grad_ps[j][:104, D:])
        gs = p * step_apply(gp, step_reduce(gp * p, jnp.add), jnp.subtract)
        gss.append(jnp.concatenate([gs, pad], 0).astype(BF16))
    gks = [dot(gss[j], expand(slot(w_ref, e, R_Q, R_WP), mask16)) for j, e in enumerate(es)]
    gkvs = [
        jnp.concatenate([gks[j], gvs[j]], 1).astype(BF16) for j in range(SB)
    ]
    grad_contexts = [
        dot_nt(gkvs[j], stem_kv_weight(w_ref, e)).astype(BF16) for j, e in enumerate(es)
    ]
    grad_prows = []
    for k in range(0, SB, 4):
        rows = jnp.zeros((8, D), F32)
        for j in range(k, k + 4):
            tail = pltpu.roll(grad_contexts[j][96:112].astype(F32)[:8], (2 * (j % 4) - 2) % 8, 0)
            rows = jnp.where(row8 // 2 == j % 4, tail, rows)
        grad_prows.append(rows)
    grad_q = [contract(dot_tn(gss[j], kvs[j][:, :D]), SQ) * 0.25 for j in range(SB)]
    grad_wkv = [dot_tn(kept["ctx"][j], gkvs[j]) for j in range(SB)]
    for j, e in enumerate(es):
        acc["add"](
            j, e,
            ((0, grad_wkv[j][:, :D]), (D, grad_wkv[j][:, D:]), (2 * D, grad_wo[j]), (R_Q, grad_q[j])),
        )
    return grad_first, grad_contexts, jnp.concatenate(grad_prows, 0)


ACC = ("stem", "wqkv", "wout", "up", "down", "vec", "mb")


def acc_shapes(entries):
    return [
        pltpu.VMEM((entries, STEM_ROWS, D), F32),
        pltpu.VMEM((D, 3 * D), F32),
        pltpu.VMEM((D, D), F32),
        pltpu.VMEM((D, FF), F32),
        pltpu.VMEM((D, FF), F32),
        pltpu.VMEM((8, 8, D), F32),
        pltpu.VMEM((8, FF), F32),
    ]


def clear(acc):
    for ref in acc.values():
        ref[...] = jnp.zeros(ref.shape, ref.dtype)


def add_in_place(acc):
    def add(j, e, pieces):
        for row, value in pieces:
            acc["stem"][e, row : row + value.shape[0], :] += value

    return {**acc, "add": add}


def trunk_blocks(acc):
    wqkv = acc["wqkv"][...]
    attn = [wqkv[:, :D], wqkv[:, D : 2 * D], wqkv[:, 2 * D :], acc["wout"][...]]
    return (
        jnp.concatenate(attn, 0).astype(BF16).reshape(STEMS, 16, D),
        acc["up"][...].T.astype(BF16).reshape(STEMS, 16, D),
        acc["down"][...].T.astype(BF16).reshape(STEMS, 16, D),
    )


def small_rows(acc):
    mb = jnp.sum(acc["mb"][...], 0, keepdims=True)
    return jnp.concatenate(
        [jnp.sum(acc["vec"][...], 1)] + [mb[:, i * D : (i + 1) * D] for i in range(4)]
        + [jnp.zeros((4, D), F32)], 0
    )


def other_blocks(acc, grads):
    grad_wp, grad_pin = grads
    return (
        (R_WP, grad_wp.astype(BF16).reshape(STEMS, D, D)),
        (R_PIN, grad_pin.astype(BF16).reshape(STEMS, PROP, D)),
    ) + tuple((R_ATT + 16 * i, part) for i, part in enumerate(trunk_blocks(acc)))


def finish(acc, grads, bias, grad_ref, small_ref):
    def stem_out(e, carry):
        grad_ref[e, 0:STEM_ROWS, :] = acc["stem"][e].astype(grad_ref.dtype)
        return carry

    lax.fori_loop(0, STEMS, stem_out, 0)
    for start, part in other_blocks(acc, grads):
        grad_ref[:, start : start + part.shape[1], :] = part
    small_ref[0:16, :] = small_rows(acc)
    small_ref[16:SMALL, :] = bias


SAVED = ("ctx", "kv", "prob", "mix", "first", "qkv", "sprob", "smix", "second", "act", "slope")
PER_SAMPLE = ("ctx", "kv", "prob", "sprob")


def saved_shapes(samples):
    rows = samples * TOK
    return dict(
        ctx=((samples, CR, D), BF16),
        kv=((samples, CR, 2 * D), BF16),
        prob=((samples, CR, D), BF16),
        mix=((rows, D), BF16),
        first=((rows, D), F32),
        qkv=((rows, 3 * D), BF16),
        sprob=((samples, TOK, HEADS * TOK), BF16),
        smix=((rows, D), BF16),
        second=((rows, D), F32),
        act=((rows, FF), BF16),
        slope=((rows, FF), BF16),
    )


def layer_inputs(layer, vec_ref, mb_ref):
    return vec_ref[layer].astype(F32), mb_ref[layer : layer + 1, :].astype(F32)


def start_forward(layer, emb_ref, prop_ref, w_ref, sb_ref, act_ref, slope_ref, rows_ref):
    act_ref[...], slope_ref[...], rows_ref[...] = proprio_forward(emb_ref, prop_ref, w_ref, sb_ref[layer])


def block_rows(step):
    return pl.ds(pl.multiple_of(step * SB * STEPS, SB * STEPS), SB * STEPS)


def save(kept, saved):
    for name, ref in zip(SAVED, saved):
        if name in PER_SAMPLE:
            for j in range(SB):
                ref[j] = kept[name][j].astype(ref.dtype)
        else:
            ref[...] = kept[name].astype(ref.dtype)


def load(saved):
    return {
        name: [ref[j] for j in range(SB)] if name in PER_SAMPLE else ref[...]
        for name, ref in zip(SAVED, saved)
    }


def forward_kernel(
    emb_ref, ids_ref, tok_ref, feat_ref, prop_ref, w_ref, vec_ref, mb_ref, sb_ref, out_ref, act_ref, slope_ref, *rest
):
    saved, rows_ref = rest[:-1], rest[-1]
    step = pl.program_id(0)
    pl.when(step == 0)(
        lambda: start_forward(0, ids_ref, prop_ref, w_ref, sb_ref, act_ref, slope_ref, rows_ref)
    )
    es = [emb_ref[step * SB + j] for j in range(SB)]
    out, kept = forward_block(
        es, tok_ref[...].astype(F32), feat_ref, rows_ref[block_rows(step), :], w_ref,
        *layer_inputs(0, vec_ref, mb_ref)
    )
    out_ref[...] = out
    save(kept, saved)


def link_samples(emb_ref, before_ref, last_ref):
    def unset(e, carry):
        last_ref[e] = -1
        return carry

    def link(s, carry):
        e = emb_ref[s]
        before_ref[s] = last_ref[e]
        last_ref[e] = s
        return carry

    lax.fori_loop(0, STEMS, unset, 0)
    lax.fori_loop(0, before_ref.shape[0], link, 0)


def middle_kernel(
    emb_ref, ids_ref, hid_ref, feat_ref, prop_ref, w_ref, vec_ref, mb_ref, sb_ref, cot_ref,
    out_ref, ghid_ref, gfeat_ref, gprop_ref, gw_ref, gsmall_ref, before_ref, last_ref,
    act_ref, slope_ref, rows_ref, grows_ref, *accs
):
    step = pl.program_id(0)
    acc = dict(zip(ACC, accs))

    @pl.when(step == 0)
    def _():
        clear(acc)
        link_samples(emb_ref, before_ref, last_ref)
        start_forward(1, ids_ref, prop_ref, w_ref, sb_ref, act_ref, slope_ref, rows_ref)

    es = [emb_ref[step * SB + j] for j in range(SB)]
    vec, mb = layer_inputs(1, vec_ref, mb_ref)
    out, kept = forward_block(
        es, hid_ref[...], feat_ref, rows_ref[block_rows(step), :], w_ref, vec, mb
    )
    out_ref[...] = out.astype(BF16)
    ghid, gctx, grows = backward_block(
        es, cot_ref[...].astype(F32), kept, w_ref, vec, add_in_place(acc)
    )
    ghid_ref[...] = ghid
    grows_ref[block_rows(step), :] = grows
    for j in range(SB):
        gfeat_ref[j] = gctx[j]

    @pl.when(step == pl.num_programs(0) - 1)
    def _():
        *grads, bias, gprop_ref[...] = proprio_backward(
            ids_ref, prop_ref, w_ref, act_ref[...], slope_ref[...], grows_ref[...]
        )
        finish(acc, grads, bias, gw_ref, gsmall_ref)


def write_features(gctx, gfeat1_ref, gfeat_ref):
    for j in range(0, SB, 4):
        totals = [gctx[i].astype(F32) + gfeat1_ref[i].astype(F32) for i in range(j, j + 4)]
        gfeat_ref[j * STEPS * FR : (j + 4) * STEPS * FR, :] = jnp.concatenate(
            [total[: STEPS * FR] for total in totals], 0
        )


def write_proprio(rows, gprop_ref):
    samples = gprop_ref.shape[2]
    place_ = sample_rows(samples)
    high = rows.astype(BF16)
    rest = rows - high.astype(F32)
    middle = rest.astype(BF16)
    low = (rest - middle.astype(F32)).astype(BF16)
    out = dot_tn(high, place_) + (dot_tn(middle, place_) + dot_tn(low, place_))
    for t in range(STEPS):
        gprop_ref[t] = out[:, t * samples : (t + 1) * samples]


def backward_kernel(
    emb_ref, ids_ref, grad_ref, prop_ref, w_ref, vec_ref, gfeat1_ref, gprop1_ref, act_ref, slope_ref, *rest
):
    n = len(SAVED)
    saved = rest[:n]
    gtok_ref, gfeat_ref, gprop_ref, gw_ref, gsmall_ref, grows_ref = rest[n : n + 6]
    acc = dict(zip(ACC, rest[n + 6 :]))
    step = pl.program_id(0)
    pl.when(step == 0)(lambda: clear(acc))
    es = [emb_ref[step * SB + j] for j in range(SB)]
    vec = vec_ref[0].astype(F32)
    ghid, gctx, grows = backward_block(es, grad_ref[...], load(saved), w_ref, vec, add_in_place(acc))
    gtok_ref[...] = ghid
    grows_ref[block_rows(step), :] = grows
    write_features(gctx, gfeat1_ref, gfeat_ref)

    @pl.when(step == pl.num_programs(0) - 1)
    def _():
        *grads, bias, gprop = proprio_backward(
            ids_ref, prop_ref, w_ref, act_ref[...], slope_ref[...], grows_ref[...]
        )
        finish(acc, grads, bias, gw_ref, gsmall_ref)
        write_proprio(gprop + gprop1_ref[...], gprop_ref)


def blocked(shape, per_step):
    block = (per_step,) + tuple(shape[1:])
    zeros = (0,) * (len(shape) - 1)
    return pl.BlockSpec(block, lambda i, *_: (i,) + zeros)


def whole(shape):
    zeros = (0,) * len(shape)
    return pl.BlockSpec(tuple(shape), lambda i, *_: zeros, pipeline_mode=pl.Buffered(1))


def call(kernel, steps, emb, ins, outs, scratch):
    return pl.pallas_call(
        kernel,
        grid_spec=pltpu.PrefetchScalarGridSpec(
            num_scalar_prefetch=1,
            grid=(steps,),
            in_specs=[blocked(a.shape, n) if n else whole(a.shape) for a, n in ins],
            out_specs=[
                pl.BlockSpec(memory_space=pltpu.SMEM) if n is None else blocked(s, n) if n else whole(s)
                for s, _, n in outs
            ],
            scratch_shapes=scratch,
        ),
        out_shape=[jax.ShapeDtypeStruct(s, d) for s, d, _ in outs],
        compiler_params=pltpu.CompilerParams(
            dimension_semantics=("arbitrary",), vmem_limit_bytes=VMEM_LIMIT
        ),
    )(emb, *[a for a, _ in ins])


def compute(tokens, features, proprio, emb, shards, vecs, mbs, sbs, cot, weights=None):
    samples = emb.shape[0]
    steps = samples // SB
    rows = samples * TOK
    rb = SB * TOK
    tok = tokens.reshape(rows, D)
    feat = jnp.swapaxes(features, 1, 2).reshape(samples * FR * STEPS, D)
    prop = proprio.transpose(1, 2, 0)
    ids = emb.reshape(1, samples)
    sbs = sbs.reshape(LAYERS, 2 * STEMS, D)
    fb = SB * FR * STEPS
    prows = (STEPS * samples, D)
    shapes = saved_shapes(samples)
    per = lambda s: s[0] // steps
    forward_ins = [(ids, 0), (tok, rb), (feat, fb), (prop, 0), (vecs, 0), (mbs, 0), (sbs, 0)]
    forward_outs = [((rows, D), F32, rb), (prows, BF16, 0), (prows, F32, 0)] + [
        (shapes[n][0], shapes[n][1], per(shapes[n][0])) for n in SAVED
    ]
    if weights is None:
        hidden, act, slope, w0, w1, *saved = gather_forward(steps, emb, forward_ins, forward_outs, shards)
    else:
        w0, w1 = weights
        forward_ins = forward_ins[:4] + [(w0, 0)] + forward_ins[4:]
        hidden, act, slope, *saved = call(
            forward_kernel, steps, emb, forward_ins, forward_outs, [pltpu.VMEM(prows, F32)]
        )
    grad_outs = [((STEMS, ROWS, D), BF16, 0), ((SMALL, D), F32, 0)]
    out, ghid, gfeat1, gprop1, *grads1, before, last = call(
        middle_kernel, steps, emb,
        [(ids, 0), (hidden, rb), (feat, fb), (prop, 0), (w1, 0), (vecs, 0), (mbs, 0), (sbs, 0),
         (cot.reshape(rows, D), rb)],
        [((rows, D), BF16, rb), ((rows, D), F32, rb), ((samples, CR, D), BF16, SB),
         ((STEPS * samples, PROP), F32, 0)] + grad_outs
        + [((samples,), jnp.int32, None), ((STEMS,), jnp.int32, None)],
        [pltpu.VMEM(prows, BF16)] + [pltpu.VMEM(prows, F32)] * 3 + acc_shapes(STEMS),
    )
    backward_ins = (
        [(ids, 0), (ghid, rb), (prop, 0), (w0, 0), (vecs, 0), (gfeat1, SB), (gprop1, 0), (act, 0), (slope, 0)]
        + [(a, per(a.shape)) for a in saved]
    )
    backward_outs = [
        ((rows, D), F32, rb), ((samples * FR * STEPS, D), F32, fb), ((STEPS, PROP, samples), F32, 0)
    ]
    if weights is None:
        gtok, gfeat, gprop, mats, small = backward_scatter(
            steps, (emb, before, last), backward_ins, backward_outs, *grads1
        )
        gtok, gfeat, *mats, small = unpack(mats, small, gtok, gfeat)
    else:
        gtok, gfeat, gprop, *grads0 = call(
            backward_kernel, steps, emb, backward_ins, backward_outs + grad_outs,
            [pltpu.VMEM(prows, F32)] + acc_shapes(STEMS),
        )
        mats, small = (jnp.stack(pair) for pair in zip(grads0, grads1))
    gfeat = jnp.swapaxes(gfeat.reshape(samples, FR, STEPS, D), 1, 2)
    return (
        out.reshape(tokens.shape), gtok.reshape(tokens.shape), gfeat, gprop.transpose(2, 0, 1),
        mats, small
    )


def chunks_of(layer, bounds):
    groups = []
    for start, stop in zip(bounds[:-1], bounds[1:]):
        half = (stop - start) // 32 * 16
        groups.append(
            [(layer, start, half, ("z", "x", "y")), (layer, start + half, stop - start - half, ("z", "y", "x"))]
        )
    return groups


SIZES = {"z": 4, "y": 2, "x": 2, "c": 2}
AXES = ("z", "y", "x", "c")
MESH = pl.DeviceIdType.MESH


def place():
    me = lax.axis_index("fsdp")
    return {"z": me // 8, "y": (me // 4) % 2, "x": (me // 2) % 2, "c": me % 2}


def number(at):
    return ((at["z"] * 2 + at["y"]) * 2 + at["x"]) * 2 + at["c"]


def moved(at, axis, by):
    out = dict(at)
    out[axis] = (at[axis] + by) % SIZES[axis]
    return out


def greet(at):
    barrier = pltpu.get_barrier_semaphore()
    count = 0
    for axis in AXES:
        for by in range(1, SIZES[axis]):
            pl.semaphore_signal(
                barrier, inc=1, device_id=(number(moved(at, axis, by)),), device_id_type=MESH
            )
            count += 1
    pl.semaphore_wait(barrier, count)


def block(ref, at, done, row, count):
    index = tuple(pl.ds(0, SIZES[a]) if a in done else pl.ds(at[a], 1) for a in AXES)
    return ref.at[index + (pl.ds(row, count), slice(None))]


class Gather:
    def __init__(self, at, outs, groups, send_sem, recv_sem):
        self.at, self.outs, self.groups = at, outs, groups
        self.send_sem, self.recv_sem = send_sem, recv_sem

    def copies(self, g, phase, arriving):
        for i, (layer, row, count, order) in enumerate(self.groups[g]):
            order = order + ("c",)
            axis, done = order[phase], order[:phase]
            for by in range(1, SIZES[axis]):
                whose = moved(self.at, axis, -by) if arriving else self.at
                ref = block(self.outs[layer], whose, done, row, count)
                sem = (2 * g + i, AXES.index(axis), by - 1)
                yield pltpu.make_async_remote_copy(
                    ref, ref, self.send_sem.at[sem], self.recv_sem.at[sem],
                    device_id=(number(moved(self.at, axis, by)),), device_id_type=MESH,
                )

    def start(self, g, phase):
        for copy in self.copies(g, phase, False):
            copy.start()

    def land(self, g, phase):
        for copy in self.copies(g, phase, True):
            copy.wait_recv()

    def run(self, moves):
        for g, phase in moves:
            if phase > 0:
                self.land(g, phase - 1)
            if phase < 4:
                self.start(g, phase)

    def close(self):
        for g in range(len(self.groups)):
            for phase in range(4):
                for copy in self.copies(g, phase, False):
                    copy.wait_send()


BOUNDS = (0, 160, 320, 480, ROWS)
HALVES = (0, 320, ROWS)
PROPRIO = None
THIRDS = (0, 256, 448, ROWS)
GATHER_GROUPS = chunks_of(0, (0, 160, 352, 512, ROWS))[::-1] + chunks_of(1, THIRDS)
GATHER_FIRST = (
    (0, 0), (1, 0), (0, 1), (2, 0), (1, 1), (0, 2), (3, 0), (2, 1), (1, 2), (0, 3), (4, 0), (3, 1), (2, 2),
    (5, 0), (1, 3), (0, 4), (3, 2), (2, 3), (1, 4), (6, 0), (4, 1), PROPRIO, (3, 3), (2, 4), (5, 1), (3, 4),
)
GATHER_LATER = ((), ((4, 2), (6, 1)), (), ((5, 2),), ((6, 2),), ((4, 3),), (), ((5, 3),))
GATHER_END = ((6, 3), (4, 4), (5, 4), (6, 4))


def place_own(at, shards, outs, local_sem):
    att, up, down, stem, q, pin = shards
    copies = []
    for layer in range(LAYERS):
        own = outs[layer].at[at["z"], at["y"], at["x"], at["c"]]
        pieces = [
            (stem.at[layer, :, pl.ds(j * D, D)], row, D) for j, row in enumerate(MAT_ROWS)
        ] + [
            (q.at[layer], R_Q, SQ), (pin.at[layer], R_PIN, PROP), (att.at[layer], R_ATT, 16),
            (up.at[layer], R_UP, 16), (down.at[layer], R_DOWN, 16),
        ]
        for i, (piece, row, count) in enumerate(pieces):
            copies.append(
                pltpu.make_async_copy(piece, own.at[pl.ds(row, count), :], local_sem.at[layer, i])
            )
    return copies


def gather_forward_kernel(emb_ref, ids_ref, tok_ref, feat_ref, prop_ref, vec_ref, mb_ref, sb_ref, *rest):
    shards, (out_ref, act_ref, slope_ref, g0, g1), rest = rest[:6], rest[6:11], rest[11:]
    saved, (rows_ref, w_ref, local_sem, send_sem, recv_sem, keep_sem) = rest[:-6], rest[-6:]
    step = pl.program_id(0)
    at = place()
    move = Gather(at, (w_ref, g1), GATHER_GROUPS, send_sem, recv_sem)
    keep = pltpu.make_async_copy(w_ref, g0, keep_sem)

    @pl.when(step == 0)
    def _():
        local = place_own(at, shards, (w_ref, g1), local_sem)
        for copy in local:
            copy.start()
        greet(at)
        for copy in local:
            copy.wait()
        for step_ in GATHER_FIRST:
            if step_ is PROPRIO:
                start_forward(0, ids_ref, prop_ref, w_ref, sb_ref, act_ref, slope_ref, rows_ref)
            else:
                move.run((step_,))
        keep.start()

    def moves_at(half):
        for i in range(len(GATHER_LATER) // 2):
            pl.when(step == i)(functools.partial(move.run, GATHER_LATER[2 * i + half]))

    moves_at(0)
    es = [emb_ref[step * SB + j] for j in range(SB)]
    out, kept = forward_block(
        es, tok_ref[...].astype(F32), feat_ref, rows_ref[block_rows(step), :], w_ref,
        *layer_inputs(0, vec_ref, mb_ref), tick=lambda: moves_at(1)
    )
    out_ref[...] = out
    save(kept, saved)

    @pl.when(step == pl.num_programs(0) - 1)
    def _():
        move.run(GATHER_END)
        keep.wait()
        move.close()


def gather_forward(steps, emb, ins, outs, shards):
    assert 2 * steps == len(GATHER_LATER)
    lead = (4, 2, 2, 2, ROWS, D)
    any_spec = pl.BlockSpec(memory_space=pl.ANY)
    smem = pl.BlockSpec(memory_space=pltpu.SMEM)
    weights = jax.ShapeDtypeStruct(lead, BF16)
    ins = ins + [(a, 0) for a in shards]
    specs = [blocked(s, n) if n else whole(s) for s, _, n in outs]
    shapes = [jax.ShapeDtypeStruct(s, d) for s, d, _ in outs]
    groups = 2 * len(GATHER_GROUPS)
    res = pl.pallas_call(
        gather_forward_kernel,
        grid=(steps,),
        in_specs=[smem] + [blocked(a.shape, n) if n else whole(a.shape) for a, n in ins],
        out_specs=specs[:3] + [any_spec, any_spec] + specs[3:],
        out_shape=shapes[:3] + [weights, weights] + shapes[3:],
        scratch_shapes=[
            pltpu.VMEM(outs[2][0], F32),
            pltpu.VMEM(lead, BF16),
            pltpu.SemaphoreType.DMA((LAYERS, 9)),
            pltpu.SemaphoreType.DMA((groups, 4, 3)),
            pltpu.SemaphoreType.DMA((groups, 4, 3)),
            pltpu.SemaphoreType.DMA(()),
        ],
        compiler_params=pltpu.CompilerParams(
            dimension_semantics=("arbitrary",), vmem_limit_bytes=VMEM_LIMIT, collective_id=0,
            has_side_effects=True,
        ),
    )(emb, *[a for a, _ in ins])
    hidden, act, slope, w0, w1, *saved = res
    return (hidden, act, slope, w0.reshape(STEMS, ROWS, D), w1.reshape(STEMS, ROWS, D), *saved)


class Scatter:
    def __init__(self, at, groups, source, acc, lands, out, small, sems):
        self.at, self.groups, self.source, self.acc, self.lands, self.out = at, groups, source, acc, lands, out
        self.send_sem, self.recv_sem, self.small_send, self.small_recv = sems
        self.sm, self.smr, self.smz, self.small_out = small

    def order(self, chunk):
        return ("c",) + chunk[3][::-1]

    def left(self, chunk, phase):
        return [a for a in AXES if a not in self.order(chunk)[: phase + 1]]

    def copies(self, g, phase):
        for i, chunk in enumerate(self.groups[g]):
            _, row, count, _ = chunk
            axis, left = self.order(chunk)[phase], self.left(chunk, phase)
            for by in range(1, SIZES[axis]):
                to = moved(self.at, axis, by)
                src = []
                for a in "zyx":
                    spot = to if a == axis else self.at
                    src.append(pl.ds(0, SIZES[a]) if a in left else spot[a])
                dst = [by - 1] if axis == "z" else [pl.ds(0, SIZES[a]) for a in left]
                source = self.source(to["c"]) if phase == 0 else self.acc
                rows = (pl.ds(row, count), slice(None))
                sem = (2 * g + i, AXES.index(axis), by - 1)
                yield pltpu.make_async_remote_copy(
                    source.at[tuple(src) + rows], self.lands[phase].at[tuple(dst) + rows],
                    self.send_sem.at[sem], self.recv_sem.at[sem],
                    device_id=(number(to),), device_id_type=MESH,
                )

    def add(self, g, phase):
        for chunk in self.groups[g]:
            _, row, count, _ = chunk
            axis, left = self.order(chunk)[phase], self.left(chunk, phase)
            rows = (pl.ds(row, count), slice(None))
            keep = tuple(slice(None) if a in left else self.at[a] for a in "zyx") + rows
            value = self.acc[keep].astype(F32)
            if axis == "z":
                for by in range(SIZES["z"] - 1):
                    value = value + self.lands[3][(by,) + rows].astype(F32)
                self.out[rows] = value
            else:
                land = (slice(None),) * len(left) + rows
                self.acc[keep] = (value + self.lands[phase][land].astype(F32)).astype(BF16)

    def small_copies(self, phase, arriving):
        axis = "cxyz"[phase]
        for by in range(1, SIZES[axis]):
            whose = moved(self.at, axis, -by) if arriving else self.at
            dst = self.smz.at[whose["z"]] if axis == "z" else self.smr.at[phase]
            yield pltpu.make_async_remote_copy(
                self.sm.at[phase], dst, self.small_send.at[phase, by - 1], self.small_recv.at[phase, by - 1],
                device_id=(number(moved(self.at, axis, by)),), device_id_type=MESH,
            )

    def small_add(self, phase):
        if phase < 3:
            self.sm[phase + 1] = self.sm[phase] + self.smr[phase]
        else:
            self.smz[self.at["z"]] = self.sm[phase]
            self.small_out[...] = (self.smz[0] + self.smz[1]) + (self.smz[2] + self.smz[3])

    def run(self, moves):
        for g, phase in moves:
            if phase > 0:
                for copy in self.small_copies(phase - 1, True) if g < 0 else self.copies(g, phase - 1):
                    copy.wait_recv()
                self.small_add(phase - 1) if g < 0 else self.add(g, phase - 1)
            if phase < 4:
                for copy in self.small_copies(phase, False) if g < 0 else self.copies(g, phase):
                    copy.start()

    def close(self):
        for phase in range(4):
            for g in range(len(self.groups)):
                for copy in self.copies(g, phase):
                    copy.wait_send()
            for copy in self.small_copies(phase, False):
                copy.wait_send()


SCATTER_GROUPS = (chunks_of(0, BOUNDS), chunks_of(1, HALVES))
SCATTER_BESIDE = (
    ((-1, 0), (0, 0), (1, 0)),
    ((-1, 1),),
    ((-1, 2), (0, 1), (1, 1)),
    ((-1, 3),),
    ((-1, 4),),
    ((0, 2),),
    (),
    ((1, 2),),
)
SCATTER_END = (
    (0, 0, 0), (1, 0, 3), (0, 1, 0), (0, 0, 1), PROPRIO, (0, -1, 0), (0, 2, 0), (0, 1, 1), (0, -1, 1), (1, 1, 3),
    (0, 0, 2), (0, 3, 0), (0, 2, 1), (0, -1, 2), (0, 1, 2), (0, 0, 3), (0, 3, 1), (0, 2, 2), (0, -1, 3), (1, 0, 4),
    (0, 1, 3), (0, 0, 4), (0, 3, 2), (1, 1, 4), (0, 2, 3), (0, 1, 4), (0, 3, 3), (0, 2, 4), (0, -1, 4), (0, 3, 4),
)


def backward_scatter_kernel(
    emb_ref, before_ref, last_ref, ids_ref, grad_ref, prop_ref, w_ref, vec_ref, gfeat1_ref, gprop1_ref,
    act_ref, slope_ref, *rest
):
    n = len(SAVED)
    saved, (g1, s1), rest = rest[:n], rest[n : n + 2], rest[n + 2 :]
    (gtok_ref, gfeat_ref, gprop_ref, mats_ref, small_ref, grows_ref), rest = rest[:6], rest[6:]
    acc, rest = dict(zip(ACC, rest[: len(ACC)])), rest[len(ACC) :]
    others, sbuf, own_sem = rest[:3]
    per_layer = rest[3:]
    step = pl.program_id(0)
    samples = before_ref.shape[0]
    at = place()

    def scatter_of(layer):
        accum, r0, r1, r2, r3, sm, smr, smz, *sems = per_layer[12 * layer : 12 * (layer + 1)]
        source = (lambda c: g1.at[:, :, :, c]) if layer else (lambda c: sbuf)
        return Scatter(
            at, SCATTER_GROUPS[layer], source, accum, (r0, r1, r2, r3), mats_ref.at[layer],
            (sm, smr, smz, small_ref.at[layer]), sems,
        )

    first, second = scatter_of(0), scatter_of(1)
    own = pltpu.make_async_copy(g1.at[:, :, :, at["c"]], second.acc, own_sem)

    @pl.when(step == 0)
    def _():
        own.start()
        greet(at)
        for name in ACC[1:]:
            acc[name][...] = jnp.zeros(acc[name].shape, F32)
        second.sm[0] = s1[...]
        second.run(SCATTER_BESIDE[0])

    pl.when(step == 1)(own.wait)

    def moves_at(half):
        for i in range(len(SCATTER_BESIDE) // 2):
            if 2 * i + half:
                pl.when(step == i)(functools.partial(second.run, SCATTER_BESIDE[2 * i + half]))

    moves_at(0)
    es = [emb_ref[step * SB + j] for j in range(SB)]
    befores = [before_ref[step * SB + j] for j in range(SB)]
    stem = acc["stem"]

    def add(j, e, pieces):
        for row, value in pieces:
            old = stem[jnp.maximum(befores[j], 0), row : row + value.shape[0], :]
            stem[step * SB + j, row : row + value.shape[0], :] = value + jnp.where(befores[j] >= 0, old, 0.0)

    ghid, gctx, grows = backward_block(
        es, grad_ref[...], load(saved), w_ref, vec_ref[0].astype(F32), {**acc, "add": add},
        lambda: moves_at(1)
    )
    gtok_ref[...] = ghid
    grows_ref[block_rows(step), :] = grows
    write_features(gctx, gfeat1_ref, gfeat_ref)

    def gather_group(g):
        start, stop = BOUNDS[g], BOUNDS[g + 1]

        def line(z, carry):
            for i in range(4):
                spot = (z, i // 2, i % 2)
                for ref, c in ((first.acc, at["c"]), (sbuf, 1 - at["c"])):
                    e = 8 * z + 2 * i + c
                    s = last_ref[e]
                    if start < STEM_ROWS:
                        end = min(stop, STEM_ROWS)
                        value = stem[jnp.maximum(s, 0), start:end, :]
                        ref[spot + (slice(start, end), slice(None))] = jnp.where(s >= 0, value, 0.0).astype(BF16)
                    if stop > STEM_ROWS:
                        begin = max(start, STEM_ROWS)
                        ref[spot + (slice(begin, stop), slice(None))] = others[
                            e, begin - STEM_ROWS : stop - STEM_ROWS, :
                        ]
            return carry

        lax.fori_loop(0, SIZES["z"], line, 0)

    @pl.when(step == pl.num_programs(0) - 1)
    def _():
        for move in SCATTER_END:
            if move is PROPRIO:
                *grads, bias, gprop = proprio_backward(
                    ids_ref, prop_ref, w_ref, act_ref[...], slope_ref[...], grows_ref[...]
                )
                for row, part in other_blocks(acc, grads):
                    row -= STEM_ROWS
                    others[:, row : row + part.shape[1], :] = part
                first.sm[0, 0:16, :] = small_rows(acc)
                first.sm[0, 16:SMALL, :] = bias
                write_proprio(gprop + gprop1_ref[...], gprop_ref)
                continue
            layer, g, phase = move
            if layer == 0 and phase == 0 and g >= 0:
                gather_group(g)
            (first, second)[layer].run(((g, phase),))
        second.close()
        first.close()


def backward_scatter(steps, scalars, ins, outs, g1, s1):
    lead = (4, 2, 2, 2, ROWS, D)
    samples = scalars[0].shape[0]
    smem = pl.BlockSpec(memory_space=pltpu.SMEM)
    any_spec = pl.BlockSpec(memory_space=pl.ANY)
    outs = outs + [((LAYERS, ROWS, D), F32, 0), ((LAYERS, SMALL, D), F32, 0)]
    per_layer = [
        pltpu.VMEM((4, 2, 2, ROWS, D), BF16),
        pltpu.VMEM((4, 2, 2, ROWS, D), BF16),
        pltpu.VMEM((4, 2, ROWS, D), BF16),
        pltpu.VMEM((4, ROWS, D), BF16),
        pltpu.VMEM((3, ROWS, D), BF16),
        pltpu.VMEM((4, SMALL, D), F32),
        pltpu.VMEM((3, SMALL, D), F32),
        pltpu.VMEM((4, SMALL, D), F32),
        pltpu.SemaphoreType.DMA((2 * len(BOUNDS), 4, 3)),
        pltpu.SemaphoreType.DMA((2 * len(BOUNDS), 4, 3)),
        pltpu.SemaphoreType.DMA((4, 3)),
        pltpu.SemaphoreType.DMA((4, 3)),
    ]
    return pl.pallas_call(
        backward_scatter_kernel,
        grid=(steps,),
        in_specs=[smem] * 3 + [blocked(a.shape, n) if n else whole(a.shape) for a, n in ins]
        + [any_spec, whole(s1.shape)],
        out_specs=[blocked(s, n) if n else whole(s) for s, _, n in outs],
        out_shape=[jax.ShapeDtypeStruct(s, d) for s, d, _ in outs],
        scratch_shapes=[pltpu.VMEM((STEPS * samples, D), F32)] + acc_shapes(samples)
        + [
            pltpu.VMEM((STEMS, ROWS - STEM_ROWS, D), BF16),
            pltpu.VMEM((4, 2, 2, ROWS, D), BF16),
            pltpu.SemaphoreType.DMA(()),
        ]
        + per_layer * LAYERS,
        compiler_params=pltpu.CompilerParams(
            dimension_semantics=("arbitrary",), vmem_limit_bytes=VMEM_LIMIT, collective_id=1,
            has_side_effects=True,
        ),
    )(*scalars, *[a for a, _ in ins], g1.reshape(lead), s1)


def unpack_kernel(mats, small, gtok_in, gfeat_in, gtok, gfeat, att, up, down, stem, q, pin, vec, mb, sb):
    gtok[...] = gtok_in[...]
    gfeat[...] = gfeat_in[...]
    pl.when(pl.program_id(0) == 0)(
        lambda: split_gradients(mats, small, att, up, down, stem, q, pin, vec, mb, sb)
    )


def split_gradients(mats, small, att, up, down, stem, q, pin, vec, mb, sb):
    for layer in range(LAYERS):
        for j, row in enumerate(MAT_ROWS):
            stem[layer, :, j * D : (j + 1) * D] = mats[layer, row : row + D, :]
        q[layer] = mats[layer, R_Q:R_WP, :]
        pin[layer] = mats[layer, R_PIN:R_ATT, :]
        att[layer] = mats[layer, R_ATT:R_UP, :]
        up[layer] = mats[layer, R_UP:R_DOWN, :]
        down[layer] = mats[layer, R_DOWN:ROWS, :]
        vec[layer] = small[layer, 0:8, :]
        for i in range(4):
            mb[layer : layer + 1, i * D : (i + 1) * D] = small[layer, 8 + i : 9 + i, :]
        sb[layer] = small[layer, 16:SMALL, :]


def unpack(mats, small, gtok, gfeat):
    outs = [
        (LAYERS, 16, D), (LAYERS, 16, D), (LAYERS, 16, D), (LAYERS, D, 4 * D), (LAYERS, SQ, D),
        (LAYERS, PROP, D), (LAYERS, 8, D), (LAYERS, FF), (LAYERS, 2 * STEMS, D),
    ]
    steps = 2
    moved_through = [blocked(a.shape, a.shape[0] // steps) for a in (gtok, gfeat)]
    return pl.pallas_call(
        unpack_kernel,
        grid=(steps,),
        out_shape=[jax.ShapeDtypeStruct(s, F32) for s in [gtok.shape, gfeat.shape] + outs],
        in_specs=[whole(mats.shape), whole(small.shape)] + moved_through,
        out_specs=moved_through + [whole(s) for s in outs],
        compiler_params=pltpu.CompilerParams(
            dimension_semantics=("arbitrary",), vmem_limit_bytes=VMEM_LIMIT
        ),
    )(mats, small, gtok, gfeat)


def pack(attn, up, down, stem, queries, pin):
    gathered = [lax.all_gather(a, "fsdp", axis=1, tiled=True) for a in (attn, up, down, stem, queries, pin)]
    attn, up, down, stem, queries, pin = gathered
    stem = stem.reshape(LAYERS, STEMS, D, 4, D).transpose(0, 1, 3, 2, 4).reshape(LAYERS, STEMS, 4 * D, D)
    queries, *parts = [a.reshape(LAYERS, STEMS, -1, D) for a in (queries, pin, attn, up, down)]
    return jnp.concatenate([stem[:, :, : 3 * D], queries, stem[:, :, 3 * D :], *parts], 2)


def unpack_blocks(grad):
    stem = jnp.concatenate([grad[..., row : row + D, :] for row in MAT_ROWS], -1)
    return (
        grad[..., R_ATT:R_UP, :], grad[..., R_UP:R_DOWN, :], grad[..., R_DOWN:ROWS, :],
        stem, grad[..., R_Q:R_WP, :], grad[..., R_PIN:R_ATT, :],
    )


def body(n, tokens, features, proprio, embodiment, trunk_attn, feedforward_up_weight, mlp_down,
         stem_mats, stem_queries, prop_in, trunk_vectors, mlp_bias, stem_bias, cotangent):
    shards = (trunk_attn, feedforward_up_weight, mlp_down, stem_mats, stem_queries, prop_in)
    out, gtok, gfeat, gprop, mats, small = compute(
        tokens, features, proprio, embodiment, shards, trunk_vectors, mlp_bias, stem_bias,
        cotangent, None if n == 32 else pack(*shards),
    )
    if n == 32:
        return (out, gtok, gfeat, gprop, *mats, small.reshape(LAYERS, STEMS, 2, D))
    mats = [
        lax.psum_scatter(a.reshape(LAYERS, -1, a.shape[-1]), "fsdp", scatter_dimension=1, tiled=True)
        for a in unpack_blocks(mats.astype(F32))
    ]
    small = lax.psum(small, "fsdp")
    gvec = small[:, :8]
    gmb = small[:, 8:12].reshape(LAYERS, FF)
    gsb = small[:, 16:].reshape(LAYERS, STEMS, 2, D)
    return (out, gtok, gfeat, gprop, *mats, gvec, gmb, gsb)


def solution(mesh):
    n = mesh.shape["fsdp"]
    return jax.shard_map(
        functools.partial(body, n),
        mesh=mesh,
        in_specs=(
            P("fsdp"), P("fsdp"), P("fsdp"), P("fsdp"),
            P(None, "fsdp"), P(None, "fsdp"), P(None, "fsdp"), P(None, "fsdp"), P(None, "fsdp"),
            P(None, "fsdp"), P(), P(), P(), P("fsdp"),
        ),
        out_specs=(
            P("fsdp"), P("fsdp"), P("fsdp"), P("fsdp"),
            P(None, "fsdp"), P(None, "fsdp"), P(None, "fsdp"), P(None, "fsdp"), P(None, "fsdp"),
            P(None, "fsdp"), P(), P(), P(),
        ),
        check_vma=False,
    )
```
